32 devices in a mesh: sp: 8 (over z, y), tp: 4 (over x, core).
Axes of the slice: x: 2, y: 2, z: 4, core: 2. Of those that a mesh axis runs over, the one named last changes fastest.
Arguments:
- patches: bfloat16 [4, 96, 768, 256], P(None, 'sp', 'tp'), may hold values from -6 to 6
- present: int32 [4, 768], P(None, 'tp'), may hold values from 0 to 1, as said below
- first_gain: float32 [768], P('tp'), may hold values from 0.1 to 1.9
- first_shift: float32 [768], P('tp'), may hold values from -3 to 3
- filter_inner: bfloat16 [2, 8, 96, 96], P(None, 'tp'), may hold values from -0.4375 to 0.4375
- inner_bias: float32 [2, 8, 96], P(None, 'tp'), may hold values from -3 to 3
- filter_outer: bfloat16 [2, 8, 96, 96], P(None, 'tp'), may hold values from -0.4375 to 0.4375
- outer_bias: float32 [2, 8, 96], P(None, 'tp'), may hold values from -3 to 3
- second_gain: float32 [768], P('tp'), may hold values from 0.1 to 1.9
- second_shift: float32 [768], P('tp'), may hold values from -3 to 3
- expand_weight: bfloat16 [768, 3072], P(None, 'tp'), may hold values from -0.21875 to 0.21875
- expand_bias: float32 [3072], P('tp'), may hold values from -3 to 3
- project_weight: bfloat16 [3072, 768], P('tp'), may hold values from -0.109375 to 0.109375
- project_bias: float32 [768], P('tp'), may hold values from -3 to 3
- cotangent: bfloat16 [4, 96, 768, 256], P(None, 'sp', 'tp'), may hold values from -6 to 6
Outputs:
- result: float32 [4, 96, 768, 256], P(None, 'sp', 'tp')
- patches_grad: float32 [4, 96, 768, 256], P(None, 'sp', 'tp')
- first_gain_grad: float32 [768], replicated
- first_shift_grad: float32 [768], replicated
- filter_inner_grad: float32 [2, 8, 96, 96], P(None, 'tp', 'sp')
- inner_bias_grad: float32 [2, 8, 96], P(None, 'tp', 'sp')
- filter_outer_grad: float32 [2, 8, 96, 96], P(None, 'tp', 'sp')
- outer_bias_grad: float32 [2, 8, 96], P(None, 'tp', 'sp')
- second_gain_grad: float32 [768], replicated
- second_shift_grad: float32 [768], replicated
- expand_weight_grad: float32 [768, 3072], P('sp', 'tp')
- expand_bias_grad: float32 [3072], replicated
- project_weight_grad: float32 [3072, 768], P('tp', 'sp')
- project_bias_grad: float32 [768], replicated
- shrink_share: float32 [], replicated
The draws below stay inside these ranges and needn't reach their ends.
Inputs may be any that keep to these rules, and one draw needn't show every extreme that they name: 1 marks a feature present in the snapshot, 0 an absent one.
All inputs are finite; a program needn't handle non-finite values.
Results may differ from the reference program's by a relative error of at most 0.008.
The reference program's roundings to bfloat16 on the way count: a program that leaves them out, or rounds other values in their place, can miss the bound.
Values may be sent and summed in bfloat16 or wider, within the bound.
No kernel may reach another device: no remote copies, remote signals or barrier semaphores. Data moves between devices by JAX's collectives and lax.ppermute only.
A program may use at most 448 MiB of HBM per device.

```python
import jax
import jax.numpy as jnp
from jax import lax

BLOCKS = 8
BLOCK = 96
D = 768
FF = 3072
H = 96
W = 256
KW = 128
SNAPS = 4


def draw_present(key, part):
    key = jax.random.fold_in(key, 7)
    level_key, order_key = jax.random.split(key)
    level = jax.random.randint(level_key, (SNAPS,), 0, 32)
    absent = 1 + level * level * level * (D * 7 // 8 - 1) // 29791
    orders = jax.vmap(lambda sub: jax.random.permutation(sub, D))(jax.random.split(order_key, SNAPS))
    return (orders >= absent[:, None]).astype(jnp.int32)


def spiked(drawn, rng, source, target, shards_of, factor):
    def block_of(dim):
        return (jnp.arange(drawn.shape[dim]) // (drawn.shape[dim] // shards_of)).reshape((-1,) + (1,) * (drawn.ndim - 1 - dim))

    first = jax.random.permutation(rng, shards_of)[block_of(target)]
    second = (block_of(target) + shards_of // 2) % shards_of
    return jnp.where((block_of(source) == first) | (block_of(source) == second), factor * drawn, drawn)


def block_levels(key, shape, pieces, least, high):
    loudness, own = 1.0, jax.random.fold_in(key, 6)
    for axis_at, shards_of in pieces:
        steps = jnp.exp(jax.random.uniform(jax.random.fold_in(own, axis_at), (shards_of,), jnp.float32, least / len(pieces), high / len(pieces)))
        loudness = loudness * jnp.repeat(steps, shape[axis_at] // shards_of).reshape([-1 if axis == axis_at else 1 for axis in range(len(shape))])
    return loudness


def scatter_about(key, dims, deviation, most, cuts=(), kind=jnp.bfloat16):
    values = jax.random.normal(key, dims, jnp.float32) * deviation
    if len(cuts) > 0:
        values = block_levels(key, dims, cuts, -0.22, 0.18) * values
    return jnp.clip(values, min=-most, max=most).astype(kind)


def gaussian_with(key, shape, spread, limit, shards, heavy, kind=jnp.bfloat16):
    values = spread * jax.random.normal(key, shape, jnp.float32)
    if shards:
        values = values * block_levels(key, shape, shards, -0.22, 0.18)
    return jnp.clip(spiked(values, jax.random.fold_in(key, 3), *heavy), -limit, limit).astype(kind)


def setup_inputs(seed: int = 0) -> dict:
    keys = jax.random.split(jax.random.key(seed), 16)
    return {
        "patches": gaussian_with(keys[0], (SNAPS, H, D, W), 1.0, 6.0, ((1, 8), (2, 4)), (1, 2, 8, 2.0)),
        "present": draw_present(jax.random.fold_in(keys[15], 71), 0),
        "first_gain": jnp.clip(1.0 + 0.18 * jax.random.normal(keys[2], (D,), jnp.float32), 0.1, 1.9),
        "first_shift": scatter_about(keys[3], (D,), 0.3, 3.0, ((0, 4),), jnp.float32),
        "filter_inner": scatter_about(keys[4], (2, BLOCKS, BLOCK, BLOCK), (2 * BLOCK) ** -0.5, 0.4375, ((1, 4),)),
        "inner_bias": scatter_about(keys[5], (2, BLOCKS, BLOCK), 0.3, 3.0, ((1, 4),), jnp.float32),
        "filter_outer": scatter_about(keys[6], (2, BLOCKS, BLOCK, BLOCK), (2 * BLOCK) ** -0.5, 0.4375, ((1, 4),)),
        "outer_bias": scatter_about(keys[7], (2, BLOCKS, BLOCK), 0.3, 3.0, ((1, 4),), jnp.float32),
        "second_gain": jnp.clip(1.0 + 0.18 * jax.random.normal(keys[8], (D,), jnp.float32), 0.1, 1.9),
        "second_shift": scatter_about(keys[9], (D,), 0.3, 3.0, ((0, 4),), jnp.float32),
        "expand_weight": scatter_about(keys[10], (D, FF), D ** -0.5, 0.21875, ((1, 4),)),
        "expand_bias": scatter_about(keys[11], (FF,), 0.3, 3.0, ((0, 4),), jnp.float32),
        "project_weight": scatter_about(keys[12], (FF, D), FF ** -0.5, 0.109375, ((0, 4),)),
        "project_bias": scatter_about(keys[13], (D,), 0.3, 3.0, ((0, 4),), jnp.float32),
        "cotangent": gaussian_with(keys[14], (SNAPS, H, D, W), 1.0, 6.0, ((1, 8), (2, 4)), (1, 2, 8, 2.0)),
    }


@jax.custom_vjp
def low(v):
    return lax.optimization_barrier(v.astype(jnp.bfloat16)).astype(jnp.float32)

@jax.custom_vjp
def low_back(v):
    return v

def low_keep(v):
    return (low(v), None)

def low_pass(kept, grad):
    return (grad,)

def back_keep(v):
    return (v, None)

def back_low(kept, grad):
    return (low(grad),)
low.defvjp(low_keep, low_pass)
low_back.defvjp(back_keep, back_low)
SHRINK = 0.01
NORM_EPS = 1e-05
HIGH = lax.Precision.HIGHEST

def gelu_exact(value):
    return jax.nn.gelu(value, approximate=False)

def layer_norm(value, gain, shift):
    mean = lax.optimization_barrier(jnp.mean(value, axis=-1, keepdims=True))
    centered = value - mean
    var = lax.optimization_barrier(jnp.mean(centered * centered, axis=-1, keepdims=True))
    return centered * lax.rsqrt(var + NORM_EPS) * gain + shift

def block_mix(left, right):
    return jnp.einsum('ykbi,bio->ykbo', left, right, precision=HIGH)

def spectral_filter(mixed, filter_inner, inner_bias, filter_outer, outer_bias):
    spectrum = jnp.fft.rfft2(mixed, axes=(0, 1), norm='ortho')[:, :KW, :]
    spec_re = low(jnp.real(spectrum)).reshape(H, KW, BLOCKS, BLOCK)
    spec_im = low(jnp.imag(spectrum)).reshape(H, KW, BLOCKS, BLOCK)
    first_re = low_back(block_mix(spec_re, filter_inner[0]) - block_mix(spec_im, filter_inner[1]) + inner_bias[0])
    first_im = low_back(block_mix(spec_im, filter_inner[0]) + block_mix(spec_re, filter_inner[1]) + inner_bias[1])
    mid_re = low(gelu_exact(first_re))
    mid_im = low(gelu_exact(first_im))
    second_re = low_back(block_mix(mid_re, filter_outer[0]) - block_mix(mid_im, filter_outer[1]) + outer_bias[0])
    second_im = low_back(block_mix(mid_im, filter_outer[0]) + block_mix(mid_re, filter_outer[1]) + outer_bias[1])
    bend_re = jnp.tanh(second_re / SHRINK)
    bend_im = jnp.tanh(second_im / SHRINK)
    share_part = jnp.sum(1.0 - bend_re * bend_re) + jnp.sum(1.0 - bend_im * bend_im)
    kept_re = (second_re - SHRINK * bend_re).reshape(H, KW, D)
    kept_im = (second_im - SHRINK * bend_im).reshape(H, KW, D)
    nyquist = jnp.zeros((H, 1, D), kept_re.dtype)
    whole = lax.complex(jnp.concatenate([kept_re, nyquist], axis=1), jnp.concatenate([kept_im, nyquist], axis=1))
    return (jnp.fft.irfft2(whole, s=(H, W), axes=(0, 1), norm='ortho'), share_part)

def block(field, keep, first_gain, first_shift, filter_inner, inner_bias, filter_outer, outer_bias, second_gain, second_shift, expand_weight, expand_bias, project_weight, project_bias):
    mixed = layer_norm(field, first_gain, first_shift) * keep
    spectral, share_part = spectral_filter(mixed, filter_inner, inner_bias, filter_outer, outer_bias)
    section = field + mixed + spectral
    normal = low(layer_norm(section, second_gain, second_shift)).reshape(H * W, D)
    hidden_pre = low_back(jnp.dot(normal, expand_weight, precision=HIGH) + expand_bias)
    hidden = low(gelu_exact(hidden_pre))
    branch = jnp.dot(hidden, project_weight, precision=HIGH) + project_bias
    return (section + branch.reshape(H, W, D), share_part)

def reference(patches, present, first_gain, first_shift, filter_inner, inner_bias, filter_outer, outer_bias, second_gain, second_shift, expand_weight, expand_bias, project_weight, project_bias, cotangent):
    weights = tuple((weight_arg.astype(jnp.float32) for weight_arg in (first_gain, first_shift, filter_inner, inner_bias, filter_outer, outer_bias, second_gain, second_shift, expand_weight, expand_bias, project_weight, project_bias)))

    def snapshot(totals, item):
        frame, mask_row, frame_cot = item
        keep = mask_row.astype(jnp.float32)
        frame_last = jnp.swapaxes(frame, 1, 2).astype(jnp.float32)
        cot_last = jnp.swapaxes(frame_cot, 1, 2).astype(jnp.float32)

        def forward(field, *params):
            return block(field, keep, *params)
        output, pull, share_part = jax.vjp(forward, frame_last, *weights, has_aux=True)
        grads = pull(cot_last)
        summed = tuple((total + grad for total, grad in zip(totals[:-1], grads[1:])))
        return (summed + (totals[-1] + share_part,), (jnp.swapaxes(output, 1, 2), jnp.swapaxes(grads[0], 1, 2)))
    start = tuple((jnp.zeros_like(weight_arg) for weight_arg in weights)) + (jnp.zeros((), jnp.float32),)
    totals, (result, patches_grad) = lax.scan(snapshot, start, (patches, present, cotangent))
    share = totals[12] / (SNAPS * H * KW * D * 2)
    return (result, patches_grad, totals[0], totals[1], totals[2], totals[3], totals[4], totals[5], totals[6], totals[7], totals[8], totals[9], totals[10], totals[11], share)
```

```python
import functools
import math

import jax
import jax.numpy as jnp
import numpy as np
from jax import lax
from jax.experimental import pallas as pl
from jax.experimental.pallas import tpu as pltpu
from jax.sharding import Mesh, PartitionSpec as P

BLOCK = 96
SHRINK = 0.01
NORM_EPS = 1e-05
BF = jnp.bfloat16
F32 = jnp.float32
NN = (((1,), (0,)), ((), ()))
NT = (((1,), (1,)), ((), ()))
TN = (((0,), (0,)), ((), ()))
ERF_T = 0.3275911
ERF_POLY = (0.254829592, -0.284496736, 1.421413741, -1.453152027, 1.061405429)


def dot(left, right, dims=NN):
    return lax.dot_general(left, right, dims, preferred_element_type=F32)


def gelu_pair(value):
    root = jnp.abs(value) * (1.0 / math.sqrt(2.0))
    t = 1.0 / (1.0 + ERF_T * root)
    bell = jnp.exp(-0.5 * value * value)
    poly = 0.5 * ERF_POLY[4]
    for coef in ERF_POLY[3::-1]:
        poly = poly * t + 0.5 * coef
    tail = poly * t * bell
    phi = jnp.where(value >= 0, 1.0 - tail, tail)
    return value * phi, phi + value * bell * (1.0 / math.sqrt(2.0 * math.pi))


def split(value):
    high = value.astype(BF)
    return high, (value - high.astype(F32)).astype(BF)


def np_split(table):
    high = table.astype(np.float32).astype(jnp.bfloat16)
    low = (table - high.astype(np.float64)).astype(np.float32).astype(jnp.bfloat16)
    return jnp.asarray(high), jnp.asarray(low)


def lon_tables(width, modes):
    angle = 2.0 * np.pi * (np.outer(np.arange(modes), np.arange(width)) % width) / width
    scale = 1.0 / math.sqrt(width)
    cos, sin = np.cos(angle) * scale, np.sin(angle) * scale
    doubled = np.where(np.arange(modes) == 0, 1.0, 2.0)[:, None]
    plain = np.concatenate([cos, -sin], 0)
    weighted = np.concatenate([cos * doubled, -sin * doubled], 0)
    return plain, weighted


def lat_table(rows):
    angle = 2.0 * np.pi * (np.outer(np.arange(rows), np.arange(rows)) % rows) / rows
    scale = 1.0 / math.sqrt(rows)
    cos, sin = np.cos(angle) * scale, np.sin(angle) * scale
    return np.block([[cos, sin], [-sin, cos]])


def fold_lanes(value):
    total = value[:, :128]
    for at in range(128, value.shape[1], 128):
        total = total + value[:, at : at + 128]
    return total


def collect(place, pieces, field):
    per = pieces[0].shape[0]
    for k, piece in enumerate(pieces):
        field[pl.ds(place[k] * per, per)] = piece[...].astype(F32)


def plane_forward(parts, table, lat_hi, lat_lo, lons, spectra):
    rows, modes = lat_hi.shape[0] // 2, spectra.shape[1]
    feats = spectra.shape[0] // (2 * rows)
    table_hi, table_lo = table
    total = dot(parts[0], table_lo)
    if len(parts) > 1:
        total = total + dot(parts[1], table_hi)
    total = total + dot(parts[0], table_hi)
    for c in range(2):
        lons[c] = total[:, c * modes : (c + 1) * modes]
    for f in range(0, feats, 2):
        pair = []
        for g in (f, f + 1):
            pair.append(jnp.concatenate([lons[c, pl.ds(g, rows, stride=feats), :] for c in range(2)], axis=0))
        high, low = split(jnp.concatenate(pair, axis=1))
        out = dot(lat_hi, high) + (dot(lat_lo, high) + dot(lat_hi, low))
        for i, g in enumerate((f, f + 1)):
            spectra[pl.ds(g, 2 * rows, stride=feats), :] = out[:, i * modes : (i + 1) * modes]


def plane_inverse(table, lat_hi, lat_lo, lons, spectra):
    rows, modes = lat_hi.shape[0] // 2, spectra.shape[1]
    feats = spectra.shape[0] // (2 * rows)
    table_hi, table_lo = table
    for f in range(0, feats, 2):
        pair = [spectra[pl.ds(g, 2 * rows, stride=feats), :] for g in (f, f + 1)]
        high, low = split(jnp.concatenate(pair, axis=1))
        out = dot(lat_hi, high) + (dot(lat_lo, high) + dot(lat_hi, low))
        for i, g in enumerate((f, f + 1)):
            for c in range(2):
                lons[c, pl.ds(g, rows, stride=feats), :] = out[c * rows : (c + 1) * rows, i * modes : (i + 1) * modes]
    high, low = split(jnp.concatenate([lons[0], lons[1]], axis=1))
    return dot(high, table_hi) + (dot(high, table_lo) + dot(low, table_hi))


def spectrum_kernel(n, place, *refs):
    pieces, (mean, rstd, scale, shift, hi, lo, lat_hi, lat_lo, spec, field, lons, spectra) = refs[:n], refs[n:]
    collect(place, pieces, field)
    mixed = (field[...] - mean[...]) * rstd[...] * scale[...] + shift[...]
    rows, feats, width = mixed.shape
    parts = split(mixed.reshape(rows * feats, width))
    plane_forward(parts, (hi[...], lo[...]), lat_hi[...], lat_lo[...], lons, spectra)
    spec[...] = spectra[...].reshape(spec.shape).astype(BF)


def spectrum_back_kernel(sgrad, hi, lo, lat_hi, lat_lo, freq, lons, spectra):
    value = sgrad[...]
    rows, feats, width = value.shape
    if feats % 16:
        value = value.astype(F32).reshape(rows * feats, width).astype(BF)
    else:
        value = value.reshape(rows * feats, width)
    plane_forward((value,), (hi[...], lo[...]), lat_hi[...], lat_lo[...], lons, spectra)
    freq[...] = spectra[...].reshape(freq.shape)


def two_modes(ref, ky):
    return jnp.concatenate([jnp.concatenate([ref[0, k], ref[1, k]], axis=0) for k in (ky, ky + 1)], axis=1)


def put_modes(ref, ky, value):
    feats, modes = ref.shape[2], ref.shape[3]
    for i in range(2):
        for c in range(2):
            ref[c, ky + i] = value[c * feats : (c + 1) * feats, i * modes : (i + 1) * modes]


def filter_kernel(spec, w1, bias1, w2, bias2, kept, mid, slope, bend, share):
    @pl.when(pl.program_id(0) == 0)
    def _():
        share[...] = jnp.zeros_like(share)

    for ky in range(0, spec.shape[1], 2):
        act, deriv = gelu_pair(dot(w1[...], two_modes(spec, ky)) + bias1[...])
        act = act.astype(BF)
        put_modes(mid, ky, act)
        put_modes(slope, ky, deriv)
        second = dot(w2[...], act) + bias2[...]
        bent = jnp.tanh(second * (1.0 / SHRINK))
        square = bent * bent
        put_modes(bend, ky, square)
        put_modes(kept, ky, second - SHRINK * bent)
        share[...] += jnp.sum((1.0 - square).reshape(-1, 8, square.shape[1]), axis=0)


def filter_back_kernel(
    freq, spec, mid, slope, bend, w1, w2, sgrad, inner, outer, inner_bias, outer_bias
):
    @pl.when(pl.program_id(0) == 0)
    def _():
        for ref in (inner, outer, inner_bias, outer_bias):
            ref[...] = jnp.zeros_like(ref)

    for ky in range(0, spec.shape[1], 2):
        two = (two_modes(freq, ky) * two_modes(bend, ky)).astype(BF)
        outer[...] += dot(two_modes(mid, ky), two, NT)
        outer_bias[...] += fold_lanes(two.astype(F32))
        one = (dot(w2[...], two, TN) * two_modes(slope, ky)).astype(BF)
        inner[...] += dot(two_modes(spec, ky), one, NT)
        inner_bias[...] += fold_lanes(one.astype(F32))
        put_modes(sgrad, ky, dot(w1[...], one, TN))


def section_kernel(n, place, *refs):
    pieces, (mean, rstd, scale, shift, kept, hi, lo, lat_hi, lat_lo, section, field, lons, spectra) = refs[:n], refs[n:]
    spectra[...] = kept[...].reshape(spectra.shape)
    collect(place, pieces, field)
    value = field[...]
    mixed = (value - mean[...]) * rstd[...] * scale[...] + shift[...]
    spectral = plane_inverse((hi[...], lo[...]), lat_hi[...], lat_lo[...], lons, spectra)
    section[...] = (value + mixed + spectral.reshape(value.shape)).astype(BF)


def last_kernel(n, place, *refs):
    pieces = refs[:n]
    mean, rstd, scale, sgrad, freq, hi, lo, lat_hi, lat_lo, out, one, two, gain_sum, shift_sum, field, lons, spectra = refs[n:]
    spectra[...] = freq[...].reshape(spectra.shape)
    collect(place, pieces, field)
    normed = (field[...] - mean[...]) * rstd[...]
    grad = sgrad[...].astype(F32)
    mixed = grad + plane_inverse((hi[...], lo[...]), lat_hi[...], lat_lo[...], lons, spectra).reshape(grad.shape)
    gain_sum[...] = fold_lanes(jnp.sum(mixed * normed, axis=0))
    shift_sum[...] = fold_lanes(jnp.sum(mixed, axis=0))
    scaled = mixed * scale[...]
    out[...] = (grad + rstd[...] * scaled).astype(BF)

    @pl.when(pl.program_id(0) == 0)
    def _():
        one[...] = jnp.zeros_like(one)
        two[...] = jnp.zeros_like(two)

    one[...] += jnp.sum(scaled, axis=1, keepdims=True)
    two[...] += jnp.sum(scaled * normed, axis=1, keepdims=True)


def column_norm(value):
    mean = jnp.mean(value, axis=0, keepdims=True)
    centered = value - mean
    var = jnp.mean(centered * centered, axis=0, keepdims=True)
    rstd = lax.rsqrt(var + NORM_EPS)
    return centered * rstd, rstd


def feed_kernel(
    n, quarter, chunk, place, *refs
):
    cots = refs[:n]
    (section, we_t, wp, we, bias, gain, shift,
     normal, hidden, pre, cot, sgrad, bias_sum, gain_sum, shift_sum, cot_sum) = refs[n:]

    @pl.when(pl.program_id(0) == 0)
    def _():
        for ref in (bias_sum, gain_sum, shift_sum, cot_sum):
            ref[...] = jnp.zeros_like(ref)

    for k, piece in enumerate(cots):
        cot[pl.ds(place[k] * quarter, quarter), :] = piece[0]
    normed, rstd = column_norm(section[...].astype(F32).reshape(normal.shape))
    value = (normed * gain[...] + shift[...]).astype(BF)
    normal[...] = value
    wide = cot[...]
    part = we.shape[2]
    total = None
    for start in range(0, hidden.shape[0], chunk):
        rows = slice(start, start + chunk)
        before = dot(we_t[rows], value) + jnp.concatenate([bias[rows]] * (value.shape[1] // 128), axis=1)
        act, slope = gelu_pair(before)
        hidden[rows] = act.astype(BF)
        grad = (dot(wp[rows], wide) * slope).astype(BF)
        pre[rows] = grad
        bias_sum[rows] += fold_lanes(grad.astype(F32))
        t, at = start // part, start % part
        term = dot(we[t, :, at : at + chunk], grad)
        total = term if total is None else total + term
    gain_sum[...] += fold_lanes(total * normed)
    shift_sum[...] += fold_lanes(total)
    wide = wide.astype(F32)
    cot_sum[...] += fold_lanes(wide)
    scaled = total * gain[...]
    one = jnp.mean(scaled, axis=0, keepdims=True)
    two = jnp.mean(scaled * normed, axis=0, keepdims=True)
    grad = wide + rstd * (scaled - one - normed * two)
    sgrad[...] = grad.reshape(sgrad.shape).astype(BF)


def widen_kernel(slot, p0, p1, p2, p3, out):
    for k, piece in enumerate((p0, p1, p2, p3)):

        @pl.when(pl.program_id(0) == k)
        def _(piece=piece):
            out[0, 0] = piece[...].astype(F32)


def finish_kernel(n, feats, snap, part, *refs):
    pieces, (patches, mean, rstd, one, two, out) = refs[:n], refs[n:]
    normed = (patches[0].astype(F32) - mean[0]) * rstd[0]
    fix = rstd[0] * (one[0] + normed * two[0]) * (1.0 / feats)
    for k, piece in enumerate(pieces):

        @pl.when(pl.program_id(0) == k)
        def _(piece=piece):
            out[0] = piece[...].astype(F32) - fix


def whole(shape):
    return pl.BlockSpec(shape, lambda *_: (0,) * len(shape), pipeline_mode=pl.Buffered(1))


def fixed(shape):
    return pl.BlockSpec(shape, lambda *_: (0,) * len(shape))


def run(name, kernel, grid, ins, specs, outs, out_specs, scratch, mib, scalars=()):
    grid_spec = pltpu.PrefetchScalarGridSpec(
        num_scalar_prefetch=len(scalars), grid=grid, in_specs=specs, out_specs=out_specs, scratch_shapes=scratch
    )
    call = pl.pallas_call(
        kernel,
        grid_spec=grid_spec,
        out_shape=outs,
        compiler_params=pltpu.CompilerParams(vmem_limit_bytes=mib << 20),
        name=name,
    )
    return call(*scalars, *ins)


def complex_weight(pair):
    real, imag = pair[0].T, pair[1].T
    return jnp.concatenate([jnp.concatenate([real, -imag], 1), jnp.concatenate([imag, real], 1)], 0)


def weight_pair(full):
    full = full.reshape(2, BLOCK, 2, BLOCK)
    return jnp.stack([full[0, :, 0] + full[1, :, 1], full[0, :, 1] - full[1, :, 0]])


def per_device(
    sizes, patches, present, first_gain, first_shift, filter_inner, inner_bias, filter_outer, outer_bias,
    second_gain, second_shift, expand_weight, expand_bias, project_weight, project_bias, cotangent,
):
    planes, blocks_local, cut, tp = sizes
    inner = blocks_local * cut
    ranks = inner * tp
    owners = planes * inner
    snaps, per, quarter, width = patches.shape
    feats = quarter * tp
    mine = quarter // inner
    modes = width // 2
    rows = per * ranks
    toks = per * width
    hidden_local = expand_bias.shape[0]
    hiddens = hidden_local * tp
    z, y, j, t = (lax.axis_index(name) for name in ("z", "y", "j", "t"))
    r = y * cut + j
    me = z * inner + r
    every, sp = ("z", "y", "j", "t"), ("z", "y", "j")
    shape = jax.ShapeDtypeStruct

    def to_plane(array):
        array = array.reshape(snaps, per, inner, mine, width)
        out = []
        for k in range(owners):
            there = me ^ k
            piece = lax.dynamic_slice(
                array, (there // inner, 0, there % inner, 0, 0), (1, per, 1, mine, width)
            ).reshape(per, mine, width)
            out.append(lax.ppermute(piece, sp, [(a, a ^ k) for a in range(owners)]) if k else piece)
        return out

    pieces = to_plane(patches)
    origin = jnp.stack([me ^ k for k in range(owners)]).astype(jnp.int32)

    def route(k, back):
        pairs = [
            ((zz * inner + rr) * tp + tt, (((tt + k) % tp) * inner + rr) * tp + zz)
            for zz in range(planes)
            for rr in range(inner)
            for tt in range(tp)
        ]
        return [(b, a) for a, b in pairs] if back else pairs

    place = jnp.stack([(z - k) % tp for k in range(tp)]).astype(jnp.int32)
    slot = jnp.stack([(t + k) % tp for k in range(tp)]).astype(jnp.int32)
    late, pieces = lax.optimization_barrier((cotangent, pieces))
    cots = [
        lax.ppermute(lax.dynamic_index_in_dim(late, (t + k) % tp, 0, False), every, route(k, False)) for k in range(tp)
    ]

    field = patches.astype(F32)
    mean = jnp.mean(field, 2)
    square = jnp.sum(jnp.square(field - mean[:, :, None]), 2)
    gathered = lax.all_gather(jnp.stack([mean, square]), "t")
    mean = jnp.mean(gathered[:, 0], 0)
    square = jnp.sum(gathered[:, 1] + quarter * jnp.square(gathered[:, 0] - mean), 0)
    stats = jnp.stack([mean, lax.rsqrt(square / feats + NORM_EPS)], 2)
    sent = jnp.broadcast_to(stats[:, None], (snaps, inner, per, 2, width)).reshape(owners, per, 2, width)
    plane_stats = lax.all_to_all(sent, sp, 0, 0, tiled=True).reshape(rows, 2, 1, width)
    mean_one, rstd_one = plane_stats[:, 0], plane_stats[:, 1]

    def lanes(vector, width=width):
        return jnp.broadcast_to(vector[:, None], (vector.shape[0], width))

    def own_features(vector):
        return lax.dynamic_slice_in_dim(vector, r * mine, mine)

    keep = own_features(lax.dynamic_index_in_dim(present, z, 0, False).astype(F32))
    scale1, shift1 = lanes(own_features(first_gain) * keep), lanes(own_features(first_shift) * keep)

    def own_block(array):
        return lax.dynamic_index_in_dim(array, y, 1, False)

    w1, w2 = complex_weight(own_block(filter_inner)), complex_weight(own_block(filter_outer))
    bias1 = lanes(own_block(inner_bias).reshape(-1), 2 * modes)
    bias2 = lanes(own_block(outer_bias).reshape(-1), 2 * modes)
    plain, weighted = lon_tables(width, modes)
    lat = lat_table(rows)
    plain_t, weighted_t, plain_n, weighted_n = (np_split(a) for a in (plain.T, weighted.T, plain, weighted))
    lat_f, lat_b = np_split(lat), np_split(lat.T)

    some = 16 if mine % 16 == 0 else mine
    grid = (mine // some,)
    piece_specs = [pl.BlockSpec((per, some, width), lambda g, *_: (0, g, 0))] * owners
    stat_spec, feat_spec = whole((rows, 1, width)), pl.BlockSpec((some, width), lambda g, *_: (g, 0))
    lon_f, lon_b = [whole((width, 2 * modes))] * 2, [whole((2 * modes, width))] * 2
    lat_specs = [whole((2 * rows, 2 * rows))] * 2
    image_spec = pl.BlockSpec((rows, some, width), lambda g, *_: (0, g, 0))
    modes_spec = pl.BlockSpec((2, rows, some, modes), lambda g, *_: (0, 0, g, 0))
    scratch = [
        pltpu.VMEM((rows, some, width), F32),
        pltpu.VMEM((2, rows * some, modes), F32),
        pltpu.VMEM((2 * rows * some, modes), F32),
    ]
    mine_modes = (2, rows, mine, modes)
    spec = run(
        "spectrum", functools.partial(spectrum_kernel, owners), grid,
        (*pieces, mean_one, rstd_one, scale1, shift1, *plain_t, *lat_f),
        [*piece_specs, stat_spec, stat_spec, feat_spec, feat_spec, *lon_f, *lat_specs],
        shape(mine_modes, BF), modes_spec, scratch, 48, (origin,),
    )

    def to_blocks(array):
        return lax.all_to_all(array, "j", 1, 2, tiled=True) if cut > 1 else array

    def to_features(array):
        return lax.all_to_all(array, "j", 2, 1, tiled=True) if cut > 1 else array

    spec = to_blocks(spec)
    lats = rows // cut
    step = 8
    block_modes = (2, lats, BLOCK, modes)
    block_spec = pl.BlockSpec((2, step, BLOCK, modes), lambda g: (0, g, 0, 0))
    square_spec, lane_spec = whole((2 * BLOCK, 2 * BLOCK)), whole((2 * BLOCK, 2 * modes))
    kept, mid, slope, bend, share = run(
        "filter", filter_kernel, (lats // step,), (spec, w1, bias1, w2, bias2),
        [block_spec, square_spec, lane_spec, square_spec, lane_spec],
        (shape(block_modes, F32), shape(block_modes, BF), shape(block_modes, F32), shape(block_modes, F32),
         shape((8, 2 * modes), F32)),
        (block_spec, block_spec, block_spec, block_spec, fixed((8, 2 * modes))), [], 48,
    )
    section = run(
        "section", functools.partial(section_kernel, owners), grid,
        (*pieces, mean_one, rstd_one, scale1, shift1, to_features(kept), *weighted_n, *lat_b),
        [*piece_specs, stat_spec, stat_spec, feat_spec, feat_spec, modes_spec, *lon_b, *lat_specs],
        shape((rows, mine, width), BF), image_spec, scratch, 56, (origin,),
    )

    def exchange(array):
        return lax.all_to_all(array.reshape(ranks, per, mine, width), ("t", "y", "j"), 0, 0, tiled=True)

    section = exchange(section)

    small = lax.all_gather(jnp.stack([second_gain, second_shift, project_bias]), "t", axis=1, tiled=True)
    bias_all = lax.all_gather(expand_bias, "t", tiled=True)
    we = lax.all_gather(expand_weight, "t")
    wp = lax.all_gather(project_weight, "t", tiled=True)
    we_t = jnp.swapaxes(we, 1, 2).reshape(hiddens, feats)
    gain2, shift2 = lanes(small[0]), lanes(small[1])
    tok_spec = pl.BlockSpec((feats, width), lambda h, *_: (0, h))
    hid_spec = pl.BlockSpec((hiddens, width), lambda h, *_: (0, h))
    cot_specs = [pl.BlockSpec((1, quarter, width), lambda h, *_: (h, 0, 0))] * tp
    line_spec = pl.BlockSpec((ranks, 1, mine, width), lambda h, *_: (0, h, 0, 0))
    normal, hidden, pre, cot, sgrad, bias_sum, gain_sum, shift_sum, cot_sum = run(
        "feed", functools.partial(feed_kernel, tp, quarter, min(512, hidden_local // 2)), (per,),
        (*cots, section, we_t, wp, we, lanes(bias_all, 128), gain2, shift2),
        [*cot_specs, line_spec, whole((hiddens, feats)), whole((hiddens, feats)), whole((tp, feats, hidden_local)),
         whole((hiddens, 128)), whole((feats, width)), whole((feats, width))],
        (shape((feats, toks), BF), shape((hiddens, toks), BF), shape((hiddens, toks), BF), shape((feats, toks), BF),
         shape((ranks, per, mine, width), BF), shape((hiddens, 128), F32), *[shape((feats, 128), F32)] * 3),
        (tok_spec, hid_spec, hid_spec, tok_spec, line_spec, fixed((hiddens, 128)), *[fixed((feats, 128))] * 3),
        [], 60, (place,),
    )
    sgrad = exchange(sgrad).reshape(rows, mine, width)

    lines = jnp.moveaxis(section, 1, 2).reshape(feats, toks).astype(F32)
    result = dot(wp, hidden, TN) + lines + small[2][:, None]
    result = result.astype(BF).reshape(tp, quarter, toks)
    result = [
        lax.ppermute(lax.dynamic_index_in_dim(result, place[k], 0, False), every, route(k, True)) for k in range(tp)
    ]
    project_grad = dot(hidden, cot, NT)
    expand_grad = dot(normal, pre, NT)

    freq = run(
        "spectrum_back", spectrum_back_kernel, grid, (sgrad, *weighted_t, *lat_f),
        [image_spec, *lon_f, *lat_specs], shape(mine_modes, F32), modes_spec, scratch[1:], 48,
    )
    freq, inner_grad, outer_grad, inner_bias_grad, outer_bias_grad = run(
        "filter_back", filter_back_kernel, (lats // step,), (to_blocks(freq), spec, mid, slope, bend, w1, w2),
        [*[block_spec] * 5, square_spec, square_spec],
        (shape(block_modes, F32), *[shape((2 * BLOCK, 2 * BLOCK), F32)] * 2, *[shape((2 * BLOCK, 128), F32)] * 2),
        (block_spec, *[fixed((2 * BLOCK, 2 * BLOCK))] * 2, *[fixed((2 * BLOCK, 128))] * 2), [], 48,
    )
    grads, one, two, first_gain_sum, first_shift_sum = run(
        "last", functools.partial(last_kernel, owners), grid,
        (*pieces, mean_one, rstd_one, scale1, sgrad, to_features(freq), *plain_n, *lat_b),
        [*piece_specs, stat_spec, stat_spec, feat_spec, image_spec, modes_spec, *lon_b, *lat_specs],
        (shape((rows, mine, width), BF), *[shape((rows, 1, width), F32)] * 2, *[shape((mine, 128), F32)] * 2),
        (image_spec, *[fixed((rows, 1, width))] * 2, *[pl.BlockSpec((some, 128), lambda g, *_: (g, 0))] * 2),
        scratch, 56, (origin,),
    )
    grads = grads.reshape(owners, per, mine, width)
    outs = []
    for k in range(owners):
        piece = lax.dynamic_index_in_dim(grads, me ^ k, 0, False)
        outs.append(lax.ppermute(piece, sp, [(a, a ^ k) for a in range(owners)]) if k else piece)
    sums = jnp.stack([one.reshape(owners, per, width), two.reshape(owners, per, width)], 1)
    sums = lax.all_to_all(sums, sp, 0, 0, tiled=True).reshape(planes, inner, 2, per, 1, width)
    sums = lax.psum(jnp.sum(sums, 1), "t")

    line_specs = [
        pl.BlockSpec((quarter, width), lambda i, h, s, k=k: (0, jnp.where(i == k, h, jnp.where(i < k, 0, per - 1))))
        for k in range(tp)
    ]
    result = run(
        "widen", widen_kernel, (tp, per), result, line_specs, shape((snaps, per, quarter, width), F32),
        pl.BlockSpec((1, 1, quarter, width), lambda i, h, s: (s[i], h, 0, 0)), [], 32, (slot,),
    )
    one_spec = pl.BlockSpec((1, per, 1, width), lambda i, s, b: (s[i], 0, 0, 0))
    patch_spec = pl.BlockSpec((1, per, mine, width), lambda i, s, b: (s[i], 0, b[i], 0))
    patches_grad = run(
        "finish", functools.partial(finish_kernel, owners, feats), (owners,),
        (*outs, patches, stats[:, :, 0, None], stats[:, :, 1, None], sums[:, 0], sums[:, 1]),
        [*[fixed((per, mine, width))] * owners, patch_spec, *[one_spec] * 4],
        shape((snaps, per, quarter, width), F32), patch_spec, [], 48, (origin // inner, origin % inner),
    )

    def own(array, dim):
        array = lax.psum_scatter(array, "t", scatter_dimension=dim[0], tiled=True)
        return lax.psum_scatter(array, sp, scatter_dimension=dim[1], tiled=True)

    project_sum = own(project_grad, (0, 1))
    expand_sum = own(expand_grad, (1, 0))

    def with_bias(full, bias):
        bias = jnp.sum(bias, 1).reshape(2, BLOCK)
        return jnp.concatenate([weight_pair(full), bias[:, :, None]], 2)

    both = jnp.stack([with_bias(inner_grad, inner_bias_grad), with_bias(outer_grad, outer_bias_grad)])
    both = jnp.moveaxis(both, 2, 0)[:, :, :, None]
    both = lax.dynamic_update_slice(
        jnp.zeros((BLOCK, 2, 2, blocks_local, BLOCK + 1), F32), both, (0, 0, 0, y, 0)
    )
    both = lax.psum_scatter(both, sp, scatter_dimension=0, tiled=True)
    both = jnp.moveaxis(both, 0, 3)
    early = jnp.concatenate(
        [jnp.sum(gain_sum, 1), jnp.sum(shift_sum, 1), jnp.sum(cot_sum, 1), jnp.sum(bias_sum, 1), jnp.sum(share)[None]]
    )
    early = lax.psum(early, every)
    last = jnp.stack([jnp.sum(first_gain_sum, 1) * keep, jnp.sum(first_shift_sum, 1) * keep])
    last = lax.psum(
        lax.dynamic_update_slice(jnp.zeros((2, feats), F32), last, (0, t * quarter + r * mine)), every
    )
    return (
        result, patches_grad, last[0], last[1], both[0, ..., :BLOCK], both[0, ..., BLOCK],
        both[1, ..., :BLOCK], both[1, ..., BLOCK],
        early[:feats], early[feats : 2 * feats], expand_sum, early[3 * feats : 3 * feats + hiddens],
        project_sum, early[2 * feats : 3 * feats], early[-1] / (snaps * rows * modes * feats * 2),
    )


def solution(mesh):
    tp = mesh.shape["tp"]
    planes = tp
    inner = mesh.shape["sp"] // planes
    blocks_local = 2
    cut = inner // blocks_local
    mesh = Mesh(mesh.devices.reshape(planes, blocks_local, cut, tp), ("z", "y", "j", "t"))
    sp = ("z", "y", "j")
    image = P(None, sp, "t", None)
    return jax.shard_map(
        functools.partial(per_device, (planes, blocks_local, cut, tp)),
        mesh=mesh,
        in_specs=(
            image, P(None, "t"), P("t"), P("t"),
            P(None, "t", None, None), P(None, "t", None), P(None, "t", None, None), P(None, "t", None),
            P("t"), P("t"), P(None, "t"), P("t"), P("t", None), P("t"), image,
        ),
        out_specs=(
            image, image, P(), P(),
            P(None, "t", sp, None), P(None, "t", sp), P(None, "t", sp, None), P(None, "t", sp),
            P(), P(), P(sp, "t"), P(), P("t", sp), P(), P(),
        ),
        check_vma=False,
    )
```

```python
import functools
import math

import jax
import jax.numpy as jnp
import numpy as np
from jax import lax
from jax.experimental import pallas as pl
from jax.experimental.pallas import tpu as pltpu
from jax.sharding import Mesh, PartitionSpec as P

BLOCK = 96
SHRINK = 0.01
NORM_EPS = 1e-05
BF = jnp.bfloat16
F32 = jnp.float32
FLOPS, BYTES = 1_000_000_000, 3_400_000
NN = (((1,), (0,)), ((), ()))
NT = (((1,), (1,)), ((), ()))
TN = (((0,), (0,)), ((), ()))
ERF_T = 0.3275911
ERF_POLY = (0.254829592, -0.284496736, 1.421413741, -1.453152027, 1.061405429)


def dot(left, right, dims=NN):
    return lax.dot_general(left, right, dims, preferred_element_type=F32)


def gelu_pair(value):
    root = jnp.abs(value) * (1.0 / math.sqrt(2.0))
    t = 1.0 / (1.0 + ERF_T * root)
    bell = jnp.exp(-0.5 * value * value)
    poly = 0.5 * ERF_POLY[4]
    for coef in ERF_POLY[3::-1]:
        poly = poly * t + 0.5 * coef
    tail = poly * t * bell
    phi = jnp.where(value >= 0, 1.0 - tail, tail)
    return value * phi, phi + value * bell * (1.0 / math.sqrt(2.0 * math.pi))


def split(value):
    high = value.astype(BF)
    return high, (value - high.astype(F32)).astype(BF)


def np_split(table):
    high = table.astype(np.float32).astype(jnp.bfloat16)
    low = (table - high.astype(np.float64)).astype(np.float32).astype(jnp.bfloat16)
    return jnp.asarray(high), jnp.asarray(low)


def lon_tables(width, modes):
    angle = 2.0 * np.pi * (np.outer(np.arange(modes), np.arange(width)) % width) / width
    scale = 1.0 / math.sqrt(width)
    cos, sin = np.cos(angle) * scale, np.sin(angle) * scale
    doubled = np.where(np.arange(modes) == 0, 1.0, 2.0)[:, None]
    plain = np.concatenate([cos, -sin], 0)
    weighted = np.concatenate([cos * doubled, -sin * doubled], 0)
    return plain, weighted


def lat_table(rows):
    angle = 2.0 * np.pi * (np.outer(np.arange(rows), np.arange(rows)) % rows) / rows
    scale = 1.0 / math.sqrt(rows)
    cos, sin = np.cos(angle) * scale, np.sin(angle) * scale
    return np.block([[cos, sin], [-sin, cos]])


def fold_lanes(value):
    total = value[:, :128]
    for at in range(128, value.shape[1], 128):
        total = total + value[:, at : at + 128]
    return total


def collect(place, pieces, field):
    per = pieces[0].shape[0]
    for k, piece in enumerate(pieces):
        field[pl.ds(place[k] * per, per)] = piece[...].astype(F32)


def plane_forward(parts, table, lat_hi, lat_lo, lons, spectra):
    rows, modes = lat_hi.shape[0] // 2, spectra.shape[1]
    feats = spectra.shape[0] // (2 * rows)
    table_hi, table_lo = table
    total = dot(parts[0], table_lo)
    if len(parts) > 1:
        total = total + dot(parts[1], table_hi)
    total = total + dot(parts[0], table_hi)
    for c in range(2):
        lons[c] = total[:, c * modes : (c + 1) * modes]
    for f in range(0, feats, 2):
        pair = []
        for g in (f, f + 1):
            pair.append(jnp.concatenate([lons[c, pl.ds(g, rows, stride=feats), :] for c in range(2)], axis=0))
        high, low = split(jnp.concatenate(pair, axis=1))
        out = dot(lat_hi, high) + (dot(lat_lo, high) + dot(lat_hi, low))
        for i, g in enumerate((f, f + 1)):
            spectra[pl.ds(g, 2 * rows, stride=feats), :] = out[:, i * modes : (i + 1) * modes]


def plane_inverse(table, lat_hi, lat_lo, lons, spectra):
    rows, modes = lat_hi.shape[0] // 2, spectra.shape[1]
    feats = spectra.shape[0] // (2 * rows)
    table_hi, table_lo = table
    for f in range(0, feats, 2):
        pair = [spectra[pl.ds(g, 2 * rows, stride=feats), :] for g in (f, f + 1)]
        high, low = split(jnp.concatenate(pair, axis=1))
        out = dot(lat_hi, high) + (dot(lat_lo, high) + dot(lat_hi, low))
        for i, g in enumerate((f, f + 1)):
            for c in range(2):
                lons[c, pl.ds(g, rows, stride=feats), :] = out[c * rows : (c + 1) * rows, i * modes : (i + 1) * modes]
    high, low = split(jnp.concatenate([lons[0], lons[1]], axis=1))
    return dot(high, table_hi) + (dot(high, table_lo) + dot(low, table_hi))


def spectrum_kernel(n, place, *refs):
    pieces, (mean, rstd, scale, shift, hi, lo, lat_hi, lat_lo, spec, field, lons, spectra) = refs[:n], refs[n:]
    collect(place, pieces, field)
    mixed = (field[...] - mean[...]) * rstd[...] * scale[...] + shift[...]
    rows, feats, width = mixed.shape
    parts = split(mixed.reshape(rows * feats, width))
    plane_forward(parts, (hi[...], lo[...]), lat_hi[...], lat_lo[...], lons, spectra)
    spec[...] = spectra[...].reshape(spec.shape).astype(BF)


def join_lines(parts):
    value = jnp.concatenate([part[...] for part in parts], axis=1)
    return value.reshape(value.shape[0] * value.shape[1], *value.shape[2:])


def spectrum_back_kernel(n, *refs):
    parts, (hi, lo, lat_hi, lat_lo, freq, lons, spectra) = refs[:n], refs[n:]
    value = join_lines(parts)
    rows, feats, width = value.shape
    if feats % 16:
        value = value.astype(F32).reshape(rows * feats, width).astype(BF)
    else:
        value = value.reshape(rows * feats, width)
    plane_forward((value,), (hi[...], lo[...]), lat_hi[...], lat_lo[...], lons, spectra)
    freq[...] = spectra[...].reshape(freq.shape)


def two_modes(ref, ky):
    return jnp.concatenate([jnp.concatenate([ref[0, k], ref[1, k]], axis=0) for k in (ky, ky + 1)], axis=1)


def put_modes(ref, ky, value):
    feats, modes = ref.shape[2], ref.shape[3]
    for i in range(2):
        for c in range(2):
            ref[c, ky + i] = value[c * feats : (c + 1) * feats, i * modes : (i + 1) * modes]


def filter_kernel(spec, w1, bias1, w2, bias2, kept, mid, slope, bend, share):
    @pl.when(pl.program_id(0) == 0)
    def _():
        share[...] = jnp.zeros_like(share)

    for ky in range(0, spec.shape[1], 2):
        act, deriv = gelu_pair(dot(w1[...], two_modes(spec, ky)) + bias1[...])
        act = act.astype(BF)
        put_modes(mid, ky, act)
        put_modes(slope, ky, deriv)
        second = dot(w2[...], act) + bias2[...]
        bent = jnp.tanh(second * (1.0 / SHRINK))
        square = bent * bent
        put_modes(bend, ky, square)
        put_modes(kept, ky, second - SHRINK * bent)
        share[...] += jnp.sum((1.0 - square).reshape(-1, 8, square.shape[1]), axis=0)


def filter_back_kernel(
    freq, spec, mid, slope, bend, w1, w2, sgrad, inner, outer, inner_bias, outer_bias
):
    @pl.when(pl.program_id(0) == 0)
    def _():
        for ref in (inner, outer, inner_bias, outer_bias):
            ref[...] = jnp.zeros_like(ref)

    for ky in range(0, spec.shape[1], 2):
        two = (two_modes(freq, ky) * two_modes(bend, ky)).astype(BF)
        outer[...] += dot(two_modes(mid, ky), two, NT)
        outer_bias[...] += fold_lanes(two.astype(F32))
        one = (dot(w2[...], two, TN) * two_modes(slope, ky)).astype(BF)
        inner[...] += dot(two_modes(spec, ky), one, NT)
        inner_bias[...] += fold_lanes(one.astype(F32))
        put_modes(sgrad, ky, dot(w1[...], one, TN))


def section_kernel(n, place, *refs):
    pieces, (mean, rstd, scale, shift, kept, hi, lo, lat_hi, lat_lo), rest = refs[:n], refs[n : n + 9], refs[n + 9 :]
    outs, (field, lons, spectra) = rest[:-3], rest[-3:]
    spectra[...] = kept[...].reshape(spectra.shape)
    collect(place, pieces, field)
    value = field[...]
    mixed = (value - mean[...]) * rstd[...] * scale[...] + shift[...]
    spectral = plane_inverse((hi[...], lo[...]), lat_hi[...], lat_lo[...], lons, spectra)
    section = (value + mixed + spectral.reshape(value.shape)).astype(BF)
    per = pieces[0].shape[0]
    section = section.reshape(value.shape[0] // per, per, *value.shape[1:])
    at = 0
    for out in outs:
        out[...] = section[:, at : at + out.shape[1]]
        at += out.shape[1]


def last_kernel(n, m, place, *refs):
    pieces, sgrad = refs[:n], refs[n : n + m]
    mean, rstd, scale, freq, hi, lo, lat_hi, lat_lo, out, one, two, gain_sum, shift_sum, field, lons, spectra = refs[n + m :]
    spectra[...] = freq[...].reshape(spectra.shape)
    collect(place, pieces, field)
    normed = (field[...] - mean[...]) * rstd[...]
    grad = join_lines(sgrad).astype(F32)
    mixed = grad + plane_inverse((hi[...], lo[...]), lat_hi[...], lat_lo[...], lons, spectra).reshape(grad.shape)
    gain_sum[...] = fold_lanes(jnp.sum(mixed * normed, axis=0))
    shift_sum[...] = fold_lanes(jnp.sum(mixed, axis=0))
    scaled = mixed * scale[...]
    out[...] = (grad + rstd[...] * scaled).astype(BF)

    @pl.when(pl.program_id(0) == 0)
    def _():
        one[...] = jnp.zeros_like(one)
        two[...] = jnp.zeros_like(two)

    one[...] += jnp.sum(scaled, axis=1, keepdims=True)
    two[...] += jnp.sum(scaled * normed, axis=1, keepdims=True)


def column_norm(value):
    mean = jnp.mean(value, axis=0, keepdims=True)
    centered = value - mean
    var = jnp.mean(centered * centered, axis=0, keepdims=True)
    rstd = lax.rsqrt(var + NORM_EPS)
    return centered * rstd, rstd


def feed_kernel(
    n, quarter, chunk, place, *refs
):
    cots = refs[:n]
    section, we_t, wp, we, bias, gain, shift = refs[n : n + 7]
    normal, hidden, pre, cot, sgrad, bias_sum, gain_sum, shift_sum, cot_sum = refs[-9:]

    @pl.when(pl.program_id(0) == 0)
    def _():
        for ref in (bias_sum, gain_sum, shift_sum, cot_sum):
            ref[...] = jnp.zeros_like(ref)

    for k, piece in enumerate(cots):
        cot[pl.ds(place[k] * quarter, quarter), :] = piece[0]
    normed, rstd = column_norm(section[...].astype(F32).reshape(normal.shape))
    value = (normed * gain[...] + shift[...]).astype(BF)
    normal[...] = value
    wide = cot[...]
    part = we.shape[2]
    total = None
    for start in range(0, hidden.shape[0], chunk):
        rows = slice(start, start + chunk)
        before = dot(we_t[rows], value) + jnp.concatenate([bias[rows]] * (value.shape[1] // 128), axis=1)
        act, slope = gelu_pair(before)
        hidden[rows] = act.astype(BF)
        grad = (dot(wp[rows], wide) * slope).astype(BF)
        pre[rows] = grad
        bias_sum[rows] += fold_lanes(grad.astype(F32))
        t, at = start // part, start % part
        term = dot(we[t, :, at : at + chunk], grad)
        total = term if total is None else total + term
    gain_sum[...] += fold_lanes(total * normed)
    shift_sum[...] += fold_lanes(total)
    wide = wide.astype(F32)
    cot_sum[...] += fold_lanes(wide)
    scaled = total * gain[...]
    one = jnp.mean(scaled, axis=0, keepdims=True)
    two = jnp.mean(scaled * normed, axis=0, keepdims=True)
    grad = wide + rstd * (scaled - one - normed * two)
    sgrad[...] = grad.reshape(sgrad.shape).astype(BF)


def result_kernel(quarter, n, place, hidden, wp_t, bias, *refs):
    sections, outs, field = refs[:n], refs[n:-1], refs[-1]
    value = dot(wp_t[...], hidden[...]) + jnp.concatenate([bias[...]] * (hidden.shape[1] // 128), axis=1)
    at = 0
    for section in sections:

        @pl.when((pl.program_id(0) >= at) & (pl.program_id(0) < at + section.shape[1]))
        def _(section=section, at=at):
            line = section[:, pl.program_id(0) - at].astype(F32)
            field[...] = value + line.reshape(value.shape)

        at += section.shape[1]
    for k, out in enumerate(outs):
        out[...] = field[pl.ds(place[k] * quarter, quarter), :].astype(BF)


def weight_kernel(place, normal, pre, cot, hidden, expand, project):
    expand[0] = dot(normal[...], pre[...], NT)
    project[0] = dot(cot[...], hidden[...], NT)


def widen_kernel(slot, p0, p1, p2, p3, out):
    for k, piece in enumerate((p0, p1, p2, p3)):

        @pl.when(pl.program_id(0) == k)
        def _(piece=piece):
            out[0, 0] = piece[...].astype(F32)


def finish_kernel(feats, grads, patches, mean, rstd, one, two, out):
    normed = (patches[0].astype(F32) - mean[0]) * rstd[0]
    out[0] = grads[0].astype(F32) - rstd[0] * (one[0] + normed * two[0]) * (1.0 / feats)


def whole(shape):
    return pl.BlockSpec(shape, lambda *_: (0,) * len(shape), pipeline_mode=pl.Buffered(1))


def fixed(shape):
    return pl.BlockSpec(shape, lambda *_: (0,) * len(shape))


def run(name, kernel, grid, ins, specs, outs, out_specs, scratch, mib, micros, scalars=(), aliases=None):
    grid_spec = pltpu.PrefetchScalarGridSpec(
        num_scalar_prefetch=len(scalars), grid=grid, in_specs=specs, out_specs=out_specs, scratch_shapes=scratch
    )
    call = pl.pallas_call(
        kernel,
        grid_spec=grid_spec,
        out_shape=outs,
        compiler_params=pltpu.CompilerParams(vmem_limit_bytes=mib << 20),
        input_output_aliases=aliases or {},
        cost_estimate=pl.CostEstimate(flops=int(micros * FLOPS), bytes_accessed=int(micros * BYTES), transcendentals=0),
        name=name,
    )
    return call(*scalars, *ins)


def complex_weight(pair):
    real, imag = pair[0].T, pair[1].T
    return jnp.concatenate([jnp.concatenate([real, -imag], 1), jnp.concatenate([imag, real], 1)], 0)


def weight_pair(full):
    full = full.reshape(2, BLOCK, 2, BLOCK)
    return jnp.stack([full[0, :, 0] + full[1, :, 1], full[0, :, 1] - full[1, :, 0]])


def per_device(
    sizes, patches, present, first_gain, first_shift, filter_inner, inner_bias, filter_outer, outer_bias,
    second_gain, second_shift, expand_weight, expand_bias, project_weight, project_bias, cotangent,
):
    planes, blocks_local, cut, tp = sizes
    inner = blocks_local * cut
    ranks = inner * tp
    owners = planes * inner
    snaps, per, quarter, width = patches.shape
    feats = quarter * tp
    mine = quarter // inner
    modes = width // 2
    rows = per * ranks
    toks = per * width
    hidden_local = expand_bias.shape[0]
    hiddens = hidden_local * tp
    z, y, j, t = (lax.axis_index(name) for name in ("z", "y", "j", "t"))
    r = y * cut + j
    me = z * inner + r
    every, sp = ("z", "y", "j", "t"), ("z", "y", "j")
    shape = jax.ShapeDtypeStruct

    def to_plane(array):
        array = array.reshape(snaps, per, inner, mine, width)
        out = []
        for k in range(owners):
            there = me ^ k
            piece = lax.dynamic_slice(
                array, (there // inner, 0, there % inner, 0, 0), (1, per, 1, mine, width)
            ).reshape(per, mine, width)
            out.append(lax.ppermute(piece, sp, [(a, a ^ k) for a in range(owners)]) if k else piece)
        return out

    pieces = to_plane(patches)
    origin = jnp.stack([me ^ k for k in range(owners)]).astype(jnp.int32)

    def route(k, back):
        pairs = [
            ((zz * inner + rr) * tp + tt, (((tt + k) % tp) * inner + rr) * tp + zz)
            for zz in range(planes)
            for rr in range(inner)
            for tt in range(tp)
        ]
        return [(b, a) for a, b in pairs] if back else pairs

    place = jnp.stack([(z - k) % tp for k in range(tp)]).astype(jnp.int32)
    slot = jnp.stack([(t + k) % tp for k in range(tp)]).astype(jnp.int32)
    parts = [per // 2, per - per // 2]
    late, pieces = lax.optimization_barrier((cotangent, pieces))

    def cot_part(array, start, n):
        array = lax.slice_in_dim(array, start, start + n, axis=1)
        return [
            lax.ppermute(lax.dynamic_index_in_dim(array, (t + k) % tp, 0, False), every, route(k, False))
            for k in range(tp)
        ]

    cots = [cot_part(late, 0, parts[0])]

    field = patches.astype(F32)
    mean = jnp.mean(field, 2)
    square = jnp.sum(jnp.square(field - mean[:, :, None]), 2)
    moments = (2, snaps, per, width)
    count = math.prod(moments)
    packed = jnp.concatenate(
        [jnp.stack([mean, square]).reshape(-1), second_gain, second_shift, project_bias, expand_bias]
    )
    packed = lax.all_gather(packed, "t")
    gathered = packed[:, :count].reshape(tp, *moments)
    small = [packed[:, count + i * quarter : count + (i + 1) * quarter].reshape(-1) for i in range(3)]
    bias_all = packed[:, count + 3 * quarter :].reshape(-1)
    mean = jnp.mean(gathered[:, 0], 0)
    square = jnp.sum(gathered[:, 1] + quarter * jnp.square(gathered[:, 0] - mean), 0)
    stats = jnp.stack([mean, lax.rsqrt(square / feats + NORM_EPS)], 2)
    sent = jnp.broadcast_to(stats[:, None], (snaps, inner, per, 2, width)).reshape(owners, per, 2, width)
    plane_stats = lax.all_to_all(sent, sp, 0, 0, tiled=True).reshape(rows, 2, 1, width)
    mean_one, rstd_one = plane_stats[:, 0], plane_stats[:, 1]

    def lanes(vector, width=width):
        return jnp.broadcast_to(vector[:, None], (vector.shape[0], width))

    def own_features(vector):
        return lax.dynamic_slice_in_dim(vector, r * mine, mine)

    keep = own_features(lax.dynamic_index_in_dim(present, z, 0, False).astype(F32))
    scale1, shift1 = lanes(own_features(first_gain) * keep), lanes(own_features(first_shift) * keep)

    def own_block(array):
        return lax.dynamic_index_in_dim(array, y, 1, False)

    w1, w2 = complex_weight(own_block(filter_inner)), complex_weight(own_block(filter_outer))
    bias1 = lanes(own_block(inner_bias).reshape(-1), 2 * modes)
    bias2 = lanes(own_block(outer_bias).reshape(-1), 2 * modes)
    plain, weighted = lon_tables(width, modes)
    lat = lat_table(rows)
    plain_t, weighted_t, plain_n, weighted_n = (np_split(a) for a in (plain.T, weighted.T, plain, weighted))
    lat_f, lat_b = np_split(lat), np_split(lat.T)

    we = lax.all_gather(expand_weight, "t")
    wp = lax.all_gather(project_weight, "t", tiled=True)
    we_t, wp_t = jnp.swapaxes(we, 1, 2).reshape(hiddens, feats), wp.T
    gain2, shift2, bias_lanes = lanes(small[0]), lanes(small[1]), lanes(bias_all, 128)

    some = 16 if mine % 16 == 0 else mine
    grid = (mine // some,)
    piece_specs = [pl.BlockSpec((per, some, width), lambda g, *_: (0, g, 0))] * owners
    stat_spec, feat_spec = whole((rows, 1, width)), pl.BlockSpec((some, width), lambda g, *_: (g, 0))
    lon_f, lon_b = [whole((width, 2 * modes))] * 2, [whole((2 * modes, width))] * 2
    lat_specs = [whole((2 * rows, 2 * rows))] * 2
    image_spec = pl.BlockSpec((rows, some, width), lambda g, *_: (0, g, 0))
    modes_spec = pl.BlockSpec((2, rows, some, modes), lambda g, *_: (0, 0, g, 0))
    scratch = [
        pltpu.VMEM((rows, some, width), F32),
        pltpu.VMEM((2, rows * some, modes), F32),
        pltpu.VMEM((2 * rows * some, modes), F32),
    ]
    mine_modes = (2, rows, mine, modes)
    spec = run(
        "spectrum", functools.partial(spectrum_kernel, owners), grid,
        (*pieces, mean_one, rstd_one, scale1, shift1, *plain_t, *lat_f),
        [*piece_specs, stat_spec, stat_spec, feat_spec, feat_spec, *lon_f, *lat_specs],
        shape(mine_modes, BF), modes_spec, scratch, 48, 22, (origin,),
    )

    def to_blocks(array):
        return lax.all_to_all(array, "j", 1, 2, tiled=True) if cut > 1 else array

    def to_features(array):
        return lax.all_to_all(array, "j", 2, 1, tiled=True) if cut > 1 else array

    spec = to_blocks(spec)
    lats = rows // cut
    step = 8
    block_modes = (2, lats, BLOCK, modes)
    block_spec = pl.BlockSpec((2, step, BLOCK, modes), lambda g: (0, g, 0, 0))
    square_spec, lane_spec = whole((2 * BLOCK, 2 * BLOCK)), whole((2 * BLOCK, 2 * modes))
    kept, mid, slope, bend, share = run(
        "filter", filter_kernel, (lats // step,), (spec, w1, bias1, w2, bias2),
        [block_spec, square_spec, lane_spec, square_spec, lane_spec],
        (shape(block_modes, F32), shape(block_modes, BF), shape(block_modes, F32), shape(block_modes, F32),
         shape((8, 2 * modes), F32)),
        (block_spec, block_spec, block_spec, block_spec, fixed((8, 2 * modes))), [], 48, 17,
    )
    kept, late, cots[0] = lax.optimization_barrier((kept, late, cots[0]))
    cots.append(cot_part(late, parts[0], parts[1]))
    part_specs = [pl.BlockSpec((ranks, n, some, width), lambda g, *_: (0, 0, g, 0)) for n in parts]
    sections = run(
        "section", functools.partial(section_kernel, owners), grid,
        (*pieces, mean_one, rstd_one, scale1, shift1, to_features(kept), *weighted_n, *lat_b),
        [*piece_specs, stat_spec, stat_spec, feat_spec, feat_spec, modes_spec, *lon_b, *lat_specs],
        [shape((ranks, n, mine, width), BF) for n in parts], part_specs, scratch, 56, 17, (origin,),
    )

    def exchange(array):
        return lax.all_to_all(array, ("t", "y", "j"), 0, 0, tiled=True)

    outs = (
        shape((feats, toks), BF), shape((hiddens, toks), BF), shape((hiddens, toks), BF), shape((feats, toks), BF),
    )
    sum_shapes = [shape((hiddens, 128), F32), *[shape((feats, 128), F32)] * 3]
    sgrads, sums, done, start = [], [], (), 0
    received = []
    for n, section, part_cots in zip(parts, sections, cots):
        section = exchange(section)
        tok_spec = pl.BlockSpec((feats, width), lambda h, *_, start=start: (0, h + start))
        hid_spec = pl.BlockSpec((hiddens, width), lambda h, *_, start=start: (0, h + start))
        cot_specs = [pl.BlockSpec((1, quarter, width), lambda h, *_: (h, 0, 0))] * tp
        line_spec = pl.BlockSpec((ranks, 1, mine, width), lambda h, *_: (0, h, 0, 0))
        any_spec = pl.BlockSpec(memory_space=pl.ANY)
        *done, sgrad, s0, s1, s2, s3 = run(
            "feed", functools.partial(feed_kernel, tp, quarter, min(512, hidden_local // 2)), (n,),
            (*part_cots, section, we_t, wp, we, bias_lanes, gain2, shift2, *done),
            [*cot_specs, line_spec, whole((hiddens, feats)), whole((hiddens, feats)),
             whole((tp, feats, hidden_local)), whole((hiddens, 128)), whole((feats, width)), whole((feats, width)),
             *[any_spec] * len(done)],
            (*outs, shape((ranks, n, mine, width), BF), *sum_shapes),
            (tok_spec, hid_spec, hid_spec, tok_spec, line_spec, fixed((hiddens, 128)), *[fixed((feats, 128))] * 3),
            [], 60, 43, (place,), {8 + tp + i: i for i in range(len(done))},
        )
        sgrads.append(exchange(sgrad))
        sums.append((s0, s1, s2, s3))
        received.append(section)
        start += n
    normal, hidden, pre, cot = done
    bias_sum, gain_sum, shift_sum, cot_sum = (a + b for a, b in zip(*sums))

    piece_out = pl.BlockSpec((quarter, width), lambda h, *_: (0, h))
    result = run(
        "result", functools.partial(result_kernel, quarter, len(parts)), (per,),
        (hidden, wp_t, lanes(small[2], 128), *received),
        [pl.BlockSpec((hiddens, width), lambda h, *_: (0, h)), whole((feats, hiddens)), whole((feats, 128)),
         *[pl.BlockSpec((ranks, n, mine, width), lambda *_: (0, 0, 0, 0), pipeline_mode=pl.Buffered(1)) for n in parts]],
        [shape((quarter, toks), BF)] * tp, [piece_out] * tp, [pltpu.VMEM((feats, width), F32)], 48, 22, (place,),
    )
    result = [lax.ppermute(result[k], every, route(k, True)) for k in range(tp)]

    freq = run(
        "spectrum_back", functools.partial(spectrum_back_kernel, len(parts)), grid, (*sgrads, *weighted_t, *lat_f),
        [*part_specs, *lon_f, *lat_specs], shape(mine_modes, F32), modes_spec, scratch[1:], 48, 17,
    )
    freq, inner_grad, outer_grad, inner_bias_grad, outer_bias_grad = run(
        "filter_back", filter_back_kernel, (lats // step,), (to_blocks(freq), spec, mid, slope, bend, w1, w2),
        [*[block_spec] * 5, square_spec, square_spec],
        (shape(block_modes, F32), *[shape((2 * BLOCK, 2 * BLOCK), F32)] * 2, *[shape((2 * BLOCK, 128), F32)] * 2),
        (block_spec, *[fixed((2 * BLOCK, 2 * BLOCK))] * 2, *[fixed((2 * BLOCK, 128))] * 2), [], 48, 24,
    )
    grads, one, two, first_gain_sum, first_shift_sum = run(
        "last", functools.partial(last_kernel, owners, len(parts)), grid,
        (*pieces, *sgrads, mean_one, rstd_one, scale1, to_features(freq), *plain_n, *lat_b),
        [*piece_specs, *part_specs, stat_spec, stat_spec, feat_spec, modes_spec, *lon_b, *lat_specs],
        (shape((rows, mine, width), BF), *[shape((rows, 1, width), F32)] * 2, *[shape((mine, 128), F32)] * 2),
        (image_spec, *[fixed((rows, 1, width))] * 2, *[pl.BlockSpec((some, 128), lambda g, *_: (g, 0))] * 2),
        scratch, 56, 22, (origin,),
    )
    _, normal, hidden, pre, cot = lax.optimization_barrier((first_gain_sum, normal, hidden, pre, cot))
    def with_bias(full, bias):
        bias = jnp.sum(bias, 1).reshape(2, BLOCK)
        return jnp.concatenate([weight_pair(full), bias[:, :, None]], 2)

    filters = jnp.stack([with_bias(inner_grad, inner_bias_grad), with_bias(outer_grad, outer_bias_grad)])
    filters = jnp.moveaxis(filters, 2, 0).reshape(owners, -1)
    early = jnp.concatenate(
        [jnp.sum(gain_sum, 1), jnp.sum(shift_sum, 1), jnp.sum(cot_sum, 1), jnp.sum(bias_sum, 1), jnp.sum(share)[None]]
    )
    line = per * width
    feature_sums = jnp.stack([jnp.sum(first_gain_sum, 1) * keep, jnp.sum(first_shift_sum, 1) * keep]).reshape(-1)
    tail = jnp.concatenate(
        [one.reshape(owners, line), two.reshape(owners, line), filters,
         jnp.broadcast_to(jnp.concatenate([feature_sums, early]), (owners, 2 * mine + early.shape[0]))], 1
    )
    tail = lax.all_to_all(tail, sp, 0, 0, tiled=True)
    tail, grads = lax.optimization_barrier((tail, grads))
    grads = lax.all_to_all(grads.reshape(owners, per, mine, width), sp, 0, 0, tiled=True)
    cuts = [2 * line, 2 * line + filters.shape[1], 2 * line + filters.shape[1] + 2 * mine]
    lines, filters, feature_sums, early = jnp.split(tail, cuts, axis=1)
    lines = jnp.sum(lines.reshape(planes, inner, -1), 1).reshape(-1)
    filters = jnp.sum(filters.reshape(planes, blocks_local, cut, BLOCK // owners, 2, 2, BLOCK + 1), (0, 2))
    filters = jnp.transpose(filters, (2, 3, 0, 1, 4))
    feature_sums = jnp.sum(feature_sums.reshape(planes, inner, 2, mine), 0).swapaxes(0, 1).reshape(-1)
    tail = lax.all_gather(jnp.concatenate([lines, feature_sums, jnp.sum(early, 0)]), "t")
    cuts = [planes * 2 * line, planes * 2 * line + 2 * quarter]
    lines, last, early = jnp.split(tail, cuts, axis=1)
    fixes = jnp.sum(lines, 0).reshape(planes, 2, per, 1, width)
    last = last.reshape(tp, 2, quarter).swapaxes(0, 1).reshape(2, feats)
    early = jnp.sum(early, 0)

    order = jnp.stack([t ^ k for k in range(tp)]).astype(jnp.int32)
    half = hidden_local // 2
    hid_rows = pl.BlockSpec((half, toks), lambda k, i, o: (o[k] * 2 + i, 0))
    out_cols = pl.BlockSpec((1, feats, half), lambda k, i, o: (k, 0, i))
    expand_grad, project_grad = run(
        "weights", weight_kernel, (tp, 2), (normal, pre, cot, hidden),
        [whole((feats, toks)), hid_rows, whole((feats, toks)), hid_rows],
        [shape((tp, feats, hidden_local), F32)] * 2, [out_cols] * 2, [], 60, 44, (order,),
    )

    expand_grad, *result = lax.optimization_barrier((expand_grad, *result))
    line_specs = [
        pl.BlockSpec((quarter, width), lambda i, h, s, k=k: (0, jnp.where(i == k, h, jnp.where(i < k, 0, per - 1))))
        for k in range(tp)
    ]
    result = run(
        "widen", widen_kernel, (tp, per), result, line_specs, shape((snaps, per, quarter, width), F32),
        pl.BlockSpec((1, 1, quarter, width), lambda i, h, s: (s[i], h, 0, 0)), [], 32, 22, (slot,),
    )
    one_spec = pl.BlockSpec((1, per, 1, width), lambda i: (i // inner, 0, 0, 0))
    patch_spec = pl.BlockSpec((1, per, mine, width), lambda i: (i // inner, 0, i % inner, 0))
    patches_grad = run(
        "finish", functools.partial(finish_kernel, feats), (owners,),
        (grads, patches, stats[:, :, 0, None], stats[:, :, 1, None], fixes[:, 0], fixes[:, 1]),
        [pl.BlockSpec((1, per, mine, width), lambda i: (i, 0, 0, 0)), patch_spec, *[one_spec] * 4],
        shape((snaps, per, quarter, width), F32), patch_spec, [], 48, 11,
    )

    def trade(theirs, axes, bit, size):
        return lax.ppermute(theirs.astype(BF), axes, [(a, a ^ bit) for a in range(size)]).astype(F32)

    def trade_rows(array, bit):
        side = (me // bit) % 2
        array = array.reshape(2, array.shape[0] // 2, *array.shape[1:])
        theirs = lax.dynamic_index_in_dim(array, 1 - side, 0, False)
        return lax.dynamic_index_in_dim(array, side, 0, False) + trade(theirs, sp, bit, owners)

    bits = [1 << i for i in range(owners.bit_length() - 1)]

    def total_of(blocks, rows_first):
        blocks = [block.reshape(owners, feats // owners, hidden_local) for block in blocks]
        near = [blocks[k] + trade(blocks[k + 1], "t", 1, tp) for k in range(0, tp, 2)]
        if rows_first:
            near = [n.reshape(owners // 2, 2, feats // owners, hidden_local).swapaxes(0, 1).reshape(n.shape) for n in near]
            near = trade_rows(jnp.concatenate(near, 2), bits[0])
            near = [near[..., i * hidden_local : (i + 1) * hidden_local] for i in range(tp // 2)]
        step = 1
        while len(near) > 1:
            near = [near[i] + trade(near[i + 1], "t", 2 * step, tp) for i in range(0, len(near), 2)]
            step *= 2
        total = near[0]
        if not rows_first:
            total = total.reshape(owners // 2, 2, feats // owners, hidden_local).swapaxes(0, 1)
            total = trade_rows(total.reshape(owners, feats // owners, hidden_local), bits[0])
        for bit in bits[:0:-1]:
            total = trade_rows(total, bit)
        return total[0]

    expand_sum = total_of([expand_grad[k] for k in range(tp)], False)
    project_sum = total_of([project_grad[k] for k in range(tp)], True).T
    return (
        result, patches_grad, last[0], last[1], filters[0, ..., :BLOCK], filters[0, ..., BLOCK],
        filters[1, ..., :BLOCK], filters[1, ..., BLOCK],
        early[:feats], early[feats : 2 * feats], expand_sum, early[3 * feats : 3 * feats + hiddens],
        project_sum, early[2 * feats : 3 * feats], early[-1] / (snaps * rows * modes * feats * 2),
    )


def solution(mesh):
    tp = mesh.shape["tp"]
    planes = tp
    inner = mesh.shape["sp"] // planes
    blocks_local = 2
    cut = inner // blocks_local
    mesh = Mesh(mesh.devices.reshape(planes, blocks_local, cut, tp), ("z", "y", "j", "t"))
    sp = ("z", "y", "j")
    image = P(None, sp, "t", None)
    return jax.shard_map(
        functools.partial(per_device, (planes, blocks_local, cut, tp)),
        mesh=mesh,
        in_specs=(
            image, P(None, "t"), P("t"), P("t"),
            P(None, "t", None, None), P(None, "t", None), P(None, "t", None, None), P(None, "t", None),
            P("t"), P("t"), P(None, "t"), P("t"), P("t", None), P("t"), image,
        ),
        out_specs=(
            image, image, P(), P(),
            P(None, "t", sp, None), P(None, "t", sp), P(None, "t", sp, None), P(None, "t", sp),
            P(), P(), P(sp, "t"), P(), P("t", sp), P(), P(),
        ),
        check_vma=False,
    )
```

```python
import functools
import math

import jax
import jax.numpy as jnp
import numpy as np
from jax import lax
from jax.experimental import pallas as pl
from jax.experimental.pallas import tpu as pltpu
from jax.sharding import Mesh, PartitionSpec as P

BLOCK = 96
SHRINK = 0.01
NORM_EPS = 1e-05
BF = jnp.bfloat16
F32 = jnp.float32
FLOPS, BYTES = 1_000_000_000, 3_400_000
NN = (((1,), (0,)), ((), ()))
NT = (((1,), (1,)), ((), ()))
TN = (((0,), (0,)), ((), ()))
ERF_T = 0.3275911
ERF_POLY = (0.254829592, -0.284496736, 1.421413741, -1.453152027, 1.061405429)


def dot(left, right, dims=NN):
    return lax.dot_general(left, right, dims, preferred_element_type=F32)


def gelu_pair(value):
    root = jnp.abs(value) * (1.0 / math.sqrt(2.0))
    t = 1.0 / (1.0 + ERF_T * root)
    bell = jnp.exp(-0.5 * value * value)
    poly = 0.5 * ERF_POLY[4]
    for coef in ERF_POLY[3::-1]:
        poly = poly * t + 0.5 * coef
    tail = poly * t * bell
    phi = jnp.where(value >= 0, 1.0 - tail, tail)
    return value * phi, phi + value * bell * (1.0 / math.sqrt(2.0 * math.pi))


def split(value):
    high = value.astype(BF)
    return high, (value - high.astype(F32)).astype(BF)


def np_split(table):
    high = table.astype(np.float32).astype(jnp.bfloat16)
    low = (table - high.astype(np.float64)).astype(np.float32).astype(jnp.bfloat16)
    return jnp.asarray(high), jnp.asarray(low)


def lon_tables(width, modes):
    angle = 2.0 * np.pi * (np.outer(np.arange(modes), np.arange(width)) % width) / width
    scale = 1.0 / math.sqrt(width)
    cos, sin = np.cos(angle) * scale, np.sin(angle) * scale
    doubled = np.where(np.arange(modes) == 0, 1.0, 2.0)[:, None]
    plain = np.concatenate([cos, -sin], 0)
    weighted = np.concatenate([cos * doubled, -sin * doubled], 0)
    return plain, weighted


def swapped(index):
    return index % 2 * 2 + index // 2


def swap_planes(array):
    return array.reshape(2, 2, -1, *array.shape[1:]).swapaxes(0, 1).reshape(array.shape)


def lat_table(rows):
    angle = 2.0 * np.pi * (np.outer(np.arange(rows), np.arange(rows)) % rows) / rows
    scale = 1.0 / math.sqrt(rows)
    cos, sin = swap_planes((np.cos(angle) * scale).T).T, swap_planes((np.sin(angle) * scale).T).T
    return np.block([[cos, sin], [-sin, cos]])


def fold_lanes(value):
    total = value[:, :128]
    for at in range(128, value.shape[1], 128):
        total = total + value[:, at : at + 128]
    return total


def collect(pieces):
    value = pieces[...].astype(F32)
    value = value.reshape(4, value.shape[0] // 4 * value.shape[1], *value.shape[2:])
    return jnp.concatenate([value[swapped(i)] for i in range(4)], axis=0)


def lat_product(lat, high, low):
    size = lat.shape[1]
    both = dot(lat, high)
    return both[:size] + (both[size:] + dot(lat[:size], low))


def plane_forward(parts, table, lat, lons, spectra):
    rows, modes = lat.shape[1] // 2, spectra.shape[1]
    feats = spectra.shape[0] // (2 * rows)
    table_hi, table_lo = table
    total = dot(parts[0], table_lo)
    if len(parts) > 1:
        total = total + dot(parts[1], table_hi)
    total = total + dot(parts[0], table_hi)
    for c in range(2):
        lons[c] = total[:, c * modes : (c + 1) * modes]
    for f in range(0, feats, 2):
        pair = []
        for g in (f, f + 1):
            pair.append(jnp.concatenate([lons[c, pl.ds(g, rows, stride=feats), :] for c in range(2)], axis=0))
        high, low = split(jnp.concatenate(pair, axis=1))
        out = lat_product(lat, high, low)
        for i, g in enumerate((f, f + 1)):
            spectra[pl.ds(g, 2 * rows, stride=feats), :] = out[:, i * modes : (i + 1) * modes]


def plane_inverse(table, lat, lons, spectra):
    rows, modes = lat.shape[1] // 2, spectra.shape[1]
    feats = spectra.shape[0] // (2 * rows)
    table_hi, table_lo = table
    for f in range(0, feats, 2):
        pair = [spectra[pl.ds(g, 2 * rows, stride=feats), :] for g in (f, f + 1)]
        high, low = split(jnp.concatenate(pair, axis=1))
        out = lat_product(lat, high, low)
        for i, g in enumerate((f, f + 1)):
            for c in range(2):
                lons[c, pl.ds(g, rows, stride=feats), :] = out[c * rows : (c + 1) * rows, i * modes : (i + 1) * modes]
    high, low = split(jnp.concatenate([lons[0], lons[1]], axis=1))
    return dot(high, table_hi) + (dot(high, table_lo) + dot(low, table_hi))


def spectrum_kernel(pieces, mean, rstd, scale, shift, hi, lo, lat, spec, lons, spectra):
    mixed = (collect(pieces) - mean[...]) * rstd[...] * scale[...] + shift[...]
    rows, feats, width = mixed.shape
    parts = split(mixed.reshape(rows * feats, width))
    plane_forward(parts, (hi[...], lo[...]), lat[...], lons, spectra)
    spec[...] = spectra[...].reshape(spec.shape).astype(BF)


def join_lines(parts):
    value = jnp.concatenate([part[...] for part in parts], axis=1)
    return value.reshape(value.shape[0] * value.shape[1], *value.shape[2:])


def spectrum_back_kernel(n, *refs):
    parts, (hi, lo, lat, freq, lons, spectra) = refs[:n], refs[n:]
    value = join_lines(parts)
    rows, feats, width = value.shape
    if feats % 16:
        value = value.astype(F32).reshape(rows * feats, width).astype(BF)
    else:
        value = value.reshape(rows * feats, width)
    plane_forward((value,), (hi[...], lo[...]), lat[...], lons, spectra)
    freq[...] = spectra[...].reshape(freq.shape)


def two_modes(ref, ky):
    return jnp.concatenate([jnp.concatenate([ref[0, k], ref[1, k]], axis=0) for k in (ky, ky + 1)], axis=1)


def put_modes(ref, ky, value):
    feats, modes = ref.shape[2], ref.shape[3]
    for i in range(2):
        for c in range(2):
            ref[c, ky + i] = value[c * feats : (c + 1) * feats, i * modes : (i + 1) * modes]


def filter_kernel(spec, w1, bias1, w2, bias2, kept, mid, slope, bend, share):
    @pl.when(pl.program_id(0) == 0)
    def _():
        share[...] = jnp.zeros_like(share)

    for ky in range(0, spec.shape[1], 2):
        act, deriv = gelu_pair(dot(w1[...], two_modes(spec, ky)) + bias1[...])
        act = act.astype(BF)
        put_modes(mid, ky, act)
        put_modes(slope, ky, deriv)
        second = dot(w2[...], act) + bias2[...]
        bent = jnp.tanh(second * (1.0 / SHRINK))
        square = bent * bent
        put_modes(bend, ky, square)
        put_modes(kept, ky, second - SHRINK * bent)
        share[...] += jnp.sum((1.0 - square).reshape(-1, 8, square.shape[1]), axis=0)


def filter_back_kernel(
    freq, spec, mid, slope, bend, w1, w2, sgrad, inner, outer, inner_bias, outer_bias
):
    @pl.when(pl.program_id(0) == 0)
    def _():
        for ref in (inner, outer, inner_bias, outer_bias):
            ref[...] = jnp.zeros_like(ref)

    for ky in range(0, spec.shape[1], 2):
        two = (two_modes(freq, ky) * two_modes(bend, ky)).astype(BF)
        outer[...] += dot(two_modes(mid, ky), two, NT)
        outer_bias[...] += fold_lanes(two.astype(F32))
        one = (dot(w2[...], two, TN) * two_modes(slope, ky)).astype(BF)
        inner[...] += dot(two_modes(spec, ky), one, NT)
        inner_bias[...] += fold_lanes(one.astype(F32))
        put_modes(sgrad, ky, dot(w1[...], one, TN))


def section_kernel(pieces, mean, rstd, scale, shift, kept, hi, lo, lat, *refs):
    outs, (lons, spectra) = refs[:-2], refs[-2:]
    spectra[...] = kept[...].reshape(spectra.shape)
    value = collect(pieces)
    mixed = (value - mean[...]) * rstd[...] * scale[...] + shift[...]
    spectral = plane_inverse((hi[...], lo[...]), lat[...], lons, spectra)
    section = (value + mixed + spectral.reshape(value.shape)).astype(BF)
    section = section.reshape(pieces.shape[0], pieces.shape[1], *value.shape[1:])
    at = 0
    for out in outs:
        out[...] = section[:, at : at + out.shape[1]]
        at += out.shape[1]


def last_kernel(n, pieces, *refs):
    sgrad, (mean, rstd, scale, freq, hi, lo, lat, out, sums, gain_sum, shift_sum, lons, spectra) = refs[:n], refs[n:]
    spectra[...] = freq[...].reshape(spectra.shape)
    normed = (collect(pieces) - mean[...]) * rstd[...]
    grad = join_lines(sgrad).astype(F32)
    mixed = grad + plane_inverse((hi[...], lo[...]), lat[...], lons, spectra).reshape(grad.shape)
    gain_sum[...] = fold_lanes(jnp.sum(mixed * normed, axis=0))
    shift_sum[...] = fold_lanes(jnp.sum(mixed, axis=0))
    scaled = mixed * scale[...]
    value = (grad + rstd[...] * scaled).astype(BF)
    block = value.shape[0] // 4
    for i in range(4):
        out[i * block : (i + 1) * block] = value[swapped(i) * block : (swapped(i) + 1) * block]

    @pl.when(pl.program_id(0) == 0)
    def _():
        sums[...] = jnp.zeros_like(sums)

    for c, term in enumerate((scaled, scaled * normed)):
        term = jnp.sum(term, axis=1)
        for i in range(4):
            sums[i * block : (i + 1) * block, c] += term[swapped(i) * block : (swapped(i) + 1) * block]


def column_norm(value):
    mean = jnp.mean(value, axis=0, keepdims=True)
    centered = value - mean
    var = jnp.mean(centered * centered, axis=0, keepdims=True)
    rstd = lax.rsqrt(var + NORM_EPS)
    return centered * rstd, rstd


def feed_kernel(
    n, quarter, chunk, place, *refs
):
    cots = refs[:n]
    section, we_t, wp, we, bias, gain, shift = refs[n : n + 7]
    normal, hidden, pre, cot, sgrad, bias_sum, gain_sum, shift_sum, cot_sum = refs[-9:]

    @pl.when(pl.program_id(0) == 0)
    def _():
        for ref in (bias_sum, gain_sum, shift_sum, cot_sum):
            ref[...] = jnp.zeros_like(ref)

    for k, piece in enumerate(cots):
        cot[pl.ds(place[k] * quarter, quarter), :] = piece[0]
    normed, rstd = column_norm(section[...].astype(F32).reshape(normal.shape))
    value = (normed * gain[...] + shift[...]).astype(BF)
    normal[...] = value
    wide = cot[...]
    part = we.shape[2]
    total = None
    for start in range(0, hidden.shape[0], chunk):
        rows = slice(start, start + chunk)
        before = dot(we_t[rows], value) + jnp.concatenate([bias[rows]] * (value.shape[1] // 128), axis=1)
        act, slope = gelu_pair(before)
        hidden[rows] = act.astype(BF)
        grad = (dot(wp[rows], wide) * slope).astype(BF)
        pre[rows] = grad
        bias_sum[rows] += fold_lanes(grad.astype(F32))
        t, at = start // part, start % part
        term = dot(we[t, :, at : at + chunk], grad)
        total = term if total is None else total + term
    gain_sum[...] += fold_lanes(total * normed)
    shift_sum[...] += fold_lanes(total)
    wide = wide.astype(F32)
    cot_sum[...] += fold_lanes(wide)
    scaled = total * gain[...]
    one = jnp.mean(scaled, axis=0, keepdims=True)
    two = jnp.mean(scaled * normed, axis=0, keepdims=True)
    grad = wide + rstd * (scaled - one - normed * two)
    sgrad[...] = grad.reshape(sgrad.shape).astype(BF)


def result_kernel(quarter, place, hidden, wp_t, bias, section, *refs):
    outs, field = refs[-5:-1], refs[-1]
    value = dot(wp_t[...], hidden[...]) + jnp.concatenate([bias[...]] * (hidden.shape[1] // 128), axis=1)
    field[...] = value + section[...].astype(F32).reshape(value.shape)
    for k, out in enumerate(outs):
        out[...] = field[pl.ds(place[k] * quarter, quarter), :].astype(BF)


def weight_sent_kernel(order, normal, pre, cot, hidden, out):
    out[0, 0] = dot(normal[...], pre[...], NT).astype(BF)
    out[0, 1] = dot(cot[...], hidden[...], NT).astype(BF)


def weight_kept_kernel(order, side, normal, pre, cot, hidden, came, expand_mine, expand_sent, project_mine, project_sent):
    expand = dot(normal[...], pre[...], NT) + came[0, 0].astype(F32)
    project = dot(cot[...], hidden[...], NT) + came[0, 1].astype(F32)

    @pl.when(pl.program_id(0) == 0)
    def _():
        expand_mine[...] = expand

    @pl.when(pl.program_id(0) == 1)
    def _():
        expand_sent[...] = expand.astype(BF)

    blocks = project_mine.shape[1]
    project = project.reshape(blocks, 2, project.shape[0] // (2 * blocks), project.shape[1])
    odd = side[0] == 1
    project_mine[0] = jnp.where(odd, project[:, 1], project[:, 0])
    project_sent[0] = jnp.where(odd, project[:, 0], project[:, 1]).astype(BF)


def widen_kernel(layout, slot, *refs):
    pieces, out = refs[:-1], refs[-1]
    width = out.shape[3]
    for piece, (k, start, n) in zip(pieces, layout):

        @pl.when(pl.program_id(0) == k)
        def _(piece=piece, start=start, n=n):
            for i in range(n):
                out[0, start + i] = piece[:, i * width : (i + 1) * width].astype(F32)


def finish_kernel(feats, grads, patches, mean, rstd, one, two, out):
    normed = (patches[0].astype(F32) - mean[0]) * rstd[0]
    out[0] = grads[0].astype(F32) - rstd[0] * (one[0] + normed * two[0]) * (1.0 / feats)


def whole(shape):
    return pl.BlockSpec(shape, lambda *_: (0,) * len(shape), pipeline_mode=pl.Buffered(1))


def fixed(shape):
    return pl.BlockSpec(shape, lambda *_: (0,) * len(shape))


def run(name, kernel, grid, ins, specs, outs, out_specs, scratch, mib, micros, scalars=(), aliases=None):
    grid_spec = pltpu.PrefetchScalarGridSpec(
        num_scalar_prefetch=len(scalars), grid=grid, in_specs=specs, out_specs=out_specs, scratch_shapes=scratch
    )
    call = pl.pallas_call(
        kernel,
        grid_spec=grid_spec,
        out_shape=outs,
        compiler_params=pltpu.CompilerParams(vmem_limit_bytes=mib << 20),
        input_output_aliases=aliases or {},
        cost_estimate=pl.CostEstimate(flops=int(micros * FLOPS), bytes_accessed=int(micros * BYTES), transcendentals=0),
        name=name,
    )
    return call(*scalars, *ins)


def complex_weight(pair):
    real, imag = pair[0].T, pair[1].T
    return jnp.concatenate([jnp.concatenate([real, -imag], 1), jnp.concatenate([imag, real], 1)], 0)


def weight_pair(full):
    full = full.reshape(2, BLOCK, 2, BLOCK)
    return jnp.stack([full[0, :, 0] + full[1, :, 1], full[0, :, 1] - full[1, :, 0]])


def per_device(
    sizes, patches, present, first_gain, first_shift, filter_inner, inner_bias, filter_outer, outer_bias,
    second_gain, second_shift, expand_weight, expand_bias, project_weight, project_bias, cotangent,
):
    planes, blocks_local, cut, tp = sizes
    inner = blocks_local * cut
    ranks = inner * tp
    owners = planes * inner
    snaps, per, quarter, width = patches.shape
    feats = quarter * tp
    mine = quarter // inner
    modes = width // 2
    rows = per * ranks
    toks = per * width
    hidden_local = expand_bias.shape[0]
    hiddens = hidden_local * tp
    z, y, j, t = (lax.axis_index(name) for name in ("z", "y", "j", "t"))
    r = y * cut + j
    me = z * inner + r
    every, sp = ("z", "y", "j", "t"), ("z", "y", "j")
    shape = jax.ShapeDtypeStruct

    pieces = patches.reshape(snaps, per, inner, mine, width).swapaxes(1, 2).reshape(owners, per, mine, width)
    pieces = lax.all_to_all(pieces, sp, 0, 0, tiled=True)

    def route(k, back):
        pairs = [
            ((zz * inner + rr) * tp + tt, (((swapped(tt) + k) % tp) * inner + rr) * tp + swapped(zz))
            for zz in range(planes)
            for rr in range(inner)
            for tt in range(tp)
        ]
        return [(b, a) for a, b in pairs] if back else pairs

    place = jnp.stack([swapped((z - k) % tp) for k in range(tp)]).astype(jnp.int32)
    slot = jnp.stack([(swapped(t) + k) % tp for k in range(tp)]).astype(jnp.int32)
    field = patches.astype(F32)
    mean = jnp.mean(field, 2)
    square = jnp.sum(jnp.square(field - mean[:, :, None]), 2)
    gathered = lax.all_gather(jnp.stack([mean, square]), "t")
    packed = lax.all_gather(jnp.concatenate([second_gain, second_shift, project_bias, expand_bias]), "t")
    small = [packed[:, i * quarter : (i + 1) * quarter].reshape(-1) for i in range(3)]
    bias_all = packed[:, 3 * quarter :].reshape(-1)
    mean = jnp.mean(gathered[:, 0], 0)
    square = jnp.sum(gathered[:, 1] + quarter * jnp.square(gathered[:, 0] - mean), 0)
    stats = jnp.stack([mean, lax.rsqrt(square / feats + NORM_EPS)], 2)
    plane_stats = []
    for k in range(owners):
        piece = lax.dynamic_index_in_dim(stats, (me ^ k) // inner, 0, False)
        plane_stats.append(lax.ppermute(piece, sp, [(a, a ^ k) for a in range(owners)]) if k else piece)
    plane_stats = jnp.stack(plane_stats)
    bit = 1
    while bit < owners:
        turned = plane_stats.reshape(-1, 2, bit, per, 2, width)
        plane_stats = jnp.where((me // bit) % 2 == 1, turned[:, ::-1], turned).reshape(owners, per, 2, width)
        bit *= 2
    plane_stats = swap_planes(plane_stats.reshape(rows, 2, 1, width))

    def lanes(vector, width=width):
        return jnp.broadcast_to(vector[:, None], (vector.shape[0], width))

    def own_features(vector):
        return lax.dynamic_slice_in_dim(vector, r * mine, mine)

    keep = own_features(lax.dynamic_index_in_dim(present, z, 0, False).astype(F32))
    scale1, shift1 = lanes(own_features(first_gain) * keep), lanes(own_features(first_shift) * keep)

    def own_block(array):
        return lax.dynamic_index_in_dim(array, y, 1, False)

    w1, w2 = complex_weight(own_block(filter_inner)), complex_weight(own_block(filter_outer))
    bias1 = lanes(own_block(inner_bias).reshape(-1), 2 * modes)
    bias2 = lanes(own_block(outer_bias).reshape(-1), 2 * modes)
    plain, weighted = lon_tables(width, modes)
    lat = lat_table(rows)
    plain_t, weighted_t, plain_n, weighted_n = (np_split(a) for a in (plain.T, weighted.T, plain, weighted))
    lat_f, lat_b = (jnp.concatenate(np_split(a)) for a in (lat, lat.T))

    we = lax.all_gather(expand_weight, "t")
    wp = lax.all_gather(project_weight, "t", tiled=True)
    we_t, wp_t = jnp.swapaxes(we, 1, 2).reshape(hiddens, feats), wp.T
    parts = [per // 2, per - per // 2]
    gain2, shift2, bias_lanes = lanes(small[0]), lanes(small[1]), lanes(bias_all, 128)
    cotangents = [
        [lax.dynamic_slice(cotangent, (slot[k], at, 0, 0), (1, n, quarter, width))[0] for k in range(tp)]
        for at, n in zip((0, parts[0]), parts)
    ]
    plane_stats, we, wp, we_t, wp_t, gain2, shift2, bias_lanes = lax.optimization_barrier(
        (plane_stats, we, wp, we_t, wp_t, gain2, shift2, bias_lanes)
    )
    mean_one, rstd_one = plane_stats[:, 0], plane_stats[:, 1]
    late, pieces = lax.optimization_barrier((cotangents, pieces))
    cots = [[lax.ppermute(piece, every, route(k, False)) for k, piece in enumerate(late[0])]]

    some = 16 if mine % 16 == 0 else mine
    grid = (mine // some,)
    piece_spec = pl.BlockSpec((owners, per, some, width), lambda g, *_: (0, 0, g, 0))
    stat_spec, feat_spec = whole((rows, 1, width)), pl.BlockSpec((some, width), lambda g, *_: (g, 0))
    lon_f, lon_b = [whole((width, 2 * modes))] * 2, [whole((2 * modes, width))] * 2
    lat_specs = [whole((4 * rows, 2 * rows))]
    image_spec = pl.BlockSpec((rows, some, width), lambda g, *_: (0, g, 0))
    modes_spec = pl.BlockSpec((2, rows, some, modes), lambda g, *_: (0, 0, g, 0))
    scratch = [
        pltpu.VMEM((2, rows * some, modes), F32),
        pltpu.VMEM((2 * rows * some, modes), F32),
    ]
    mine_modes = (2, rows, mine, modes)
    spec = run(
        "spectrum", spectrum_kernel, grid,
        (pieces, mean_one, rstd_one, scale1, shift1, *plain_t, lat_f),
        [piece_spec, stat_spec, stat_spec, feat_spec, feat_spec, *lon_f, *lat_specs],
        shape(mine_modes, BF), modes_spec, scratch, 48, 22,
    )

    def to_blocks(array):
        return lax.all_to_all(array, "j", 1, 2, tiled=True) if cut > 1 else array

    def to_features(array):
        return lax.all_to_all(array, "j", 2, 1, tiled=True) if cut > 1 else array

    spec = to_blocks(spec)
    lats = rows // cut
    step = 8
    block_modes = (2, lats, BLOCK, modes)
    block_spec = pl.BlockSpec((2, step, BLOCK, modes), lambda g: (0, g, 0, 0))
    square_spec, lane_spec = whole((2 * BLOCK, 2 * BLOCK)), whole((2 * BLOCK, 2 * modes))
    kept, mid, slope, bend, share = run(
        "filter", filter_kernel, (lats // step,), (spec, w1, bias1, w2, bias2),
        [block_spec, square_spec, lane_spec, square_spec, lane_spec],
        (shape(block_modes, F32), shape(block_modes, BF), shape(block_modes, F32), shape(block_modes, F32),
         shape((8, 2 * modes), F32)),
        (block_spec, block_spec, block_spec, block_spec, fixed((8, 2 * modes))), [], 48, 17,
    )
    kept, late, cots[0] = lax.optimization_barrier((kept, late, cots[0]))
    part_specs = [pl.BlockSpec((ranks, n, some, width), lambda g, *_: (0, 0, g, 0)) for n in parts]
    sections = run(
        "section", section_kernel, grid,
        (pieces, mean_one, rstd_one, scale1, shift1, to_features(kept), *weighted_n, lat_b),
        [piece_spec, stat_spec, stat_spec, feat_spec, feat_spec, modes_spec, *lon_b, *lat_specs],
        [shape((ranks, n, mine, width), BF) for n in parts], part_specs, scratch, 56, 17,
    )

    def exchange(array):
        return lax.all_to_all(array, ("t", "y", "j"), 0, 0, tiled=True)

    outs = (
        shape((feats, toks), BF), shape((hiddens, toks), BF), shape((hiddens, toks), BF), shape((feats, toks), BF),
    )
    sum_shapes = [shape((hiddens, 128), F32), *[shape((feats, 128), F32)] * 3]
    sgrads, sums, done, start = [], [], (), 0
    received, results = [], []
    early_rounds, late_rounds = (0, 2), (1, 3)
    for n, section in zip(parts, sections):
        section = exchange(section)
        if not received:
            section, late = lax.optimization_barrier((section, late))
            cots.append([lax.ppermute(piece, every, route(k, False)) for k, piece in enumerate(late[1])])
        tok_spec = pl.BlockSpec((feats, width), lambda h, *_, start=start: (0, h + start))
        hid_spec = pl.BlockSpec((hiddens, width), lambda h, *_, start=start: (0, h + start))
        cot_specs = [pl.BlockSpec((1, quarter, width), lambda h, *_: (h, 0, 0))] * tp
        line_spec = pl.BlockSpec((ranks, 1, mine, width), lambda h, *_: (0, h, 0, 0))
        any_spec = pl.BlockSpec(memory_space=pl.ANY)
        *done, sgrad, s0, s1, s2, s3 = run(
            "feed", functools.partial(feed_kernel, tp, quarter, min(512, hidden_local // 2)), (n,),
            (*cots[len(received)], section, we_t, wp, we, bias_lanes, gain2, shift2, *done),
            [*cot_specs, line_spec, whole((hiddens, feats)), whole((hiddens, feats)),
             whole((tp, feats, hidden_local)), whole((hiddens, 128)), whole((feats, width)), whole((feats, width)),
             *[any_spec] * len(done)],
            (*outs, shape((ranks, n, mine, width), BF), *sum_shapes),
            (tok_spec, hid_spec, hid_spec, tok_spec, line_spec, fixed((hiddens, 128)), *[fixed((feats, 128))] * 3),
            [], 60, 0.01 if start else 43, (place,), {8 + tp + i: i for i in range(len(done))},
        )
        if start:
            sgrad, done, results, sgrads = lax.optimization_barrier((sgrad, done, results, sgrads))
            third = hidden_local // 3
            resident = whole((feats, toks))
            hid_rows = pl.BlockSpec((third, toks), lambda k, i, o, *_: (o[k] * 3 + i, 0))
            both_cols = pl.BlockSpec((1, 2, feats, third), lambda k, i, *_: (k, 0, 0, i))
            normal, hidden, pre, cot = done
            products = (normal, pre, cot, hidden)
            product_specs = [resident, hid_rows, resident, hid_rows]
            sent = run(
                "weights_sent", weight_sent_kernel, (tp // 2, 3), products, product_specs,
                shape((tp // 2, 2, feats, hidden_local), BF), both_cols, [], 60, 0.01,
                (jnp.stack([t ^ k for k in range(1, tp, 2)]).astype(jnp.int32),),
            )
            came = lax.ppermute(sent, "t", [(a, a ^ 1) for a in range(tp)])
        part_out = shape((quarter, n * width), BF)
        rows_out = run(
            "result", functools.partial(result_kernel, quarter), (n,), (done[1], wp_t, lanes(small[2], 128), section),
            [hid_spec, whole((feats, hiddens)), whole((feats, 128)), line_spec],
            [part_out] * tp, [pl.BlockSpec((quarter, width), lambda h, *_: (0, h))] * tp,
            [pltpu.VMEM((feats, width), F32)], 48, 0.01 if start else 43, (place,),
        )
        sgrad = exchange(sgrad)
        if start:
            side = (me % 2).astype(jnp.int32).reshape(1)
            half_rows = owners // 2
            strip = feats // owners
            mine_cols = pl.BlockSpec((feats, third), lambda k, i, *_: (0, jnp.where(k == 0, i, 2)))
            sent_cols = pl.BlockSpec((feats, third), lambda k, i, *_: (0, jnp.where(k == 0, 0, i)))
            row_cols = pl.BlockSpec((1, half_rows, strip, third), lambda k, i, *_: (k, 0, 0, i))
            row_shape = (tp // 2, half_rows, strip, hidden_local)
            kept_products = run(
                "weights_kept", weight_kept_kernel, (tp // 2, 3), (*products, came), [*product_specs, both_cols],
                (shape((feats, hidden_local), F32), shape((feats, hidden_local), BF), shape(row_shape, F32),
                 shape(row_shape, BF)),
                (mine_cols, sent_cols, row_cols, row_cols), [], 60, 0.01,
                (jnp.stack([t ^ k for k in range(0, tp, 2)]).astype(jnp.int32), side),
            )
            sgrad, kept_products = lax.optimization_barrier((sgrad, kept_products))
        else:
            rows_out, done = lax.optimization_barrier((rows_out, done))
        results += [
            lax.ppermute(rows_out[k], every, route(k, True)) for k in (early_rounds if start else range(tp))
        ]
        sgrads.append(sgrad)
        sums.append((s0, s1, s2, s3))
        received.append(section)
        start += n
    bias_sum, gain_sum, shift_sum, cot_sum = (a + b for a, b in zip(*sums))

    def trade(theirs, axes, bit, size):
        return lax.ppermute(theirs, axes, [(a, a ^ bit) for a in range(size)])

    def halves(array, bit):
        other = 1 - (me // bit) % 2
        return lax.dynamic_index_in_dim(array, 1 - other, 0, False), lax.dynamic_index_in_dim(array, other, 0, False)

    expand_mine, expand_sent, project_mine, project_sent = kept_products
    first_came = [trade(expand_sent, "t", 2, tp), trade(project_sent, sp, 1, owners)]

    freq = run(
        "spectrum_back", functools.partial(spectrum_back_kernel, len(parts)), grid, (*sgrads, *weighted_t, lat_f),
        [*part_specs, *lon_f, *lat_specs], shape(mine_modes, F32), modes_spec, scratch, 48, 0.01,
    )
    freq, results, first_came, rows_out = lax.optimization_barrier((freq, results, first_came, rows_out))
    results += [lax.ppermute(rows_out[k], every, route(k, True)) for k in late_rounds]
    expand = expand_mine + first_came[0].astype(F32)
    project = project_mine + first_came[1].astype(F32)
    expand, theirs = halves(expand.reshape(half_rows, 2, strip, hidden_local).swapaxes(0, 1), 1)
    second_came = [trade(theirs.astype(BF), sp, 1, owners), trade(project[1].astype(BF), "t", 2, tp)]
    freq, inner_grad, outer_grad, inner_bias_grad, outer_bias_grad = run(
        "filter_back", filter_back_kernel, (lats // step,), (to_blocks(freq), spec, mid, slope, bend, w1, w2),
        [*[block_spec] * 5, square_spec, square_spec],
        (shape(block_modes, F32), *[shape((2 * BLOCK, 2 * BLOCK), F32)] * 2, *[shape((2 * BLOCK, 128), F32)] * 2),
        (block_spec, *[fixed((2 * BLOCK, 2 * BLOCK))] * 2, *[fixed((2 * BLOCK, 128))] * 2), [], 48, 0.01,
    )
    freq, second_came = lax.optimization_barrier((freq, second_came))
    expand = expand + second_came[0].astype(F32)
    project = project[0] + second_came[1].astype(F32)
    weights = jnp.stack([expand, project], 1)
    bit = 2
    while bit < inner:
        weights = weights.reshape(-1, 2, *weights.shape[1:])
        weights, theirs = halves(weights.swapaxes(0, 1), bit)
        weights = weights + trade(theirs.astype(BF), sp, bit, owners).astype(F32)
        bit *= 2
    weights = [lax.dynamic_index_in_dim(weights, z, 0, False)] + [
        trade(lax.dynamic_index_in_dim(weights, z ^ k, 0, False).astype(BF), "z", k, planes) for k in range(1, planes)
    ]
    grads, lines, first_gain_sum, first_shift_sum = run(
        "last", functools.partial(last_kernel, len(parts)), grid,
        (pieces, *sgrads, mean_one, rstd_one, scale1, to_features(freq), *plain_n, lat_b),
        [piece_spec, *part_specs, stat_spec, stat_spec, feat_spec, modes_spec, *lon_b, *lat_specs],
        (shape((rows, mine, width), BF), shape((rows, 2, width), F32), *[shape((mine, 128), F32)] * 2),
        (image_spec, fixed((rows, 2, width)), *[pl.BlockSpec((some, 128), lambda g, *_: (g, 0))] * 2),
        scratch, 56, 0.01,
    )
    def with_bias(full, bias):
        bias = jnp.sum(bias, 1).reshape(2, BLOCK)
        return jnp.concatenate([weight_pair(full), bias[:, :, None]], 2)

    filters = jnp.stack([with_bias(inner_grad, inner_bias_grad), with_bias(outer_grad, outer_bias_grad)])
    filters = jnp.moveaxis(filters, 2, 0).reshape(owners, -1)
    early = jnp.concatenate(
        [jnp.sum(gain_sum, 1), jnp.sum(shift_sum, 1), jnp.sum(cot_sum, 1), jnp.sum(bias_sum, 1), jnp.sum(share)[None]]
    )
    grads, lines, results, weights = lax.optimization_barrier((grads, lines, results, weights))
    expand_sum, project_sum = weights[0] + sum(piece.astype(F32) for piece in weights[1:])
    project_sum = project_sum.T
    line = per * width
    feature_sums = jnp.stack([jnp.sum(first_gain_sum, 1) * keep, jnp.sum(first_shift_sum, 1) * keep]).reshape(-1)
    tail = jnp.concatenate(
        [lines.reshape(owners, 2 * line), filters,
         jnp.broadcast_to(jnp.concatenate([feature_sums, early]), (owners, 2 * mine + early.shape[0]))], 1
    )
    tail = lax.all_to_all(tail, sp, 0, 0, tiled=True)
    tail, grads = lax.optimization_barrier((tail, grads))
    grads = lax.all_to_all(grads.reshape(owners, per, mine, width), sp, 0, 0, tiled=True)
    cuts = [2 * line, 2 * line + filters.shape[1], 2 * line + filters.shape[1] + 2 * mine]
    lines, filters, feature_sums, early = jnp.split(tail, cuts, axis=1)
    lines = jnp.sum(lines.reshape(planes, inner, -1), 1).reshape(-1)
    filters = jnp.sum(filters.reshape(planes, blocks_local, cut, BLOCK // owners, 2, 2, BLOCK + 1), (0, 2))
    filters = jnp.transpose(filters, (2, 3, 0, 1, 4))
    feature_sums = jnp.sum(feature_sums.reshape(planes, inner, 2, mine), 0).swapaxes(0, 1)
    spread = lax.dynamic_update_slice(
        jnp.zeros((2, tp, quarter), F32), feature_sums.reshape(2, 1, quarter), (0, t, 0)
    ).reshape(-1)
    tail = jnp.concatenate([lines, spread, jnp.sum(early, 0)])
    bit = 1
    while bit < tp:
        tail = tail + trade(tail, "t", bit, tp)
        bit *= 2
    cuts = [planes * 2 * line, planes * 2 * line + 2 * feats]
    lines, last, early = jnp.split(tail, cuts)
    fixes = lines.reshape(planes, per, 2, 1, width)
    last = last.reshape(2, feats)

    layout = [(k, 0, parts[0]) for k in range(tp)] + [(k, parts[0], parts[1]) for k in (*early_rounds, *late_rounds)]
    result = run(
        "widen", functools.partial(widen_kernel, layout), (tp,), results, [whole((quarter, n * width)) for _, _, n in layout],
        shape((snaps, per, quarter, width), F32),
        pl.BlockSpec((1, per, quarter, width), lambda i, s: (s[i], 0, 0, 0)), [], 32, 8, (slot,),
    )
    one_spec = pl.BlockSpec((1, per, 1, width), lambda i: (i // inner, 0, 0, 0))
    patch_spec = pl.BlockSpec((1, per, mine, width), lambda i: (i // inner, 0, i % inner, 0))
    patches_grad = run(
        "finish", functools.partial(finish_kernel, feats), (owners,),
        (grads, patches, stats[:, :, 0, None], stats[:, :, 1, None], fixes[:, :, 0], fixes[:, :, 1]),
        [pl.BlockSpec((1, per, mine, width), lambda i: (i, 0, 0, 0)), patch_spec, *[one_spec] * 4],
        shape((snaps, per, quarter, width), F32), patch_spec, [], 48, 11,
    )

    return (
        result, patches_grad, last[0], last[1], filters[0, ..., :BLOCK], filters[0, ..., BLOCK],
        filters[1, ..., :BLOCK], filters[1, ..., BLOCK],
        early[:feats], early[feats : 2 * feats], expand_sum, early[3 * feats : 3 * feats + hiddens],
        project_sum, early[2 * feats : 3 * feats], early[-1] / (snaps * rows * modes * feats * 2),
    )


def solution(mesh):
    tp = mesh.shape["tp"]
    planes = tp
    inner = mesh.shape["sp"] // planes
    blocks_local = 2
    cut = inner // blocks_local
    mesh = Mesh(mesh.devices.reshape(planes, blocks_local, cut, tp), ("z", "y", "j", "t"))
    sp = ("z", "y", "j")
    image = P(None, sp, "t", None)
    return jax.shard_map(
        functools.partial(per_device, (planes, blocks_local, cut, tp)),
        mesh=mesh,
        in_specs=(
            image, P(None, "t"), P("t"), P("t"),
            P(None, "t", None, None), P(None, "t", None), P(None, "t", None, None), P(None, "t", None),
            P("t"), P("t"), P(None, "t"), P("t"), P("t", None), P("t"), image,
        ),
        out_specs=(
            image, image, P(), P(),
            P(None, "t", sp, None), P(None, "t", sp), P(None, "t", sp, None), P(None, "t", sp),
            P(), P(), P(sp, "t"), P(), P("t", sp), P(), P(),
        ),
        check_vma=False,
    )
```

```python
import functools
import math

import jax
import jax.numpy as jnp
import numpy as np
from jax import lax
from jax.experimental import pallas as pl
from jax.experimental.pallas import tpu as pltpu
from jax.sharding import Mesh, PartitionSpec as P

BLOCK = 96
SHRINK = 0.01
NORM_EPS = 1e-05
BF = jnp.bfloat16
F32 = jnp.float32
FLOPS, BYTES = 1_000_000_000, 3_400_000
NN = (((1,), (0,)), ((), ()))
NT = (((1,), (1,)), ((), ()))
TN = (((0,), (0,)), ((), ()))


def dot(left, right, dims=NN):
    return lax.dot_general(left, right, dims, preferred_element_type=F32)


def gelu_pair(value):
    phi = 0.5 * lax.erf(value * (1.0 / math.sqrt(2.0))) + 0.5
    bell = jnp.exp2(value * value * (-0.5 / math.log(2.0)))
    return value * phi, phi + value * bell * (1.0 / math.sqrt(2.0 * math.pi))


def split(value):
    high = value.astype(BF)
    return high, (value - high.astype(F32)).astype(BF)


def np_split(table):
    high = table.astype(np.float32).astype(jnp.bfloat16)
    low = (table - high.astype(np.float64)).astype(np.float32).astype(jnp.bfloat16)
    return jnp.asarray(high), jnp.asarray(low)


def lon_tables(width, modes):
    angle = 2.0 * np.pi * (np.outer(np.arange(modes), np.arange(width)) % width) / width
    scale = 1.0 / math.sqrt(width)
    cos, sin = np.cos(angle) * scale, np.sin(angle) * scale
    doubled = np.where(np.arange(modes) == 0, 1.0, 2.0)[:, None]
    plain = np.concatenate([cos, -sin], 0)
    weighted = np.concatenate([cos * doubled, -sin * doubled], 0)
    return plain, weighted


def swapped(index):
    return index % 2 * 2 + index // 2


class Rows:
    def __init__(self, per, inner, quarters):
        self.per, self.inner, self.quarters = per, inner, quarters
        self.even = per % 2 == 0
        self.sizes = [per // 2, per - per // 2]

    def block(self, t, part):
        return t % 2 * 2 + (t // 2 + part) % 2 if self.even else swapped(t)

    def quarter(self, block, part):
        return (block + part) % 2 * 2 + block // 2 if self.even else swapped(block)

    def start(self, block, part):
        return (block + part) % 2 * self.sizes[0] if self.even else part * self.sizes[0]

    def order(self):
        held = []
        for t in range(self.quarters):
            for r in range(self.inner):
                for part in range(2):
                    block = self.block(t, part)
                    held.append(((block * self.inner + r) * self.per + self.start(block, part), self.sizes[part]))
        return held


def in_order(array, order):
    return jnp.concatenate([array[at : at + n] for at, n in order], axis=0)


def out_of_order(array, order):
    at = 0
    for row, n in order:
        yield row, n, array[at : at + n]
        at += n


def lat_table(rows, order):
    angle = 2.0 * np.pi * (np.outer(np.arange(rows), np.arange(rows)) % rows) / rows
    scale = 1.0 / math.sqrt(rows)
    held = np.concatenate([np.arange(at, at + n) for at, n in order])
    cos, sin = np.cos(angle)[:, held] * scale, np.sin(angle)[:, held] * scale
    return np.block([[cos, sin], [-sin, cos]])


def fold_lanes(value):
    total = value[:, :128]
    for at in range(128, value.shape[1], 128):
        total = total + value[:, at : at + 128]
    return total


def collect(pieces, order):
    value = pieces[...].astype(F32)
    return in_order(value.reshape(value.shape[0] * value.shape[1], *value.shape[2:]), order)


def lat_product(lat, high, low=None):
    size = lat.shape[1]
    both = dot(lat, high)
    rest = both[size:] if low is None else both[size:] + dot(lat[:size], low)
    return both[:size] + rest


def plane_forward(parts, table, lat, lons, spectra):
    rows, modes = lat.shape[1] // 2, spectra.shape[1]
    feats = spectra.shape[0] // (2 * rows)
    table_hi, table_lo = table
    total = dot(parts[0], table_lo)
    if len(parts) > 1:
        total = total + dot(parts[1], table_hi)
    total = total + dot(parts[0], table_hi)
    for c in range(2):
        lons[c] = total[:, c * modes : (c + 1) * modes]
    for f in range(0, feats, 2):
        pair = []
        for g in (f, f + 1):
            pair.append(jnp.concatenate([lons[c, pl.ds(g, rows, stride=feats), :] for c in range(2)], axis=0))
        high, low = split(jnp.concatenate(pair, axis=1))
        out = lat_product(lat, high, low)
        for i, g in enumerate((f, f + 1)):
            spectra[pl.ds(g, 2 * rows, stride=feats), :] = out[:, i * modes : (i + 1) * modes]


def plane_inverse(table, lat, lons, spectra):
    rows, modes = lat.shape[1] // 2, spectra.shape[1]
    feats = spectra.shape[0] // (2 * rows)
    for f in range(0, feats, 2):
        pair = [spectra[pl.ds(g, 2 * rows, stride=feats), :] for g in (f, f + 1)]
        out = lat_product(lat, jnp.concatenate(pair, axis=1).astype(BF))
        for i, g in enumerate((f, f + 1)):
            for c in range(2):
                lons[c, pl.ds(g, rows, stride=feats), :] = out[c * rows : (c + 1) * rows, i * modes : (i + 1) * modes]
    table_hi, table_lo = table
    value = jnp.concatenate([lons[0], lons[1]], axis=1).astype(BF)
    return dot(value, table_hi) + dot(value, table_lo)


def spectrum_kernel(order, pieces, mean, rstd, scale, shift, hi, lo, lat, spec, lons, spectra):
    mixed = (collect(pieces, order) - mean[...]) * rstd[...] * scale[...] + shift[...]
    rows, feats, width = mixed.shape
    parts = split(mixed.reshape(rows * feats, width))
    plane_forward(parts, (hi[...], lo[...]), lat[...], lons, spectra)
    spec[...] = spectra[...].reshape(spec.shape).astype(BF)


def join_lines(parts):
    value = jnp.concatenate([part[...] for part in parts], axis=1)
    return value.reshape(value.shape[0] * value.shape[1], *value.shape[2:])


def spectrum_back_kernel(n, *refs):
    parts, (hi, lo, lat, freq, lons, spectra) = refs[:n], refs[n:]
    value = join_lines(parts)
    rows, feats, width = value.shape
    if feats % 16:
        value = value.astype(F32).reshape(rows * feats, width).astype(BF)
    else:
        value = value.reshape(rows * feats, width)
    plane_forward((value,), (hi[...], lo[...]), lat[...], lons, spectra)
    freq[...] = spectra[...].reshape(freq.shape).astype(BF)


def two_modes(ref, ky):
    return jnp.concatenate([jnp.concatenate([ref[0, k], ref[1, k]], axis=0) for k in (ky, ky + 1)], axis=1)


def put_modes(ref, ky, value):
    feats, modes = ref.shape[2], ref.shape[3]
    for i in range(2):
        for c in range(2):
            ref[c, ky + i] = value[c * feats : (c + 1) * feats, i * modes : (i + 1) * modes].astype(ref.dtype)


def filter_kernel(spec, w1, bias1, w2, bias2, kept, mid, slope, bend, share):
    @pl.when(pl.program_id(0) == 0)
    def _():
        share[...] = jnp.zeros_like(share)

    for ky in range(0, spec.shape[1], 2):
        act, deriv = gelu_pair(dot(w1[...], two_modes(spec, ky)) + bias1[...])
        act = act.astype(BF)
        put_modes(mid, ky, act)
        put_modes(slope, ky, deriv)
        second = dot(w2[...], act) + bias2[...]
        bent = jnp.tanh(second * (1.0 / SHRINK))
        square = bent * bent
        put_modes(bend, ky, square)
        put_modes(kept, ky, second - SHRINK * bent)
        share[...] += jnp.sum((1.0 - square).reshape(-1, 8, square.shape[1]), axis=0)


def filter_back_kernel(
    freq, spec, mid, slope, bend, w1, w2, sgrad, inner, outer, inner_bias, outer_bias
):
    @pl.when(pl.program_id(0) == 0)
    def _():
        for ref in (inner, outer, inner_bias, outer_bias):
            ref[...] = jnp.zeros_like(ref)

    for ky in range(0, spec.shape[1], 2):
        two = (two_modes(freq, ky).astype(F32) * two_modes(bend, ky).astype(F32)).astype(BF)
        outer[...] += dot(two_modes(mid, ky), two, NT)
        outer_bias[...] += fold_lanes(two.astype(F32))
        one = (dot(w2[...], two, TN) * two_modes(slope, ky).astype(F32)).astype(BF)
        inner[...] += dot(two_modes(spec, ky), one, NT)
        inner_bias[...] += fold_lanes(one.astype(F32))
        put_modes(sgrad, ky, dot(w1[...], one, TN))


def section_kernel(order, pieces, mean, rstd, scale, shift, kept, hi, lo, lat, *refs):
    outs, (lons, spectra) = refs[:-2], refs[-2:]
    spectra[...] = kept[...].astype(F32).reshape(spectra.shape)
    value = collect(pieces, order)
    mixed = (value - mean[...]) * rstd[...] * scale[...] + shift[...]
    spectral = plane_inverse((hi[...], lo[...]), lat[...], lons, spectra)
    section = (value + mixed + spectral.reshape(value.shape)).astype(BF)
    section = section.reshape(pieces.shape[0], pieces.shape[1], *value.shape[1:])
    at = 0
    for out in outs:
        out[...] = section[:, at : at + out.shape[1]]
        at += out.shape[1]


def last_kernel(order, n, pieces, *refs):
    sgrad, (mean, rstd, scale, freq, hi, lo, lat, out, sums, gain_sum, shift_sum, lons, spectra) = refs[:n], refs[n:]
    spectra[...] = freq[...].astype(F32).reshape(spectra.shape)
    normed = (collect(pieces, order) - mean[...]) * rstd[...]
    grad = join_lines(sgrad).astype(F32)
    mixed = grad + plane_inverse((hi[...], lo[...]), lat[...], lons, spectra).reshape(grad.shape)
    gain_sum[...] = fold_lanes(jnp.sum(mixed * normed, axis=0))
    shift_sum[...] = fold_lanes(jnp.sum(mixed, axis=0))
    scaled = mixed * scale[...]
    value = (grad + rstd[...] * scaled).astype(BF)
    for at, n, part in out_of_order(value, order):
        out[at : at + n] = part

    @pl.when(pl.program_id(0) == 0)
    def _():
        sums[...] = jnp.zeros_like(sums)

    for c, term in enumerate((scaled, scaled * normed)):
        term = jnp.sum(term, axis=1)
        for at, n, part in out_of_order(term, order):
            sums[at : at + n, c] += part


def column_norm(value):
    mean = jnp.mean(value, axis=0, keepdims=True)
    centered = value - mean
    var = jnp.mean(centered * centered, axis=0, keepdims=True)
    rstd = lax.rsqrt(var + NORM_EPS)
    return centered * rstd, rstd


def feed_kernel(
    n, quarter, chunk, place, *refs
):
    cots = refs[:n]
    section, we_t, wp, we, bias, gain, shift = refs[n : n + 7]
    normal, hidden, pre, cot, sgrad, gain_sum, shift_sum = refs[-7:]

    @pl.when(pl.program_id(0) == 0)
    def _():
        gain_sum[...] = jnp.zeros_like(gain_sum)
        shift_sum[...] = jnp.zeros_like(shift_sum)

    for k, piece in enumerate(cots):
        cot[pl.ds(place[k] * quarter, quarter), :] = piece[0]
    normed, rstd = column_norm(section[...].astype(F32).reshape(normal.shape))
    value = (normed * gain[...] + shift[...]).astype(BF)
    normal[...] = value
    wide = cot[...]

    def bend(start, before, grad):
        rows = slice(start, start + chunk)
        act, slope = gelu_pair(before + jnp.concatenate([bias[rows]] * (value.shape[1] // 128), axis=1))
        hidden[rows] = act.astype(BF)
        pre[rows] = (grad * slope).astype(BF)

    ready = None
    for start in range(0, hidden.shape[0], chunk):
        rows = slice(start, start + chunk)
        products = start, dot(we_t[rows], value), dot(wp[rows], wide)
        if ready:
            bend(*ready)
        ready = products
    bend(*ready)
    part = we.shape[2]
    total = sum(dot(we[t], pre[t * part : (t + 1) * part]) for t in range(we.shape[0]))
    gain_sum[...] += fold_lanes(total * normed)
    shift_sum[...] += fold_lanes(total)
    wide = wide.astype(F32)
    scaled = total * gain[...]
    one = jnp.mean(scaled, axis=0, keepdims=True)
    two = jnp.mean(scaled * normed, axis=0, keepdims=True)
    grad = wide + rstd * (scaled - one - normed * two)
    sgrad[...] = grad.reshape(sgrad.shape).astype(BF)


def result_kernel(quarter, parts, place, hidden, wp_t, bias, *refs):
    sections, outs, field = refs[: len(parts)], refs[len(parts) : -1], refs[-1]
    row = pl.program_id(0)
    value = dot(wp_t[...], hidden[...]) + jnp.concatenate([bias[...]] * (hidden.shape[1] // 128), axis=1)
    at = 0
    for i, (section, n) in enumerate(zip(sections, parts)):

        @pl.when((row >= at) & (row < at + n))
        def _(i=i, section=section, at=at):
            field[...] = value + section[:, row - at].astype(F32).reshape(value.shape)
            for k, out in enumerate(outs[i :: len(parts)]):
                out[...] = field[pl.ds(place[k] * quarter, quarter), :].astype(BF)

        at += n


def weight_kernel(order, normal, pre, cot, hidden, sent, kept, bias_sum, cot_sum):
    products = dot(normal[...], pre[...], NT), dot(cot[...], hidden[...], NT)
    bias_sum[...] = fold_lanes(pre[...].astype(F32))
    away = pl.program_id(0) < pl.num_programs(0) // 2

    @pl.when((pl.program_id(0) == 0) & (pl.program_id(1) == 0))
    def _():
        cot_sum[...] = fold_lanes(cot[...].astype(F32))

    @pl.when(away)
    def _():
        for kind in range(2):
            sent[0, kind] = products[kind].astype(BF)

    @pl.when(jnp.logical_not(away))
    def _():
        for kind in range(2):
            kept[0, kind] = products[kind]


def widen_kernel(parts, slot, starts, *refs):
    pieces, out = refs[:-1], refs[-1]
    width = out.shape[3]
    for i, piece in enumerate(pieces):
        k, part = divmod(i, len(parts))

        @pl.when(pl.program_id(0) == k)
        def _(piece=piece, part=part):
            for row in range(parts[part]):
                out[0, starts[part] + row] = piece[:, row * width : (row + 1) * width].astype(F32)


def finish_kernel(feats, grads, patches, mean, rstd, one, two, out):
    normed = (patches[0].astype(F32) - mean[0]) * rstd[0]
    out[0] = grads[0].astype(F32) - rstd[0] * (one[0] + normed * two[0]) * (1.0 / feats)


def whole(shape):
    return pl.BlockSpec(shape, lambda *_: (0,) * len(shape), pipeline_mode=pl.Buffered(1))


def fixed(shape):
    return pl.BlockSpec(shape, lambda *_: (0,) * len(shape))


def run(name, kernel, grid, ins, specs, outs, out_specs, scratch, mib, micros, scalars=(), aliases=None):
    grid_spec = pltpu.PrefetchScalarGridSpec(
        num_scalar_prefetch=len(scalars), grid=grid, in_specs=specs, out_specs=out_specs, scratch_shapes=scratch
    )
    call = pl.pallas_call(
        kernel,
        grid_spec=grid_spec,
        out_shape=outs,
        compiler_params=pltpu.CompilerParams(vmem_limit_bytes=mib << 20),
        input_output_aliases=aliases or {},
        cost_estimate=pl.CostEstimate(flops=int(micros * FLOPS), bytes_accessed=int(micros * BYTES), transcendentals=0),
        name=name,
    )
    return call(*scalars, *ins)


def complex_weight(pair):
    real, imag = pair[0].T, pair[1].T
    return jnp.concatenate([jnp.concatenate([real, -imag], 1), jnp.concatenate([imag, real], 1)], 0)


def weight_pair(full):
    full = full.reshape(2, BLOCK, 2, BLOCK)
    return jnp.stack([full[0, :, 0] + full[1, :, 1], full[0, :, 1] - full[1, :, 0]])


def per_device(
    sizes, patches, present, first_gain, first_shift, filter_inner, inner_bias, filter_outer, outer_bias,
    second_gain, second_shift, expand_weight, expand_bias, project_weight, project_bias, cotangent,
):
    planes, blocks_local, cut, tp = sizes
    inner = blocks_local * cut
    ranks = inner * tp
    owners = planes * inner
    snaps, per, quarter, width = patches.shape
    feats = quarter * tp
    mine = quarter // inner
    modes = width // 2
    rows = per * ranks
    toks = per * width
    hidden_local = expand_bias.shape[0]
    hiddens = hidden_local * tp
    z, y, j, t = (lax.axis_index(name) for name in ("z", "y", "j", "t"))
    r = y * cut + j
    me = z * inner + r
    every, sp = ("z", "y", "j", "t"), ("z", "y", "j")
    shape = jax.ShapeDtypeStruct

    pieces = patches.reshape(snaps, per, inner, mine, width).swapaxes(1, 2).reshape(owners, per, mine, width)
    pieces = lax.all_to_all(pieces, sp, 0, 0, tiled=True)

    held = Rows(per, inner, tp)
    order, parts = held.order(), held.sizes

    def route(k, part, back):
        pairs = [
            ((zz * inner + rr) * tp + tt, (((swapped(tt) + k) % tp) * inner + rr) * tp + held.quarter(zz, part))
            for zz in range(planes)
            for rr in range(inner)
            for tt in range(tp)
        ]
        return [(b, a) for a, b in pairs] if back else pairs

    place = jnp.stack([swapped((z - k) % tp) for k in range(tp)]).astype(jnp.int32)
    slot = jnp.stack([(swapped(t) + k) % tp for k in range(tp)]).astype(jnp.int32)
    field = patches.astype(F32)
    mean = jnp.mean(field, 2)
    square = jnp.sum(jnp.square(field - mean[:, :, None]), 2)
    gathered = lax.all_gather(jnp.stack([mean, square]), "t")
    packed = lax.all_gather(jnp.concatenate([second_gain, second_shift, project_bias, expand_bias]), "t")
    small = [packed[:, i * quarter : (i + 1) * quarter].reshape(-1) for i in range(3)]
    bias_all = packed[:, 3 * quarter :].reshape(-1)
    mean = jnp.mean(gathered[:, 0], 0)
    square = jnp.sum(gathered[:, 1] + quarter * jnp.square(gathered[:, 0] - mean), 0)
    stats = jnp.stack([mean, lax.rsqrt(square / feats + NORM_EPS)], 2)
    def lanes(vector, width=width):
        return jnp.broadcast_to(vector[:, None], (vector.shape[0], width))

    we = lax.all_gather(expand_weight, "t")
    wp = lax.all_gather(project_weight, "t", tiled=True)
    we_t, wp_t = jnp.swapaxes(we, 1, 2).reshape(hiddens, feats), wp.T
    gain2, shift2, bias_lanes = lanes(small[0]), lanes(small[1]), lanes(bias_all, 128)
    sent_stats, we, wp, we_t, wp_t, gain2, shift2, bias_lanes = lax.optimization_barrier(
        (stats, we, wp, we_t, wp_t, gain2, shift2, bias_lanes)
    )
    plane_stats = []
    for k in range(owners):
        piece = lax.dynamic_index_in_dim(sent_stats, (me ^ k) // inner, 0, False)
        plane_stats.append(lax.ppermute(piece, sp, [(a, a ^ k) for a in range(owners)]) if k else piece)
    plane_stats = jnp.stack(plane_stats)
    bit = 1
    while bit < owners:
        turned = plane_stats.reshape(-1, 2, bit, per, 2, width)
        plane_stats = jnp.where((me // bit) % 2 == 1, turned[:, ::-1], turned).reshape(owners, per, 2, width)
        bit *= 2
    plane_stats = in_order(plane_stats.reshape(rows, 2, 1, width), order)
    mean_one, rstd_one = plane_stats[:, 0], plane_stats[:, 1]

    def own_features(vector):
        return lax.dynamic_slice_in_dim(vector, r * mine, mine)

    keep = own_features(lax.dynamic_index_in_dim(present, z, 0, False).astype(F32))
    scale1, shift1 = lanes(own_features(first_gain) * keep), lanes(own_features(first_shift) * keep)

    def own_block(array):
        return lax.dynamic_index_in_dim(array, y, 1, False)

    w1, w2 = complex_weight(own_block(filter_inner)), complex_weight(own_block(filter_outer))
    bias1 = lanes(own_block(inner_bias).reshape(-1), 2 * modes)
    bias2 = lanes(own_block(outer_bias).reshape(-1), 2 * modes)
    plain, weighted = lon_tables(width, modes)
    lat = lat_table(rows, order)
    plain_t, weighted_t, plain_n, weighted_n = (np_split(a) for a in (plain.T, weighted.T, plain, weighted))
    lat_f, lat_b = (jnp.concatenate(np_split(a)) for a in (lat, lat.T))

    cotangents = [
        [lax.dynamic_slice(cotangent, (slot[k], held.start(z, part), 0, 0), (1, n, quarter, width))[0] for k in range(tp)]
        for part, n in enumerate(parts)
    ]
    late, pieces = lax.optimization_barrier((cotangents, pieces))
    cots = [[lax.ppermute(piece, every, route(k, 0, False)) for k, piece in enumerate(late[0])]]

    some = 16 if mine % 16 == 0 else mine
    grid = (mine // some,)
    piece_spec = pl.BlockSpec((owners, per, some, width), lambda g, *_: (0, 0, g, 0))
    stat_spec, feat_spec = whole((rows, 1, width)), pl.BlockSpec((some, width), lambda g, *_: (g, 0))
    lon_f, lon_b = [whole((width, 2 * modes))] * 2, [whole((2 * modes, width))] * 2
    lat_specs = [whole((4 * rows, 2 * rows))]
    image_spec = pl.BlockSpec((rows, some, width), lambda g, *_: (0, g, 0))
    modes_spec = pl.BlockSpec((2, rows, some, modes), lambda g, *_: (0, 0, g, 0))
    scratch = [
        pltpu.VMEM((2, rows * some, modes), F32),
        pltpu.VMEM((2 * rows * some, modes), F32),
    ]
    mine_modes = (2, rows, mine, modes)
    spec = run(
        "spectrum", functools.partial(spectrum_kernel, order), grid,
        (pieces, mean_one, rstd_one, scale1, shift1, *plain_t, lat_f),
        [piece_spec, stat_spec, stat_spec, feat_spec, feat_spec, *lon_f, *lat_specs],
        shape(mine_modes, BF), modes_spec, scratch, 48, 22,
    )

    def to_blocks(array):
        return lax.all_to_all(array, "j", 1, 2, tiled=True) if cut > 1 else array

    def to_features(array):
        return lax.all_to_all(array, "j", 2, 1, tiled=True) if cut > 1 else array

    spec = to_blocks(spec)
    lats = rows // cut
    step = 8
    block_modes = (2, lats, BLOCK, modes)
    block_spec = pl.BlockSpec((2, step, BLOCK, modes), lambda g: (0, g, 0, 0))
    square_spec, lane_spec = whole((2 * BLOCK, 2 * BLOCK)), whole((2 * BLOCK, 2 * modes))
    kept, mid, slope, bend, share = run(
        "filter", filter_kernel, (lats // step,), (spec, w1, bias1, w2, bias2),
        [block_spec, square_spec, lane_spec, square_spec, lane_spec],
        (*[shape(block_modes, BF)] * 4, shape((8, 2 * modes), F32)),
        (block_spec, block_spec, block_spec, block_spec, fixed((8, 2 * modes))), [], 48, 17,
    )
    kept, late, cots[0] = lax.optimization_barrier((kept, late, cots[0]))
    part_specs = [pl.BlockSpec((ranks, n, some, width), lambda g, *_: (0, 0, g, 0)) for n in parts]
    sections = run(
        "section", functools.partial(section_kernel, order), grid,
        (pieces, mean_one, rstd_one, scale1, shift1, to_features(kept), *weighted_n, lat_b),
        [piece_spec, stat_spec, stat_spec, feat_spec, feat_spec, modes_spec, *lon_b, *lat_specs],
        [shape((ranks, n, mine, width), BF) for n in parts], part_specs, scratch, 56, 17,
    )

    def exchange(array):
        return lax.all_to_all(array, ("t", "y", "j"), 0, 0, tiled=True)

    outs = (
        shape((feats, toks), BF), shape((hiddens, toks), BF), shape((hiddens, toks), BF), shape((feats, toks), BF),
    )
    sum_shapes = [shape((feats, 128), F32)] * 2
    sgrads, sums, done, start = [], [], (), 0
    received = []
    for n, section in zip(parts, sections):
        section = exchange(section)
        if not received:
            section, late = lax.optimization_barrier((section, late))
            cots.append([lax.ppermute(piece, every, route(k, 1, False)) for k, piece in enumerate(late[1])])
        tok_spec = pl.BlockSpec((feats, width), lambda h, *_, start=start: (0, h + start))
        hid_spec = pl.BlockSpec((hiddens, width), lambda h, *_, start=start: (0, h + start))
        cot_specs = [pl.BlockSpec((1, quarter, width), lambda h, *_: (h, 0, 0))] * tp
        line_spec = pl.BlockSpec((ranks, 1, mine, width), lambda h, *_: (0, h, 0, 0))
        any_spec = pl.BlockSpec(memory_space=pl.ANY)
        *done, sgrad, s0, s1 = run(
            "feed", functools.partial(feed_kernel, tp, quarter, min(256, hidden_local)), (n,),
            (*cots[len(received)], section, we_t, wp, we, bias_lanes, gain2, shift2, *done),
            [*cot_specs, line_spec, whole((hiddens, feats)), whole((hiddens, feats)),
             whole((tp, feats, hidden_local)), whole((hiddens, 128)), whole((feats, width)), whole((feats, width)),
             *[any_spec] * len(done)],
            (*outs, shape((ranks, n, mine, width), BF), *sum_shapes),
            (tok_spec, hid_spec, hid_spec, tok_spec, line_spec, *[fixed((feats, 128))] * 2),
            [], 60, 43, (place,), {8 + tp + i: i for i in range(len(done))},
        )
        if start:
            sgrad, done, sgrads = lax.optimization_barrier((sgrad, done, sgrads))
            rows_out = run(
                "result", functools.partial(result_kernel, quarter, parts), (per,),
                (done[1], wp_t, lanes(small[2], 128), *received, section),
                [pl.BlockSpec((hiddens, width), lambda h, *_: (0, h)), whole((feats, hiddens)), whole((feats, 128)),
                 *[whole((ranks, m, mine, width)) for m in parts]],
                [shape((quarter, m * width), BF) for _ in range(tp) for m in parts],
                [pl.BlockSpec((quarter, width), lambda h, *_, at=at, m=m: (0, jnp.clip(h - at, 0, m - 1)))
                 for _ in range(tp) for at, m in zip((0, parts[0]), parts)],
                [pltpu.VMEM((feats, width), F32)], 48, 0.01, (place,),
            )
            rows_out, done = lax.optimization_barrier((rows_out, done))
            results = [None] * (2 * tp)

            def send_results(rounds):
                for k in rounds:
                    for part in range(2):
                        results[2 * k + part] = lax.ppermute(rows_out[2 * k + part], every, route(k, part, True))

            send_results((0, 1))
        sgrad = exchange(sgrad)
        if start:
            third, half = hidden_local // 3, tp // 2
            resident = whole((feats, toks))
            hid_rows = pl.BlockSpec((third, toks), lambda k, i, o: (o[k] * 3 + i, 0))
            normal, hidden, pre, cot = done
            sent, kept_products, bias_sum, cot_sum = run(
                "weights", weight_kernel, (tp, 3), (normal, pre, cot, hidden), [resident, hid_rows, resident, hid_rows],
                [shape((half, 2, feats, hidden_local), BF), shape((half, 2, feats, hidden_local), F32),
                 shape((hiddens, 128), F32), shape((feats, 128), F32)],
                [pl.BlockSpec((1, 2, feats, third), lambda k, i, o: (jnp.minimum(k, half - 1), 0, 0, jnp.where(k < half, i, 2))),
                 pl.BlockSpec((1, 2, feats, third), lambda k, i, o: (jnp.maximum(k - half, 0), 0, 0, jnp.where(k < half, 0, i))),
                 pl.BlockSpec((third, 128), lambda k, i, o: (o[k] * 3 + i, 0)), fixed((feats, 128))],
                [], 60, 0.01,
                (jnp.stack([t ^ k for k in (*range(1, tp, 2), *range(0, tp, 2))]).astype(jnp.int32),),
            )
            sgrad, sent, results, rows_out = lax.optimization_barrier((sgrad, sent, results, rows_out))
            came = lax.ppermute(sent, "t", [(a, a ^ 1) for a in range(tp)])
            send_results((2, 3))
        sgrads.append(sgrad)
        sums.append((s0, s1))
        received.append(section)
        start += n
    gain_sum, shift_sum = (a + b for a, b in zip(*sums))

    def trade(theirs, axes, bit, size):
        return lax.ppermute(theirs, axes, [(a, a ^ bit) for a in range(size)])

    def halves(array, bit):
        other = 1 - (me // bit) % 2
        return lax.dynamic_index_in_dim(array, 1 - other, 0, False), lax.dynamic_index_in_dim(array, other, 0, False)


    freq = run(
        "spectrum_back", functools.partial(spectrum_back_kernel, len(parts)), grid, (*sgrads, *weighted_t, lat_f),
        [*part_specs, *lon_f, *lat_specs], shape(mine_modes, BF), modes_spec, scratch, 48, 0.01,
    )
    freq, came = lax.optimization_barrier((freq, came))
    weights = (kept_products + came.astype(F32)).reshape(half, 2, owners // 2, 2, feats // owners, hidden_local)
    weights, theirs = halves(jnp.moveaxis(weights, 3, 0), 1)
    came = trade(theirs.astype(BF), sp, 1, owners)
    freq, inner_grad, outer_grad, inner_bias_grad, outer_bias_grad = run(
        "filter_back", filter_back_kernel, (lats // step,), (to_blocks(freq), spec, mid, slope, bend, w1, w2),
        [*[block_spec] * 5, square_spec, square_spec],
        (shape(block_modes, BF), *[shape((2 * BLOCK, 2 * BLOCK), F32)] * 2, *[shape((2 * BLOCK, 128), F32)] * 2),
        (block_spec, *[fixed((2 * BLOCK, 2 * BLOCK))] * 2, *[fixed((2 * BLOCK, 128))] * 2), [], 48, 0.01,
    )
    freq, results = lax.optimization_barrier((freq, results))
    grads, lines, first_gain_sum, first_shift_sum = run(
        "last", functools.partial(last_kernel, order, len(parts)), grid,
        (pieces, *sgrads, mean_one, rstd_one, scale1, to_features(freq), *plain_n, lat_b),
        [piece_spec, *part_specs, stat_spec, stat_spec, feat_spec, modes_spec, *lon_b, *lat_specs],
        (shape((rows, mine, width), BF), shape((rows, 2, width), F32), *[shape((mine, 128), F32)] * 2),
        (image_spec, fixed((rows, 2, width)), *[pl.BlockSpec((some, 128), lambda g, *_: (g, 0))] * 2),
        scratch, 56, 0.01,
    )
    def with_bias(full, bias):
        bias = jnp.sum(bias, 1).reshape(2, BLOCK)
        return jnp.concatenate([weight_pair(full), bias[:, :, None]], 2)

    filters = jnp.stack([with_bias(inner_grad, inner_bias_grad), with_bias(outer_grad, outer_bias_grad)])
    filters = jnp.moveaxis(filters, 2, 0).reshape(owners, -1)
    early = jnp.concatenate(
        [jnp.sum(gain_sum, 1), jnp.sum(shift_sum, 1), jnp.sum(cot_sum, 1), jnp.sum(bias_sum, 1), jnp.sum(share)[None]]
    )
    grads, lines, results, came = lax.optimization_barrier((grads, lines, results, came))
    weights = weights + came.astype(F32)
    weights = jnp.moveaxis(weights[0] + trade(weights[1].astype(BF), "t", 2, tp).astype(F32), 1, 0)
    bit = 2
    while bit < inner:
        weights = weights.reshape(-1, 2, *weights.shape[1:])
        weights, theirs = halves(weights.swapaxes(0, 1), bit)
        weights = weights + trade(theirs.astype(BF), sp, bit, owners).astype(F32)
        bit *= 2
    expand_sum, project_sum = sum(
        trade(lax.dynamic_index_in_dim(weights, z ^ k, 0, False).astype(BF), "z", k, planes).astype(F32)
        for k in range(1, planes)
    ) + lax.dynamic_index_in_dim(weights, z, 0, False)
    project_sum = project_sum.T
    line = per * width
    feature_sums = jnp.stack([jnp.sum(first_gain_sum, 1) * keep, jnp.sum(first_shift_sum, 1) * keep]).reshape(-1)
    tail = jnp.concatenate(
        [lines.reshape(owners, 2 * line), filters,
         jnp.broadcast_to(jnp.concatenate([feature_sums, early]), (owners, 2 * mine + early.shape[0]))], 1
    )
    tail = lax.all_to_all(tail, sp, 0, 0, tiled=True)
    tail, grads = lax.optimization_barrier((tail, grads))
    grads = lax.all_to_all(grads.reshape(owners, per, mine, width), sp, 0, 0, tiled=True)
    cuts = [2 * line, 2 * line + filters.shape[1], 2 * line + filters.shape[1] + 2 * mine]
    lines, filters, feature_sums, early = jnp.split(tail, cuts, axis=1)
    lines = jnp.sum(lines.reshape(planes, inner, -1), 1).reshape(-1)
    filters = jnp.sum(filters.reshape(planes, blocks_local, cut, BLOCK // owners, 2, 2, BLOCK + 1), (0, 2))
    filters = jnp.transpose(filters, (2, 3, 0, 1, 4))
    feature_sums = jnp.sum(feature_sums.reshape(planes, inner, 2, mine), 0).swapaxes(0, 1)
    spread = lax.dynamic_update_slice(
        jnp.zeros((2, tp, quarter), F32), feature_sums.reshape(2, 1, quarter), (0, t, 0)
    ).reshape(-1)
    tail = jnp.concatenate([lines, spread, jnp.sum(early, 0)])
    bit = 1
    while bit < tp:
        tail = tail + trade(tail, "t", bit, tp)
        bit *= 2
    cuts = [planes * 2 * line, planes * 2 * line + 2 * feats]
    lines, last, early = jnp.split(tail, cuts)
    fixes = lines.reshape(planes, per, 2, 1, width)
    last = last.reshape(2, feats)

    starts = jnp.stack([jnp.asarray(held.start(z, part), jnp.int32) for part in range(2)])
    result = run(
        "widen", functools.partial(widen_kernel, parts), (tp,), results,
        [whole((quarter, n * width)) for _ in range(tp) for n in parts], shape((snaps, per, quarter, width), F32),
        pl.BlockSpec((1, per, quarter, width), lambda i, s, _: (s[i], 0, 0, 0)), [], 32, 8, (slot, starts),
    )
    one_spec = pl.BlockSpec((1, per, 1, width), lambda i: (i // inner, 0, 0, 0))
    patch_spec = pl.BlockSpec((1, per, mine, width), lambda i: (i // inner, 0, i % inner, 0))
    patches_grad = run(
        "finish", functools.partial(finish_kernel, feats), (owners,),
        (grads, patches, stats[:, :, 0, None], stats[:, :, 1, None], fixes[:, :, 0], fixes[:, :, 1]),
        [pl.BlockSpec((1, per, mine, width), lambda i: (i, 0, 0, 0)), patch_spec, *[one_spec] * 4],
        shape((snaps, per, quarter, width), F32), patch_spec, [], 48, 11,
    )

    return (
        result, patches_grad, last[0], last[1], filters[0, ..., :BLOCK], filters[0, ..., BLOCK],
        filters[1, ..., :BLOCK], filters[1, ..., BLOCK],
        early[:feats], early[feats : 2 * feats], expand_sum, early[3 * feats : 3 * feats + hiddens],
        project_sum, early[2 * feats : 3 * feats], early[-1] / (snaps * rows * modes * feats * 2),
    )


def solution(mesh):
    tp = mesh.shape["tp"]
    planes = tp
    inner = mesh.shape["sp"] // planes
    blocks_local = 2
    cut = inner // blocks_local
    mesh = Mesh(mesh.devices.reshape(planes, blocks_local, cut, tp), ("z", "y", "j", "t"))
    sp = ("z", "y", "j")
    image = P(None, sp, "t", None)
    return jax.shard_map(
        functools.partial(per_device, (planes, blocks_local, cut, tp)),
        mesh=mesh,
        in_specs=(
            image, P(None, "t"), P("t"), P("t"),
            P(None, "t", None, None), P(None, "t", None), P(None, "t", None, None), P(None, "t", None),
            P("t"), P("t"), P(None, "t"), P("t"), P("t", None), P("t"), image,
        ),
        out_specs=(
            image, image, P(), P(),
            P(None, "t", sp, None), P(None, "t", sp), P(None, "t", sp, None), P(None, "t", sp),
            P(), P(), P(sp, "t"), P(), P("t", sp), P(), P(),
        ),
        check_vma=False,
    )
```

```python
import functools
import math

import jax
import jax.numpy as jnp
import numpy as np
from jax import lax
from jax.experimental import pallas as pl
from jax.experimental.pallas import tpu as pltpu
from jax.sharding import Mesh, PartitionSpec as P

BLOCK = 96
SHRINK = 0.01
NORM_EPS = 1e-05
BF = jnp.bfloat16
F32 = jnp.float32
FLOPS, BYTES = 1_000_000_000, 3_400_000
NN = (((1,), (0,)), ((), ()))
NT = (((1,), (1,)), ((), ()))
TN = (((0,), (0,)), ((), ()))


def dot(left, right, dims=NN):
    return lax.dot_general(left, right, dims, preferred_element_type=F32)


def gelu_pair(value):
    phi = 0.5 * lax.erf(value * (1.0 / math.sqrt(2.0))) + 0.5
    bell = jnp.exp2(value * value * (-0.5 / math.log(2.0)))
    return value * phi, phi + value * bell * (1.0 / math.sqrt(2.0 * math.pi))


def split(value):
    high = value.astype(BF)
    return high, (value - high.astype(F32)).astype(BF)


def np_split(table):
    high = table.astype(np.float32).astype(jnp.bfloat16)
    low = (table - high.astype(np.float64)).astype(np.float32).astype(jnp.bfloat16)
    return jnp.asarray(high), jnp.asarray(low)


def lon_tables(width, modes):
    angle = 2.0 * np.pi * (np.outer(np.arange(modes), np.arange(width)) % width) / width
    scale = 1.0 / math.sqrt(width)
    cos, sin = np.cos(angle) * scale, np.sin(angle) * scale
    doubled = np.where(np.arange(modes) == 0, 1.0, 2.0)[:, None]
    plain = np.concatenate([cos, -sin], 0)
    weighted = np.concatenate([cos * doubled, -sin * doubled], 0)
    return plain, weighted


def swapped(index):
    return index % 2 * 2 + index // 2


class Rows:
    def __init__(self, per, inner, quarters):
        self.per, self.inner, self.quarters = per, inner, quarters
        self.even = per % 2 == 0
        self.sizes = [per // 2, per - per // 2]

    def block(self, t, part):
        return t % 2 * 2 + (t // 2 + part) % 2 if self.even else swapped(t)

    def quarter(self, block, part):
        return (block + part) % 2 * 2 + block // 2 if self.even else swapped(block)

    def start(self, block, part):
        return (block + part) % 2 * self.sizes[0] if self.even else part * self.sizes[0]

    def order(self):
        held = []
        for t in range(self.quarters):
            for r in range(self.inner):
                for part in range(2):
                    block = self.block(t, part)
                    held.append(((block * self.inner + r) * self.per + self.start(block, part), self.sizes[part]))
        return held


def in_order(array, order):
    return jnp.concatenate([array[at : at + n] for at, n in order], axis=0)


def out_of_order(array, order):
    at = 0
    for row, n in order:
        yield row, n, array[at : at + n]
        at += n


def lat_table(rows, order):
    angle = 2.0 * np.pi * (np.outer(np.arange(rows), np.arange(rows)) % rows) / rows
    scale = 1.0 / math.sqrt(rows)
    held = np.concatenate([np.arange(at, at + n) for at, n in order])
    cos, sin = np.cos(angle)[:, held] * scale, np.sin(angle)[:, held] * scale
    return np.block([[cos, sin], [-sin, cos]])


def fold_lanes(value):
    total = value[:, :128]
    for at in range(128, value.shape[1], 128):
        total = total + value[:, at : at + 128]
    return total


def collect(pieces, order):
    value = pieces[...].astype(F32)
    return in_order(value.reshape(value.shape[0] * value.shape[1], *value.shape[2:]), order)


def lat_product(lat, high, low=None):
    size = lat.shape[1]
    both = dot(lat, high)
    rest = both[size:] if low is None else both[size:] + dot(lat[:size], low)
    return both[:size] + rest


def plane_forward(parts, table, lat, lons, spectra):
    rows, modes = lat.shape[1] // 2, spectra.shape[1]
    feats = spectra.shape[0] // (2 * rows)
    table_hi, table_lo = table
    total = dot(parts[0], table_lo)
    if len(parts) > 1:
        total = total + dot(parts[1], table_hi)
    total = total + dot(parts[0], table_hi)
    for c in range(2):
        lons[c] = total[:, c * modes : (c + 1) * modes]
    for f in range(0, feats, 2):
        pair = []
        for g in (f, f + 1):
            pair.append(jnp.concatenate([lons[c, pl.ds(g, rows, stride=feats), :] for c in range(2)], axis=0))
        high, low = split(jnp.concatenate(pair, axis=1))
        out = lat_product(lat, high, low)
        for i, g in enumerate((f, f + 1)):
            spectra[pl.ds(g, 2 * rows, stride=feats), :] = out[:, i * modes : (i + 1) * modes]


def plane_inverse(table, lat, lons, spectra):
    rows, modes = lat.shape[1] // 2, spectra.shape[1]
    feats = spectra.shape[0] // (2 * rows)
    for f in range(0, feats, 2):
        pair = [spectra[pl.ds(g, 2 * rows, stride=feats), :] for g in (f, f + 1)]
        out = lat_product(lat, jnp.concatenate(pair, axis=1).astype(BF))
        for i, g in enumerate((f, f + 1)):
            for c in range(2):
                lons[c, pl.ds(g, rows, stride=feats), :] = out[c * rows : (c + 1) * rows, i * modes : (i + 1) * modes]
    table_hi, table_lo = table
    value = jnp.concatenate([lons[0], lons[1]], axis=1).astype(BF)
    return dot(value, table_hi) + dot(value, table_lo)


def spectrum_kernel(order, pieces, mean, rstd, scale, shift, hi, lo, lat, spec, lons, spectra):
    mixed = (collect(pieces, order) - mean[...]) * rstd[...] * scale[...] + shift[...]
    rows, feats, width = mixed.shape
    parts = split(mixed.reshape(rows * feats, width))
    plane_forward(parts, (hi[...], lo[...]), lat[...], lons, spectra)
    spec[...] = spectra[...].reshape(spec.shape).astype(BF)


def join_lines(parts):
    value = jnp.concatenate([part[...] for part in parts], axis=1)
    return value.reshape(value.shape[0] * value.shape[1], *value.shape[2:])


def spectrum_back_kernel(n, *refs):
    parts, (hi, lo, lat, freq, lons, spectra) = refs[:n], refs[n:]
    value = join_lines(parts)
    rows, feats, width = value.shape
    if feats % 16:
        value = value.astype(F32).reshape(rows * feats, width).astype(BF)
    else:
        value = value.reshape(rows * feats, width)
    plane_forward((value,), (hi[...], lo[...]), lat[...], lons, spectra)
    freq[...] = spectra[...].reshape(freq.shape).astype(BF)


def two_modes(ref, ky):
    return jnp.concatenate([jnp.concatenate([ref[0, k], ref[1, k]], axis=0) for k in (ky, ky + 1)], axis=1)


def put_modes(ref, ky, value):
    feats, modes = ref.shape[2], ref.shape[3]
    for i in range(2):
        for c in range(2):
            ref[c, ky + i] = value[c * feats : (c + 1) * feats, i * modes : (i + 1) * modes].astype(ref.dtype)


def filter_kernel(spec, w1, bias1, w2, bias2, kept, mid, slope, bend, share):
    @pl.when(pl.program_id(0) == 0)
    def _():
        share[...] = jnp.zeros_like(share)

    for ky in range(0, spec.shape[1], 2):
        act, deriv = gelu_pair(dot(w1[...], two_modes(spec, ky)) + bias1[...])
        act = act.astype(BF)
        put_modes(mid, ky, act)
        put_modes(slope, ky, deriv)
        second = dot(w2[...], act) + bias2[...]
        bent = jnp.tanh(second * (1.0 / SHRINK))
        square = bent * bent
        put_modes(bend, ky, square)
        put_modes(kept, ky, second - SHRINK * bent)
        share[...] += jnp.sum((1.0 - square).reshape(-1, 8, square.shape[1]), axis=0)


def filter_back_kernel(
    freq, spec, mid, slope, bend, w1, w2, sgrad, inner, outer, inner_bias, outer_bias
):
    @pl.when(pl.program_id(0) == 0)
    def _():
        for ref in (inner, outer, inner_bias, outer_bias):
            ref[...] = jnp.zeros_like(ref)

    for ky in range(0, spec.shape[1], 2):
        two = (two_modes(freq, ky).astype(F32) * two_modes(bend, ky).astype(F32)).astype(BF)
        outer[...] += dot(two_modes(mid, ky), two, NT)
        outer_bias[...] += fold_lanes(two.astype(F32))
        one = (dot(w2[...], two, TN) * two_modes(slope, ky).astype(F32)).astype(BF)
        inner[...] += dot(two_modes(spec, ky), one, NT)
        inner_bias[...] += fold_lanes(one.astype(F32))
        put_modes(sgrad, ky, dot(w1[...], one, TN))


def section_kernel(order, pieces, mean, rstd, scale, shift, kept, hi, lo, lat, *refs):
    outs, (lons, spectra) = refs[:-2], refs[-2:]
    spectra[...] = kept[...].astype(F32).reshape(spectra.shape)
    value = collect(pieces, order)
    mixed = (value - mean[...]) * rstd[...] * scale[...] + shift[...]
    spectral = plane_inverse((hi[...], lo[...]), lat[...], lons, spectra)
    section = (value + mixed + spectral.reshape(value.shape)).astype(BF)
    section = section.reshape(pieces.shape[0], pieces.shape[1], *value.shape[1:])
    at = 0
    for out in outs:
        out[...] = section[:, at : at + out.shape[1]]
        at += out.shape[1]


def last_kernel(order, n, pieces, *refs):
    sgrad, (mean, rstd, scale, freq, hi, lo, lat, out, sums, gain_sum, shift_sum, lons, spectra) = refs[:n], refs[n:]
    spectra[...] = freq[...].astype(F32).reshape(spectra.shape)
    normed = (collect(pieces, order) - mean[...]) * rstd[...]
    grad = join_lines(sgrad).astype(F32)
    mixed = grad + plane_inverse((hi[...], lo[...]), lat[...], lons, spectra).reshape(grad.shape)
    gain_sum[...] = fold_lanes(jnp.sum(mixed * normed, axis=0))
    shift_sum[...] = fold_lanes(jnp.sum(mixed, axis=0))
    scaled = mixed * scale[...]
    value = (grad + rstd[...] * scaled).astype(BF)
    for at, n, part in out_of_order(value, order):
        out[at : at + n] = part

    @pl.when(pl.program_id(0) == 0)
    def _():
        sums[...] = jnp.zeros_like(sums)

    for c, term in enumerate((scaled, scaled * normed)):
        term = jnp.sum(term, axis=1)
        for at, n, part in out_of_order(term, order):
            sums[at : at + n, c] += part


def column_norm(value):
    mean = jnp.mean(value, axis=0, keepdims=True)
    centered = value - mean
    var = jnp.mean(centered * centered, axis=0, keepdims=True)
    rstd = lax.rsqrt(var + NORM_EPS)
    return centered * rstd, rstd


def feed_kernel(
    n, quarter, chunk, place, *refs
):
    cots = refs[:n]
    section, we_t, wp, we, bias, gain, shift = refs[n : n + 7]
    normal, hidden, pre, cot, sgrad, gain_sum, shift_sum = refs[-7:]

    @pl.when(pl.program_id(0) == 0)
    def _():
        gain_sum[...] = jnp.zeros_like(gain_sum)
        shift_sum[...] = jnp.zeros_like(shift_sum)

    for k, piece in enumerate(cots):
        cot[pl.ds(place[k] * quarter, quarter), :] = piece[0]
    normed, rstd = column_norm(section[...].astype(F32).reshape(normal.shape))
    value = (normed * gain[...] + shift[...]).astype(BF)
    normal[...] = value
    wide = cot[...]

    def bend(start, before, grad):
        rows = slice(start, start + chunk)
        act, slope = gelu_pair(before + jnp.concatenate([bias[rows]] * (value.shape[1] // 128), axis=1))
        hidden[rows] = act.astype(BF)
        pre[rows] = (grad * slope).astype(BF)

    ready = None
    for start in range(0, hidden.shape[0], chunk):
        rows = slice(start, start + chunk)
        products = start, dot(we_t[rows], value), dot(wp[rows], wide)
        if ready:
            bend(*ready)
        ready = products
    bend(*ready)
    part = we.shape[2]
    total = sum(dot(we[t], pre[t * part : (t + 1) * part]) for t in range(we.shape[0]))
    gain_sum[...] += fold_lanes(total * normed)
    shift_sum[...] += fold_lanes(total)
    wide = wide.astype(F32)
    scaled = total * gain[...]
    one = jnp.mean(scaled, axis=0, keepdims=True)
    two = jnp.mean(scaled * normed, axis=0, keepdims=True)
    grad = wide + rstd * (scaled - one - normed * two)
    sgrad[...] = grad.reshape(sgrad.shape).astype(BF)


def result_kernel(quarter, parts, place, hidden, wp_t, bias, *refs):
    sections, outs, field = refs[: len(parts)], refs[len(parts) : -1], refs[-1]
    row = pl.program_id(0)
    value = dot(wp_t[...], hidden[...]) + jnp.concatenate([bias[...]] * (hidden.shape[1] // 128), axis=1)
    at = 0
    for i, (section, n) in enumerate(zip(sections, parts)):

        @pl.when((row >= at) & (row < at + n))
        def _(i=i, section=section):
            field[...] = value + section[...].astype(F32).reshape(value.shape)
            for k, out in enumerate(outs[i :: len(parts)]):
                out[...] = field[pl.ds(place[k] * quarter, quarter), :].astype(BF)

        at += n


def weight_kernel(order, normal, pre, cot, hidden, sent, kept, bias_sum, cot_sum):
    products = dot(normal[...], pre[...], NT), dot(cot[...], hidden[...], NT)
    bias_sum[...] = fold_lanes(pre[...].astype(F32))
    away = pl.program_id(0) < pl.num_programs(0) // 2

    @pl.when((pl.program_id(0) == 0) & (pl.program_id(1) == 0))
    def _():
        cot_sum[...] = fold_lanes(cot[...].astype(F32))

    @pl.when(away)
    def _():
        for kind in range(2):
            sent[0, kind] = products[kind].astype(BF)

    @pl.when(jnp.logical_not(away))
    def _():
        for kind in range(2):
            kept[0, kind] = products[kind]


def add_kernel(side, kept, came, mine, theirs):
    blocks = mine.shape[2]
    value = [
        (kept[i, 0] + came[i, 0].astype(F32)).reshape(blocks, 2, -1, mine.shape[4]) for i in range(2)
    ]
    own, other = [[jnp.where(side[0] == bit, v[:, 1], v[:, 0]) for v in value] for bit in (1, 0)]
    even = side[1] == 0
    for i in range(2):
        mine[i, 0] = jnp.where(even, value[0][:, i], own[i])
        theirs[i, 0] = jnp.where(even, value[1][:, i], other[i]).astype(BF)


def widen_kernel(parts, slot, starts, *refs):
    pieces, out = refs[:-1], refs[-1]
    width = out.shape[3]
    for i, piece in enumerate(pieces):
        k, part = divmod(i, len(parts))

        @pl.when(pl.program_id(0) == k)
        def _(piece=piece, part=part):
            for row in range(parts[part]):
                out[0, starts[part] + row] = piece[:, row * width : (row + 1) * width].astype(F32)


def finish_kernel(feats, patches, mean, rstd, one, two, *refs):
    grads, out = refs[:-1], refs[-1]
    normed = (patches[0].astype(F32) - mean[0]) * rstd[0]
    fix = rstd[0] * (one[0] + normed * two[0]) * (1.0 / feats)
    at = 0
    for grad in grads:
        here = slice(at, at + grad.shape[2])
        out[0, :, here] = grad[0].astype(F32) - fix[:, here]
        at += grad.shape[2]


def whole(shape):
    return pl.BlockSpec(shape, lambda *_: (0,) * len(shape), pipeline_mode=pl.Buffered(1))


def fixed(shape):
    return pl.BlockSpec(shape, lambda *_: (0,) * len(shape))


def run(name, kernel, grid, ins, specs, outs, out_specs, scratch, mib, micros, scalars=(), aliases=None):
    grid_spec = pltpu.PrefetchScalarGridSpec(
        num_scalar_prefetch=len(scalars), grid=grid, in_specs=specs, out_specs=out_specs, scratch_shapes=scratch
    )
    call = pl.pallas_call(
        kernel,
        grid_spec=grid_spec,
        out_shape=outs,
        compiler_params=pltpu.CompilerParams(vmem_limit_bytes=max(mib, 62) << 20),
        input_output_aliases=aliases or {},
        cost_estimate=pl.CostEstimate(flops=int(micros * FLOPS), bytes_accessed=int(micros * BYTES), transcendentals=0),
        name=name,
    )
    return call(*scalars, *ins)


def complex_weight(pair):
    real, imag = pair[0].T, pair[1].T
    return jnp.concatenate([jnp.concatenate([real, -imag], 1), jnp.concatenate([imag, real], 1)], 0)


def weight_pair(full):
    full = full.reshape(2, BLOCK, 2, BLOCK)
    return jnp.stack([full[0, :, 0] + full[1, :, 1], full[0, :, 1] - full[1, :, 0]])


def per_device(
    sizes, patches, present, first_gain, first_shift, filter_inner, inner_bias, filter_outer, outer_bias,
    second_gain, second_shift, expand_weight, expand_bias, project_weight, project_bias, cotangent,
):
    planes, blocks_local, cut, tp = sizes
    inner = blocks_local * cut
    ranks = inner * tp
    owners = planes * inner
    snaps, per, quarter, width = patches.shape
    feats = quarter * tp
    mine = quarter // inner
    modes = width // 2
    rows = per * ranks
    toks = per * width
    hidden_local = expand_bias.shape[0]
    hiddens = hidden_local * tp
    z, y, j, t = (lax.axis_index(name) for name in ("z", "y", "j", "t"))
    r = y * cut + j
    me = z * inner + r
    every, sp = ("z", "y", "j", "t"), ("z", "y", "j")
    shape = jax.ShapeDtypeStruct

    pieces = patches.reshape(snaps, per, inner, mine, width).swapaxes(1, 2).reshape(owners, per, mine, width)
    pieces = lax.all_to_all(pieces, sp, 0, 0, tiled=True)

    held = Rows(per, inner, tp)
    order, parts = held.order(), held.sizes

    def route(k, part, back):
        pairs = [
            ((zz * inner + rr) * tp + tt, (((swapped(tt) + k) % tp) * inner + rr) * tp + held.quarter(zz, part))
            for zz in range(planes)
            for rr in range(inner)
            for tt in range(tp)
        ]
        return [(b, a) for a, b in pairs] if back else pairs

    place = jnp.stack([swapped((z - k) % tp) for k in range(tp)]).astype(jnp.int32)
    slot = jnp.stack([(swapped(t) + k) % tp for k in range(tp)]).astype(jnp.int32)
    field = patches.astype(F32)
    mean = jnp.mean(field, 2)
    square = jnp.sum(jnp.square(field - mean[:, :, None]), 2)
    gathered = lax.all_gather(jnp.stack([mean, square]), "t")
    packed = lax.all_gather(jnp.concatenate([second_gain, second_shift, project_bias, expand_bias]), "t")
    small = [packed[:, i * quarter : (i + 1) * quarter].reshape(-1) for i in range(3)]
    bias_all = packed[:, 3 * quarter :].reshape(-1)
    mean = jnp.mean(gathered[:, 0], 0)
    square = jnp.sum(gathered[:, 1] + quarter * jnp.square(gathered[:, 0] - mean), 0)
    stats = jnp.stack([mean, lax.rsqrt(square / feats + NORM_EPS)], 2)
    def lanes(vector, width=width):
        return jnp.broadcast_to(vector[:, None], (vector.shape[0], width))

    we = lax.all_gather(expand_weight, "t")
    wp = lax.all_gather(project_weight, "t", tiled=True)
    we_t, wp_t = jnp.swapaxes(we, 1, 2).reshape(hiddens, feats), wp.T
    gain2, shift2, bias_lanes = lanes(small[0]), lanes(small[1]), lanes(bias_all, 128)
    sent_stats, we, wp, we_t, wp_t, gain2, shift2, bias_lanes = lax.optimization_barrier(
        (stats, we, wp, we_t, wp_t, gain2, shift2, bias_lanes)
    )
    plane_stats = []
    for k in range(owners):
        piece = lax.dynamic_index_in_dim(sent_stats, (me ^ k) // inner, 0, False)
        plane_stats.append(lax.ppermute(piece, sp, [(a, a ^ k) for a in range(owners)]) if k else piece)
    bit = 1
    while bit < owners:
        turn = (me // bit) % 2 == 1
        plane_stats = [jnp.where(turn, plane_stats[k ^ bit], plane_stats[k]) for k in range(owners)]
        bit *= 2
    plane_stats = jnp.stack(plane_stats)
    plane_stats = in_order(plane_stats.reshape(rows, 2, 1, width), order)
    mean_one, rstd_one = plane_stats[:, 0], plane_stats[:, 1]

    def own_features(vector):
        return lax.dynamic_slice_in_dim(vector, r * mine, mine)

    keep = own_features(lax.dynamic_index_in_dim(present, z, 0, False).astype(F32))
    scale1, shift1 = lanes(own_features(first_gain) * keep), lanes(own_features(first_shift) * keep)

    def own_block(array):
        return lax.dynamic_index_in_dim(array, y, 1, False)

    w1, w2 = complex_weight(own_block(filter_inner)), complex_weight(own_block(filter_outer))
    bias1 = lanes(own_block(inner_bias).reshape(-1), 2 * modes)
    bias2 = lanes(own_block(outer_bias).reshape(-1), 2 * modes)
    plain, weighted = lon_tables(width, modes)
    lat = lat_table(rows, order)
    plain_t, weighted_t, plain_n, weighted_n = (np_split(a) for a in (plain.T, weighted.T, plain, weighted))
    lat_f, lat_b = (jnp.concatenate(np_split(a)) for a in (lat, lat.T))

    cotangents = [
        [lax.dynamic_slice(cotangent, (slot[k], held.start(z, part), 0, 0), (1, n, quarter, width))[0] for k in range(tp)]
        for part, n in enumerate(parts)
    ]
    late, pieces = lax.optimization_barrier((cotangents, pieces))
    cots = [[lax.ppermute(piece, every, route(k, 0, False)) for k, piece in enumerate(late[0])]]

    some = 16 if mine % 16 == 0 else mine
    grid = (mine // some,)
    piece_spec = pl.BlockSpec((owners, per, some, width), lambda g, *_: (0, 0, g, 0))
    stat_spec, feat_spec = whole((rows, 1, width)), pl.BlockSpec((some, width), lambda g, *_: (g, 0))
    lon_f, lon_b = [whole((width, 2 * modes))] * 2, [whole((2 * modes, width))] * 2
    lat_specs = [whole((4 * rows, 2 * rows))]
    image_spec = pl.BlockSpec((rows, some, width), lambda g, *_: (0, g, 0))
    modes_spec = pl.BlockSpec((2, rows, some, modes), lambda g, *_: (0, 0, g, 0))
    scratch = [
        pltpu.VMEM((2, rows * some, modes), F32),
        pltpu.VMEM((2 * rows * some, modes), F32),
    ]
    mine_modes = (2, rows, mine, modes)
    spec = run(
        "spectrum", functools.partial(spectrum_kernel, order), grid,
        (pieces, mean_one, rstd_one, scale1, shift1, *plain_t, lat_f),
        [piece_spec, stat_spec, stat_spec, feat_spec, feat_spec, *lon_f, *lat_specs],
        shape(mine_modes, BF), modes_spec, scratch, 48, 22,
    )

    def to_blocks(array):
        return lax.all_to_all(array, "j", 1, 2, tiled=True) if cut > 1 else array

    def to_features(array):
        return lax.all_to_all(array, "j", 2, 1, tiled=True) if cut > 1 else array

    spec = to_blocks(spec)
    lats = rows // cut
    step = 8
    block_modes = (2, lats, BLOCK, modes)
    block_spec = pl.BlockSpec((2, step, BLOCK, modes), lambda g: (0, g, 0, 0))
    square_spec, lane_spec = whole((2 * BLOCK, 2 * BLOCK)), whole((2 * BLOCK, 2 * modes))
    kept, mid, slope, bend, share = run(
        "filter", filter_kernel, (lats // step,), (spec, w1, bias1, w2, bias2),
        [block_spec, square_spec, lane_spec, square_spec, lane_spec],
        (*[shape(block_modes, BF)] * 4, shape((8, 2 * modes), F32)),
        (block_spec, block_spec, block_spec, block_spec, fixed((8, 2 * modes))), [], 48, 17,
    )
    kept, late, cots[0] = lax.optimization_barrier((kept, late, cots[0]))
    part_specs = [pl.BlockSpec((ranks, n, some, width), lambda g, *_: (0, 0, g, 0)) for n in parts]
    sections = run(
        "section", functools.partial(section_kernel, order), grid,
        (pieces, mean_one, rstd_one, scale1, shift1, to_features(kept), *weighted_n, lat_b),
        [piece_spec, stat_spec, stat_spec, feat_spec, feat_spec, modes_spec, *lon_b, *lat_specs],
        [shape((ranks, n, mine, width), BF) for n in parts], part_specs, scratch, 56, 17,
    )

    def exchange(array):
        return lax.all_to_all(array, ("t", "y", "j"), 0, 0, tiled=True)

    outs = (
        shape((feats, toks), BF), shape((hiddens, toks), BF), shape((hiddens, toks), BF), shape((feats, toks), BF),
    )
    sum_shapes = [shape((feats, 128), F32)] * 2
    sgrads, sums, done, start = [], [], (), 0
    received = []
    for n, section in zip(parts, sections):
        section = exchange(section)
        if not received:
            section, late = lax.optimization_barrier((section, late))
            cots.append([lax.ppermute(piece, every, route(k, 1, False)) for k, piece in enumerate(late[1])])
        tok_spec = pl.BlockSpec((feats, width), lambda h, *_, start=start: (0, h + start))
        hid_spec = pl.BlockSpec((hiddens, width), lambda h, *_, start=start: (0, h + start))
        cot_specs = [pl.BlockSpec((1, quarter, width), lambda h, *_: (h, 0, 0))] * tp
        line_spec = pl.BlockSpec((ranks, 1, mine, width), lambda h, *_: (0, h, 0, 0))
        any_spec = pl.BlockSpec(memory_space=pl.ANY)
        *done, sgrad, s0, s1 = run(
            "feed", functools.partial(feed_kernel, tp, quarter, min(256, hidden_local)), (n,),
            (*cots[len(received)], section, we_t, wp, we, bias_lanes, gain2, shift2, *done),
            [*cot_specs, line_spec, whole((hiddens, feats)), whole((hiddens, feats)),
             whole((tp, feats, hidden_local)), whole((hiddens, 128)), whole((feats, width)), whole((feats, width)),
             *[any_spec] * len(done)],
            (*outs, shape((ranks, n, mine, width), BF), *sum_shapes),
            (tok_spec, hid_spec, hid_spec, tok_spec, line_spec, *[fixed((feats, 128))] * 2),
            [], 60, 43, (place,), {8 + tp + i: i for i in range(len(done))},
        )
        if start:
            sgrad, done, sgrads = lax.optimization_barrier((sgrad, done, sgrads))
            rows_out = run(
                "result", functools.partial(result_kernel, quarter, parts), (per,),
                (done[1], wp_t, lanes(small[2], 128), *received, section),
                [pl.BlockSpec((hiddens, width), lambda h, *_: (0, h)), whole((feats, hiddens)), whole((feats, 128)),
                 *[pl.BlockSpec((ranks, 1, mine, width), lambda h, *_, at=at, m=m: (0, jnp.clip(h - at, 0, m - 1), 0, 0))
                   for at, m in zip((0, parts[0]), parts)]],
                [shape((quarter, m * width), BF) for _ in range(tp) for m in parts],
                [pl.BlockSpec((quarter, width), lambda h, *_, at=at, m=m: (0, jnp.clip(h - at, 0, m - 1)))
                 for _ in range(tp) for at, m in zip((0, parts[0]), parts)],
                [pltpu.VMEM((feats, width), F32)], 48, 0.01, (place,),
            )
            rows_out, done = lax.optimization_barrier((rows_out, done))
            results = [None] * (2 * tp)

            def send_results(rounds):
                for k in rounds:
                    for part in range(2):
                        results[2 * k + part] = lax.ppermute(rows_out[2 * k + part], every, route(k, part, True))

            send_results((0, 1))
        sgrad = exchange(sgrad)
        if start:
            third, half = hidden_local // 3, tp // 2
            resident = whole((feats, toks))
            hid_rows = pl.BlockSpec((third, toks), lambda k, i, o: (o[k] * 3 + i, 0))
            normal, hidden, pre, cot = done
            sent, kept_products, bias_sum, cot_sum = run(
                "weights", weight_kernel, (tp, 3), (normal, pre, cot, hidden), [resident, hid_rows, resident, hid_rows],
                [shape((half, 2, feats, hidden_local), BF), shape((half, 2, feats, hidden_local), F32),
                 shape((hiddens, 128), F32), shape((feats, 128), F32)],
                [pl.BlockSpec((1, 2, feats, third), lambda k, i, o: (jnp.minimum(k, half - 1), 0, 0, jnp.where(k < half, i, 2))),
                 pl.BlockSpec((1, 2, feats, third), lambda k, i, o: (jnp.maximum(k - half, 0), 0, 0, jnp.where(k < half, 0, i))),
                 pl.BlockSpec((third, 128), lambda k, i, o: (o[k] * 3 + i, 0)), fixed((feats, 128))],
                [], 60, 0.01,
                (jnp.stack([t ^ k for k in (*range(1, tp, 2), *range(0, tp, 2))]).astype(jnp.int32),),
            )
            sgrad, sent, results, rows_out = lax.optimization_barrier((sgrad, sent, results, rows_out))
            came = lax.ppermute(sent, "t", [(a, a ^ 1) for a in range(tp)])
            send_results((2, 3))
        sgrads.append(sgrad)
        sums.append((s0, s1))
        received.append(section)
        start += n
    gain_sum, shift_sum = (a + b for a, b in zip(*sums))

    def trade(theirs, axes, bit, size):
        return lax.ppermute(theirs, axes, [(a, a ^ bit) for a in range(size)])

    def halves(array, bit):
        other = 1 - (me // bit) % 2
        return lax.dynamic_index_in_dim(array, 1 - other, 0, False), lax.dynamic_index_in_dim(array, other, 0, False)


    freq = run(
        "spectrum_back", functools.partial(spectrum_back_kernel, len(parts)), grid, (*sgrads, *weighted_t, lat_f),
        [*part_specs, *lon_f, *lat_specs], shape(mine_modes, BF), modes_spec, scratch, 48, 0.01,
    )
    freq, came = lax.optimization_barrier((freq, came))
    side = jnp.stack([me % 2, t % 2]).astype(jnp.int32)
    strip = feats // owners
    third = hidden_local // 3
    halves_shape = (2, 2, owners // 2, strip, hidden_local)
    halves_block = pl.BlockSpec((2, 1, owners // 2, strip, third), lambda kind, i, _: (0, kind, 0, 0, i))
    weights, theirs = run(
        "add", add_kernel, (2, 3), (kept_products, came),
        [pl.BlockSpec((half, 1, feats, third), lambda kind, i, _: (0, kind, 0, i))] * 2,
        (shape(halves_shape, F32), shape(halves_shape, BF)), (halves_block, halves_block), [], 48, 0.01, (side,),
    )
    steps_first = [
        (rank, rank ^ 2 if rank % 2 == 0 else rank ^ tp) for rank in range(planes * inner * tp)
    ]
    steps_second = [(rank, rank ^ tp if rank % 2 == 0 else rank ^ 2) for rank in range(planes * inner * tp)]
    own_half = jnp.where(t % 2 == 0, me % 2, 0)
    sent_half = jnp.where(t % 2 == 0, 1 - me % 2, 1)
    freq, theirs, weights = lax.optimization_barrier((freq, theirs, weights))
    came = lax.ppermute(theirs, every, steps_first)
    freq, inner_grad, outer_grad, inner_bias_grad, outer_bias_grad = run(
        "filter_back", filter_back_kernel, (lats // step,), (to_blocks(freq), spec, mid, slope, bend, w1, w2),
        [*[block_spec] * 5, square_spec, square_spec],
        (shape(block_modes, BF), *[shape((2 * BLOCK, 2 * BLOCK), F32)] * 2, *[shape((2 * BLOCK, 128), F32)] * 2),
        (block_spec, *[fixed((2 * BLOCK, 2 * BLOCK))] * 2, *[fixed((2 * BLOCK, 128))] * 2), [], 48, 0.01,
    )
    freq, results = lax.optimization_barrier((freq, results))
    cuts = [grid[0] // 2, grid[0] - grid[0] // 2] if grid[0] > 1 else [1]
    grads, lines, first_sums, at = [], [], [], 0
    freq = to_features(freq)
    for i, n in enumerate(cuts):
        here = lambda g, at=at: g + at
        image_part = pl.BlockSpec((rows, some, width), lambda g: (0, g, 0))
        grad, line_sums, *sums_here = run(
            "last", functools.partial(last_kernel, order, len(parts)), (n,),
            (pieces, *sgrads, mean_one, rstd_one, scale1, freq, *plain_n, lat_b),
            [pl.BlockSpec((owners, per, some, width), lambda g, here=here: (0, 0, here(g), 0)),
             *[pl.BlockSpec((ranks, m, some, width), lambda g, here=here: (0, 0, here(g), 0)) for m in parts],
             stat_spec, stat_spec, pl.BlockSpec((some, width), lambda g, here=here: (here(g), 0)),
             pl.BlockSpec((2, rows, some, modes), lambda g, here=here: (0, 0, here(g), 0)), *lon_b, *lat_specs],
            (shape((rows, n * some, width), BF), shape((rows, 2, width), F32), *[shape((n * some, 128), F32)] * 2),
            (image_part, fixed((rows, 2, width)), *[pl.BlockSpec((some, 128), lambda g: (g, 0))] * 2),
            scratch, 56, 0.01,
        )
        grads.append(grad.reshape(owners, per, n * some, width))
        lines.append(line_sums)
        first_sums.append(sums_here)
        at += n
        if i < len(cuts) - 1:
            freq, came, grads[i] = lax.optimization_barrier((freq, came, grads[i]))
            grads[i] = lax.all_to_all(grads[i], sp, 0, 0, tiled=True)
    weights = weights + came.astype(F32)
    came = lax.ppermute(lax.dynamic_index_in_dim(weights, sent_half, 0, False).astype(BF), every, steps_second)
    first_gain_sum, first_shift_sum = (jnp.concatenate(sums_here, 0) for sums_here in zip(*first_sums))
    lines = sum(lines)
    def with_bias(full, bias):
        bias = jnp.sum(bias, 1).reshape(2, BLOCK)
        return jnp.concatenate([weight_pair(full), bias[:, :, None]], 2)

    filters = jnp.stack([with_bias(inner_grad, inner_bias_grad), with_bias(outer_grad, outer_bias_grad)])
    filters = jnp.moveaxis(filters, 2, 0).reshape(owners, -1)
    early = jnp.concatenate(
        [jnp.sum(gain_sum, 1), jnp.sum(shift_sum, 1), jnp.sum(cot_sum, 1), jnp.sum(bias_sum, 1), jnp.sum(share)[None]]
    )
    grads, lines, results, came = lax.optimization_barrier((grads, lines, results, came))
    weights = jnp.moveaxis(lax.dynamic_index_in_dim(weights, own_half, 0, False) + came.astype(F32), 1, 0)
    bit = 2
    while bit < inner:
        weights = weights.reshape(-1, 2, *weights.shape[1:])
        weights, theirs = halves(weights.swapaxes(0, 1), bit)
        weights = weights + trade(theirs.astype(BF), sp, bit, owners).astype(F32)
        bit *= 2
    line = per * width
    feature_sums = jnp.stack([jnp.sum(first_gain_sum, 1) * keep, jnp.sum(first_shift_sum, 1) * keep]).reshape(-1)
    tail = jnp.concatenate(
        [lines.reshape(owners, 2 * line), filters,
         jnp.broadcast_to(jnp.concatenate([feature_sums, early]), (owners, 2 * mine + early.shape[0]))], 1
    )
    tail = lax.all_to_all(tail, sp, 0, 0, tiled=True)
    tail, grads, weights = lax.optimization_barrier((tail, grads, weights))
    def along_z(weights, bit):
        weights = weights.reshape(-1, 2, *weights.shape[1:])
        side = (z // bit) % 2
        theirs = lax.dynamic_index_in_dim(weights, 1 - side, 1, False).astype(BF)
        return lax.dynamic_index_in_dim(weights, side, 1, False) + trade(theirs, "z", bit, planes).astype(F32)

    weights = along_z(weights, 1)
    grads[-1] = lax.all_to_all(grads[-1], sp, 0, 0, tiled=True)
    grads[-1], weights = lax.optimization_barrier((grads[-1], weights))
    cuts = [2 * line, 2 * line + filters.shape[1], 2 * line + filters.shape[1] + 2 * mine]
    lines, filters, feature_sums, early = jnp.split(tail, cuts, axis=1)
    lines = jnp.sum(lines.reshape(planes, inner, -1), 1).reshape(-1)
    filters = jnp.sum(filters.reshape(planes, blocks_local, cut, BLOCK // owners, 2, 2, BLOCK + 1), (0, 2))
    filters = jnp.transpose(filters, (2, 3, 0, 1, 4))
    feature_sums = jnp.sum(feature_sums.reshape(planes, inner, 2, mine), 0).swapaxes(0, 1)
    spread = lax.dynamic_update_slice(
        jnp.zeros((2, tp, quarter), F32), feature_sums.reshape(2, 1, quarter), (0, t, 0)
    ).reshape(-1)
    tail = jnp.concatenate([lines, spread, jnp.sum(early, 0)])
    bit = 1
    while bit < tp:
        tail = tail + trade(tail, "t", bit, tp)
        bit *= 2
    cuts = [planes * 2 * line, planes * 2 * line + 2 * feats]
    lines, last, early = jnp.split(tail, cuts)
    fixes = lines.reshape(planes, per, 2, 1, width)
    last = last.reshape(2, feats)

    starts = jnp.stack([jnp.asarray(held.start(z, part), jnp.int32) for part in range(2)])
    result = run(
        "widen", functools.partial(widen_kernel, parts), (tp,), results,
        [whole((quarter, n * width)) for _ in range(tp) for n in parts], shape((snaps, per, quarter, width), F32),
        pl.BlockSpec((1, per, quarter, width), lambda i, s, _: (s[i], 0, 0, 0)), [], 32, 8, (slot, starts),
    )
    one_spec = pl.BlockSpec((1, per, 1, width), lambda i: (i // inner, 0, 0, 0))
    patch_spec = pl.BlockSpec((1, per, mine, width), lambda i: (i // inner, 0, i % inner, 0))
    patches_grad = run(
        "finish", functools.partial(finish_kernel, feats), (owners,),
        (patches, stats[:, :, 0, None], stats[:, :, 1, None], fixes[:, :, 0], fixes[:, :, 1], *grads),
        [patch_spec, *[one_spec] * 4,
         *[pl.BlockSpec((1, per, grad.shape[2], width), lambda i: (i, 0, 0, 0)) for grad in grads]],
        shape((snaps, per, quarter, width), F32), patch_spec, [], 48, 100,
    )

    expand_sum, project_sum = along_z(weights, 2)[0]
    project_sum = project_sum.T
    return (
        result, patches_grad, last[0], last[1], filters[0, ..., :BLOCK], filters[0, ..., BLOCK],
        filters[1, ..., :BLOCK], filters[1, ..., BLOCK],
        early[:feats], early[feats : 2 * feats], expand_sum, early[3 * feats : 3 * feats + hiddens],
        project_sum, early[2 * feats : 3 * feats], early[-1] / (snaps * rows * modes * feats * 2),
    )


def solution(mesh):
    tp = mesh.shape["tp"]
    planes = tp
    inner = mesh.shape["sp"] // planes
    blocks_local = 2
    cut = inner // blocks_local
    mesh = Mesh(mesh.devices.reshape(planes, blocks_local, cut, tp), ("z", "y", "j", "t"))
    sp = ("z", "y", "j")
    image = P(None, sp, "t", None)
    return jax.shard_map(
        functools.partial(per_device, (planes, blocks_local, cut, tp)),
        mesh=mesh,
        in_specs=(
            image, P(None, "t"), P("t"), P("t"),
            P(None, "t", None, None), P(None, "t", None), P(None, "t", None, None), P(None, "t", None),
            P("t"), P("t"), P(None, "t"), P("t"), P("t", None), P("t"), image,
        ),
        out_specs=(
            image, image, P(), P(),
            P(None, "t", sp, None), P(None, "t", sp), P(None, "t", sp, None), P(None, "t", sp),
            P(), P(), P(sp, "t"), P(), P("t", sp), P(), P(),
        ),
        check_vma=False,
    )
```

```python
import functools
import math

import jax
import jax.numpy as jnp
import numpy as np
from jax import lax
from jax.experimental import pallas as pl
from jax.experimental.pallas import tpu as pltpu
from jax.sharding import Mesh, PartitionSpec as P

BLOCK = 96
SHRINK = 0.01
NORM_EPS = 1e-05
BF = jnp.bfloat16
F32 = jnp.float32
FLOPS, BYTES = 1_000_000_000, 3_400_000
NN = (((1,), (0,)), ((), ()))
NT = (((1,), (1,)), ((), ()))
TN = (((0,), (0,)), ((), ()))


def dot(left, right, dims=NN):
    return lax.dot_general(left, right, dims, preferred_element_type=F32)


def gelu_pair(value):
    phi = 0.5 * lax.erf(value * (1.0 / math.sqrt(2.0))) + 0.5
    bell = jnp.exp2(value * value * (-0.5 / math.log(2.0)))
    return value * phi, phi + value * bell * (1.0 / math.sqrt(2.0 * math.pi))


def split(value):
    high = value.astype(BF)
    return high, (value - high.astype(F32)).astype(BF)


def np_split(table):
    high = table.astype(np.float32).astype(jnp.bfloat16)
    low = (table - high.astype(np.float64)).astype(np.float32).astype(jnp.bfloat16)
    return jnp.asarray(high), jnp.asarray(low)


def lon_tables(width, modes):
    angle = 2.0 * np.pi * (np.outer(np.arange(modes), np.arange(width)) % width) / width
    scale = 1.0 / math.sqrt(width)
    cos, sin = np.cos(angle) * scale, np.sin(angle) * scale
    doubled = np.where(np.arange(modes) == 0, 1.0, 2.0)[:, None]
    plain = np.concatenate([cos, -sin], 0)
    weighted = np.concatenate([cos * doubled, -sin * doubled], 0)
    return plain, weighted


def swapped(index):
    return index % 2 * 2 + index // 2


class Rows:
    def __init__(self, per, inner, quarters):
        self.per, self.inner, self.quarters = per, inner, quarters
        self.even = per % 2 == 0
        self.sizes = [per // 2, per - per // 2]

    def block(self, t, part):
        return t % 2 * 2 + (t // 2 + part) % 2 if self.even else swapped(t)

    def quarter(self, block, part):
        return (block + part) % 2 * 2 + block // 2 if self.even else swapped(block)

    def start(self, block, part):
        return (block + part) % 2 * self.sizes[0] if self.even else part * self.sizes[0]

    def order(self):
        held = []
        for t in range(self.quarters):
            for r in range(self.inner):
                for part in range(2):
                    block = self.block(t, part)
                    held.append(((block * self.inner + r) * self.per + self.start(block, part), self.sizes[part]))
        return held


def in_order(array, order):
    return jnp.concatenate([array[at : at + n] for at, n in order], axis=0)


def out_of_order(array, order):
    at = 0
    for row, n in order:
        yield row, n, array[at : at + n]
        at += n


def lat_table(rows, order):
    angle = 2.0 * np.pi * (np.outer(np.arange(rows), np.arange(rows)) % rows) / rows
    scale = 1.0 / math.sqrt(rows)
    held = np.concatenate([np.arange(at, at + n) for at, n in order])
    cos, sin = np.cos(angle)[:, held] * scale, np.sin(angle)[:, held] * scale
    return np.block([[cos, sin], [-sin, cos]])


def fold_lanes(value):
    total = value[:, :128]
    for at in range(128, value.shape[1], 128):
        total = total + value[:, at : at + 128]
    return total


def collect(pieces, order):
    value = pieces[...].astype(F32)
    return in_order(value.reshape(value.shape[0] * value.shape[1], *value.shape[2:]), order)


def lat_product(lat, high, low=None):
    size = lat.shape[1]
    both = dot(lat, high)
    rest = both[size:] if low is None else both[size:] + dot(lat[:size], low)
    return both[:size] + rest


def plane_forward(parts, table, lat, lons, spectra):
    rows, modes = lat.shape[1] // 2, spectra.shape[1]
    feats = spectra.shape[0] // (2 * rows)
    table_hi, table_lo = table
    total = dot(parts[0], table_lo)
    if len(parts) > 1:
        total = total + dot(parts[1], table_hi)
    total = total + dot(parts[0], table_hi)
    for c in range(2):
        lons[c] = total[:, c * modes : (c + 1) * modes]
    for f in range(0, feats, 2):
        pair = []
        for g in (f, f + 1):
            pair.append(jnp.concatenate([lons[c, pl.ds(g, rows, stride=feats), :] for c in range(2)], axis=0))
        high, low = split(jnp.concatenate(pair, axis=1))
        out = lat_product(lat, high, low)
        for i, g in enumerate((f, f + 1)):
            spectra[pl.ds(g, 2 * rows, stride=feats), :] = out[:, i * modes : (i + 1) * modes]


def plane_inverse(table, lat, lons, spectra):
    rows, modes = lat.shape[1] // 2, spectra.shape[1]
    feats = spectra.shape[0] // (2 * rows)
    for f in range(0, feats, 2):
        pair = [spectra[pl.ds(g, 2 * rows, stride=feats), :] for g in (f, f + 1)]
        out = lat_product(lat, jnp.concatenate(pair, axis=1).astype(BF))
        for i, g in enumerate((f, f + 1)):
            for c in range(2):
                lons[c, pl.ds(g, rows, stride=feats), :] = out[c * rows : (c + 1) * rows, i * modes : (i + 1) * modes]
    table_hi, table_lo = table
    value = jnp.concatenate([lons[0], lons[1]], axis=1).astype(BF)
    return dot(value, table_hi) + dot(value, table_lo)


def spectrum_kernel(order, pieces, mean, rstd, scale, shift, hi, lo, lat, spec, lons, spectra):
    mixed = (collect(pieces, order) - mean[...]) * rstd[...] * scale[...] + shift[...]
    rows, feats, width = mixed.shape
    parts = split(mixed.reshape(rows * feats, width))
    plane_forward(parts, (hi[...], lo[...]), lat[...], lons, spectra)
    spec[...] = spectra[...].reshape(spec.shape).astype(BF)


def join_lines(parts):
    value = jnp.concatenate([part[...] for part in parts], axis=1)
    return value.reshape(value.shape[0] * value.shape[1], *value.shape[2:])


def spectrum_back_kernel(n, *refs):
    parts, (hi, lo, lat, freq, lons, spectra) = refs[:n], refs[n:]
    value = join_lines(parts)
    rows, feats, width = value.shape
    if feats % 16:
        value = value.astype(F32).reshape(rows * feats, width).astype(BF)
    else:
        value = value.reshape(rows * feats, width)
    plane_forward((value,), (hi[...], lo[...]), lat[...], lons, spectra)
    freq[...] = spectra[...].reshape(freq.shape).astype(BF)


def two_modes(ref, ky):
    return jnp.concatenate([jnp.concatenate([ref[0, k], ref[1, k]], axis=0) for k in (ky, ky + 1)], axis=1)


def put_modes(ref, ky, value):
    feats, modes = ref.shape[2], ref.shape[3]
    for i in range(2):
        for c in range(2):
            ref[c, ky + i] = value[c * feats : (c + 1) * feats, i * modes : (i + 1) * modes].astype(ref.dtype)


def filter_kernel(spec, w1, bias1, w2, bias2, kept, mid, slope, bend, share):
    @pl.when(pl.program_id(0) == 0)
    def _():
        share[...] = jnp.zeros_like(share)

    for ky in range(0, spec.shape[1], 2):
        act, deriv = gelu_pair(dot(w1[...], two_modes(spec, ky)) + bias1[...])
        act = act.astype(BF)
        put_modes(mid, ky, act)
        put_modes(slope, ky, deriv)
        second = dot(w2[...], act) + bias2[...]
        bent = jnp.tanh(second * (1.0 / SHRINK))
        square = bent * bent
        put_modes(bend, ky, square)
        put_modes(kept, ky, second - SHRINK * bent)
        share[...] += jnp.sum((1.0 - square).reshape(-1, 8, square.shape[1]), axis=0)


def filter_back_kernel(
    freq, spec, mid, slope, bend, w1, w2, sgrad, inner, outer, inner_bias, outer_bias
):
    @pl.when(pl.program_id(0) == 0)
    def _():
        for ref in (inner, outer, inner_bias, outer_bias):
            ref[...] = jnp.zeros_like(ref)

    for ky in range(0, spec.shape[1], 2):
        two = (two_modes(freq, ky).astype(F32) * two_modes(bend, ky).astype(F32)).astype(BF)
        outer[...] += dot(two_modes(mid, ky), two, NT)
        outer_bias[...] += fold_lanes(two.astype(F32))
        one = (dot(w2[...], two, TN) * two_modes(slope, ky).astype(F32)).astype(BF)
        inner[...] += dot(two_modes(spec, ky), one, NT)
        inner_bias[...] += fold_lanes(one.astype(F32))
        put_modes(sgrad, ky, dot(w1[...], one, TN))


def section_kernel(order, pieces, mean, rstd, scale, shift, kept, hi, lo, lat, *refs):
    outs, (lons, spectra) = refs[:-2], refs[-2:]
    spectra[...] = kept[...].astype(F32).reshape(spectra.shape)
    value = collect(pieces, order)
    mixed = (value - mean[...]) * rstd[...] * scale[...] + shift[...]
    spectral = plane_inverse((hi[...], lo[...]), lat[...], lons, spectra)
    section = (value + mixed + spectral.reshape(value.shape)).astype(BF)
    section = section.reshape(pieces.shape[0], pieces.shape[1], *value.shape[1:])
    at = 0
    for out in outs:
        out[...] = section[:, at : at + out.shape[1]]
        at += out.shape[1]


def last_kernel(order, n, pieces, *refs):
    sgrad, (mean, rstd, scale, freq, hi, lo, lat, out, sums, gain_sum, shift_sum, lons, spectra) = refs[:n], refs[n:]
    spectra[...] = freq[...].astype(F32).reshape(spectra.shape)
    normed = (collect(pieces, order) - mean[...]) * rstd[...]
    grad = join_lines(sgrad).astype(F32)
    mixed = grad + plane_inverse((hi[...], lo[...]), lat[...], lons, spectra).reshape(grad.shape)
    gain_sum[...] = fold_lanes(jnp.sum(mixed * normed, axis=0))
    shift_sum[...] = fold_lanes(jnp.sum(mixed, axis=0))
    scaled = mixed * scale[...]
    value = (grad + rstd[...] * scaled).astype(BF)
    for at, n, part in out_of_order(value, order):
        out[at : at + n] = part

    @pl.when(pl.program_id(0) == 0)
    def _():
        sums[...] = jnp.zeros_like(sums)

    for c, term in enumerate((scaled, scaled * normed)):
        term = jnp.sum(term, axis=1)
        for at, n, part in out_of_order(term, order):
            sums[at : at + n, c] += part


def column_norm(value):
    mean = jnp.mean(value, axis=0, keepdims=True)
    centered = value - mean
    var = jnp.mean(centered * centered, axis=0, keepdims=True)
    rstd = lax.rsqrt(var + NORM_EPS)
    return centered * rstd, rstd


def feed_kernel(
    n, quarter, chunk, place, *refs
):
    cots = refs[:n]
    section, we_t, wp, we, bias, gain, shift = refs[n : n + 7]
    normal, hidden, pre, cot, sgrad, gain_sum, shift_sum = refs[-7:]

    @pl.when(pl.program_id(0) == 0)
    def _():
        gain_sum[...] = jnp.zeros_like(gain_sum)
        shift_sum[...] = jnp.zeros_like(shift_sum)

    for k, piece in enumerate(cots):
        cot[pl.ds(place[k] * quarter, quarter), :] = piece[0]
    normed, rstd = column_norm(section[...].astype(F32).reshape(normal.shape))
    value = (normed * gain[...] + shift[...]).astype(BF)
    normal[...] = value
    wide = cot[...]

    def bend(start, before, grad):
        rows = slice(start, start + chunk)
        act, slope = gelu_pair(before + jnp.concatenate([bias[rows]] * (value.shape[1] // 128), axis=1))
        hidden[rows] = act.astype(BF)
        pre[rows] = (grad * slope).astype(BF)

    ready = None
    for start in range(0, hidden.shape[0], chunk):
        rows = slice(start, start + chunk)
        products = start, dot(we_t[rows], value), dot(wp[rows], wide)
        if ready:
            bend(*ready)
        ready = products
    bend(*ready)
    part = we.shape[2]
    total = sum(dot(we[t], pre[t * part : (t + 1) * part]) for t in range(we.shape[0]))
    gain_sum[...] += fold_lanes(total * normed)
    shift_sum[...] += fold_lanes(total)
    wide = wide.astype(F32)
    scaled = total * gain[...]
    one = jnp.mean(scaled, axis=0, keepdims=True)
    two = jnp.mean(scaled * normed, axis=0, keepdims=True)
    grad = wide + rstd * (scaled - one - normed * two)
    sgrad[...] = grad.reshape(sgrad.shape).astype(BF)


def result_kernel(quarter, parts, place, hidden, wp_t, bias, *refs):
    sections, outs, field = refs[: len(parts)], refs[len(parts) : -1], refs[-1]
    row = pl.program_id(0)
    value = dot(wp_t[...], hidden[...]) + jnp.concatenate([bias[...]] * (hidden.shape[1] // 128), axis=1)
    at = 0
    for i, (section, n) in enumerate(zip(sections, parts)):

        @pl.when((row >= at) & (row < at + n))
        def _(i=i, section=section):
            field[...] = value + section[...].astype(F32).reshape(value.shape)
            for k, out in enumerate(outs[i :: len(parts)]):
                out[...] = field[pl.ds(place[k] * quarter, quarter), :].astype(BF)

        at += n


def weight_kernel(order, normal, pre, cot, hidden, sent, kept, bias_sum, cot_sum):
    products = dot(normal[...], pre[...], NT), dot(cot[...], hidden[...], NT)
    bias_sum[...] = fold_lanes(pre[...].astype(F32))
    away = pl.program_id(0) < pl.num_programs(0) // 2

    @pl.when((pl.program_id(0) == 0) & (pl.program_id(1) == 0))
    def _():
        cot_sum[...] = fold_lanes(cot[...].astype(F32))

    @pl.when(away)
    def _():
        for kind in range(2):
            sent[0, kind] = products[kind].astype(BF)

    @pl.when(jnp.logical_not(away))
    def _():
        for kind in range(2):
            kept[0, kind] = products[kind]


def add_kernel(side, kept, came, mine, theirs):
    for i in range(2):
        value = (kept[i, 0] + came[i, 0].astype(F32)).reshape(mine.shape[2], 2, -1, mine.shape[4])
        odd = side[0] == 1
        mine[i, 0] = jnp.where(odd, value[:, 1], value[:, 0])
        theirs[i, 0] = jnp.where(odd, value[:, 0], value[:, 1]).astype(BF)


def widen_kernel(parts, slot, starts, *refs):
    pieces, out = refs[:-1], refs[-1]
    width = out.shape[3]
    for i, piece in enumerate(pieces):
        k, part = divmod(i, len(parts))

        @pl.when(pl.program_id(0) == k)
        def _(piece=piece, part=part):
            for row in range(parts[part]):
                out[0, starts[part] + row] = piece[:, row * width : (row + 1) * width].astype(F32)


def finish_kernel(feats, patches, mean, rstd, one, two, *refs):
    grads, out = refs[:-1], refs[-1]
    normed = (patches[0].astype(F32) - mean[0]) * rstd[0]
    fix = rstd[0] * (one[0] + normed * two[0]) * (1.0 / feats)
    at = 0
    for grad in grads:
        here = slice(at, at + grad.shape[2])
        out[0, :, here] = grad[0].astype(F32) - fix[:, here]
        at += grad.shape[2]


def whole(shape):
    return pl.BlockSpec(shape, lambda *_: (0,) * len(shape), pipeline_mode=pl.Buffered(1))


def fixed(shape):
    return pl.BlockSpec(shape, lambda *_: (0,) * len(shape))


def run(name, kernel, grid, ins, specs, outs, out_specs, scratch, mib, micros, scalars=(), aliases=None):
    grid_spec = pltpu.PrefetchScalarGridSpec(
        num_scalar_prefetch=len(scalars), grid=grid, in_specs=specs, out_specs=out_specs, scratch_shapes=scratch
    )
    call = pl.pallas_call(
        kernel,
        grid_spec=grid_spec,
        out_shape=outs,
        compiler_params=pltpu.CompilerParams(vmem_limit_bytes=max(mib, 62) << 20),
        input_output_aliases=aliases or {},
        cost_estimate=pl.CostEstimate(flops=int(micros * FLOPS), bytes_accessed=int(micros * BYTES), transcendentals=0),
        name=name,
    )
    return call(*scalars, *ins)


def complex_weight(pair):
    real, imag = pair[0].T, pair[1].T
    return jnp.concatenate([jnp.concatenate([real, -imag], 1), jnp.concatenate([imag, real], 1)], 0)


def weight_pair(full):
    full = full.reshape(2, BLOCK, 2, BLOCK)
    return jnp.stack([full[0, :, 0] + full[1, :, 1], full[0, :, 1] - full[1, :, 0]])


def per_device(
    sizes, patches, present, first_gain, first_shift, filter_inner, inner_bias, filter_outer, outer_bias,
    second_gain, second_shift, expand_weight, expand_bias, project_weight, project_bias, cotangent,
):
    planes, blocks_local, cut, tp = sizes
    inner = blocks_local * cut
    ranks = inner * tp
    owners = planes * inner
    snaps, per, quarter, width = patches.shape
    feats = quarter * tp
    mine = quarter // inner
    modes = width // 2
    rows = per * ranks
    toks = per * width
    hidden_local = expand_bias.shape[0]
    hiddens = hidden_local * tp
    z, y, j, t = (lax.axis_index(name) for name in ("z", "y", "j", "t"))
    r = y * cut + j
    me = z * inner + r
    every, sp = ("z", "y", "j", "t"), ("z", "y", "j")
    shape = jax.ShapeDtypeStruct

    pieces = patches.reshape(snaps, per, inner, mine, width).swapaxes(1, 2).reshape(owners, per, mine, width)
    pieces = lax.all_to_all(pieces, sp, 0, 0, tiled=True)

    held = Rows(per, inner, tp)
    order, parts = held.order(), held.sizes

    def route(k, part, back):
        pairs = [
            ((zz * inner + rr) * tp + tt, (((swapped(tt) + k) % tp) * inner + rr) * tp + held.quarter(zz, part))
            for zz in range(planes)
            for rr in range(inner)
            for tt in range(tp)
        ]
        return [(b, a) for a, b in pairs] if back else pairs

    place = jnp.stack([swapped((z - k) % tp) for k in range(tp)]).astype(jnp.int32)
    slot = jnp.stack([(swapped(t) + k) % tp for k in range(tp)]).astype(jnp.int32)
    field = patches.astype(F32)
    mean = jnp.mean(field, 2)
    square = jnp.sum(jnp.square(field - mean[:, :, None]), 2)
    gathered = lax.all_gather(jnp.stack([mean, square]), "t")
    packed = lax.all_gather(jnp.concatenate([second_gain, second_shift, project_bias, expand_bias]), "t")
    small = [packed[:, i * quarter : (i + 1) * quarter].reshape(-1) for i in range(3)]
    bias_all = packed[:, 3 * quarter :].reshape(-1)
    mean = jnp.mean(gathered[:, 0], 0)
    square = jnp.sum(gathered[:, 1] + quarter * jnp.square(gathered[:, 0] - mean), 0)
    stats = jnp.stack([mean, lax.rsqrt(square / feats + NORM_EPS)], 2)
    def lanes(vector, width=width):
        return jnp.broadcast_to(vector[:, None], (vector.shape[0], width))

    we = lax.all_gather(expand_weight, "t")
    wp = lax.all_gather(project_weight, "t", tiled=True)
    we_t, wp_t = jnp.swapaxes(we, 1, 2).reshape(hiddens, feats), wp.T
    gain2, shift2, bias_lanes = lanes(small[0]), lanes(small[1]), lanes(bias_all, 128)
    sent_stats, we, wp, we_t, wp_t, gain2, shift2, bias_lanes = lax.optimization_barrier(
        (stats, we, wp, we_t, wp_t, gain2, shift2, bias_lanes)
    )
    plane_stats = []
    for k in range(owners):
        piece = lax.dynamic_index_in_dim(sent_stats, (me ^ k) // inner, 0, False)
        plane_stats.append(lax.ppermute(piece, sp, [(a, a ^ k) for a in range(owners)]) if k else piece)
    bit = 1
    while bit < owners:
        turn = (me // bit) % 2 == 1
        plane_stats = [jnp.where(turn, plane_stats[k ^ bit], plane_stats[k]) for k in range(owners)]
        bit *= 2
    plane_stats = jnp.stack(plane_stats)
    plane_stats = in_order(plane_stats.reshape(rows, 2, 1, width), order)
    mean_one, rstd_one = plane_stats[:, 0], plane_stats[:, 1]

    def own_features(vector):
        return lax.dynamic_slice_in_dim(vector, r * mine, mine)

    keep = own_features(lax.dynamic_index_in_dim(present, z, 0, False).astype(F32))
    scale1, shift1 = lanes(own_features(first_gain) * keep), lanes(own_features(first_shift) * keep)

    def own_block(array):
        return lax.dynamic_index_in_dim(array, y, 1, False)

    w1, w2 = complex_weight(own_block(filter_inner)), complex_weight(own_block(filter_outer))
    bias1 = lanes(own_block(inner_bias).reshape(-1), 2 * modes)
    bias2 = lanes(own_block(outer_bias).reshape(-1), 2 * modes)
    plain, weighted = lon_tables(width, modes)
    lat = lat_table(rows, order)
    plain_t, weighted_t, plain_n, weighted_n = (np_split(a) for a in (plain.T, weighted.T, plain, weighted))
    lat_f, lat_b = (jnp.concatenate(np_split(a)) for a in (lat, lat.T))

    cotangents = [
        [lax.dynamic_slice(cotangent, (slot[k], held.start(z, part), 0, 0), (1, n, quarter, width))[0] for k in range(tp)]
        for part, n in enumerate(parts)
    ]
    late, pieces = lax.optimization_barrier((cotangents, pieces))
    cots = [[lax.ppermute(piece, every, route(k, 0, False)) for k, piece in enumerate(late[0])]]

    some = 16 if mine % 16 == 0 else mine
    grid = (mine // some,)
    piece_spec = pl.BlockSpec((owners, per, some, width), lambda g, *_: (0, 0, g, 0))
    stat_spec, feat_spec = whole((rows, 1, width)), pl.BlockSpec((some, width), lambda g, *_: (g, 0))
    lon_f, lon_b = [whole((width, 2 * modes))] * 2, [whole((2 * modes, width))] * 2
    lat_specs = [whole((4 * rows, 2 * rows))]
    image_spec = pl.BlockSpec((rows, some, width), lambda g, *_: (0, g, 0))
    modes_spec = pl.BlockSpec((2, rows, some, modes), lambda g, *_: (0, 0, g, 0))
    scratch = [
        pltpu.VMEM((2, rows * some, modes), F32),
        pltpu.VMEM((2 * rows * some, modes), F32),
    ]
    mine_modes = (2, rows, mine, modes)
    spec = run(
        "spectrum", functools.partial(spectrum_kernel, order), grid,
        (pieces, mean_one, rstd_one, scale1, shift1, *plain_t, lat_f),
        [piece_spec, stat_spec, stat_spec, feat_spec, feat_spec, *lon_f, *lat_specs],
        shape(mine_modes, BF), modes_spec, scratch, 48, 22,
    )

    def to_blocks(array):
        return lax.all_to_all(array, "j", 1, 2, tiled=True) if cut > 1 else array

    def to_features(array):
        return lax.all_to_all(array, "j", 2, 1, tiled=True) if cut > 1 else array

    spec = to_blocks(spec)
    lats = rows // cut
    step = 8
    block_modes = (2, lats, BLOCK, modes)
    block_spec = pl.BlockSpec((2, step, BLOCK, modes), lambda g: (0, g, 0, 0))
    square_spec, lane_spec = whole((2 * BLOCK, 2 * BLOCK)), whole((2 * BLOCK, 2 * modes))
    kept, mid, slope, bend, share = run(
        "filter", filter_kernel, (lats // step,), (spec, w1, bias1, w2, bias2),
        [block_spec, square_spec, lane_spec, square_spec, lane_spec],
        (*[shape(block_modes, BF)] * 4, shape((8, 2 * modes), F32)),
        (block_spec, block_spec, block_spec, block_spec, fixed((8, 2 * modes))), [], 48, 17,
    )
    kept, late, cots[0] = lax.optimization_barrier((kept, late, cots[0]))
    part_specs = [pl.BlockSpec((ranks, n, some, width), lambda g, *_: (0, 0, g, 0)) for n in parts]
    sections = run(
        "section", functools.partial(section_kernel, order), grid,
        (pieces, mean_one, rstd_one, scale1, shift1, to_features(kept), *weighted_n, lat_b),
        [piece_spec, stat_spec, stat_spec, feat_spec, feat_spec, modes_spec, *lon_b, *lat_specs],
        [shape((ranks, n, mine, width), BF) for n in parts], part_specs, scratch, 56, 17,
    )

    def exchange(array):
        return lax.all_to_all(array, ("t", "y", "j"), 0, 0, tiled=True)

    outs = (
        shape((feats, toks), BF), shape((hiddens, toks), BF), shape((hiddens, toks), BF), shape((feats, toks), BF),
    )
    sum_shapes = [shape((feats, 128), F32)] * 2
    sgrads, sums, done, start = [], [], (), 0
    received = []
    for n, section in zip(parts, sections):
        section = exchange(section)
        if not received:
            section, late = lax.optimization_barrier((section, late))
            cots.append([lax.ppermute(piece, every, route(k, 1, False)) for k, piece in enumerate(late[1])])
        tok_spec = pl.BlockSpec((feats, width), lambda h, *_, start=start: (0, h + start))
        hid_spec = pl.BlockSpec((hiddens, width), lambda h, *_, start=start: (0, h + start))
        cot_specs = [pl.BlockSpec((1, quarter, width), lambda h, *_: (h, 0, 0))] * tp
        line_spec = pl.BlockSpec((ranks, 1, mine, width), lambda h, *_: (0, h, 0, 0))
        any_spec = pl.BlockSpec(memory_space=pl.ANY)
        *done, sgrad, s0, s1 = run(
            "feed", functools.partial(feed_kernel, tp, quarter, min(256, hidden_local)), (n,),
            (*cots[len(received)], section, we_t, wp, we, bias_lanes, gain2, shift2, *done),
            [*cot_specs, line_spec, whole((hiddens, feats)), whole((hiddens, feats)),
             whole((tp, feats, hidden_local)), whole((hiddens, 128)), whole((feats, width)), whole((feats, width)),
             *[any_spec] * len(done)],
            (*outs, shape((ranks, n, mine, width), BF), *sum_shapes),
            (tok_spec, hid_spec, hid_spec, tok_spec, line_spec, *[fixed((feats, 128))] * 2),
            [], 60, 43, (place,), {8 + tp + i: i for i in range(len(done))},
        )
        if start:
            sgrad, done, sgrads = lax.optimization_barrier((sgrad, done, sgrads))
            rows_out = run(
                "result", functools.partial(result_kernel, quarter, parts), (per,),
                (done[1], wp_t, lanes(small[2], 128), *received, section),
                [pl.BlockSpec((hiddens, width), lambda h, *_: (0, h)), whole((feats, hiddens)), whole((feats, 128)),
                 *[pl.BlockSpec((ranks, 1, mine, width), lambda h, *_, at=at, m=m: (0, jnp.clip(h - at, 0, m - 1), 0, 0))
                   for at, m in zip((0, parts[0]), parts)]],
                [shape((quarter, m * width), BF) for _ in range(tp) for m in parts],
                [pl.BlockSpec((quarter, width), lambda h, *_, at=at, m=m: (0, jnp.clip(h - at, 0, m - 1)))
                 for _ in range(tp) for at, m in zip((0, parts[0]), parts)],
                [pltpu.VMEM((feats, width), F32)], 48, 0.01, (place,),
            )
            rows_out, done = lax.optimization_barrier((rows_out, done))
            results = [None] * (2 * tp)

            def send_results(rounds):
                for k in rounds:
                    for part in range(2):
                        results[2 * k + part] = lax.ppermute(rows_out[2 * k + part], every, route(k, part, True))

            send_results((0, 1))
        sgrad = exchange(sgrad)
        if start:
            third, half = hidden_local // 3, tp // 2
            resident = whole((feats, toks))
            hid_rows = pl.BlockSpec((third, toks), lambda k, i, o: (o[k] * 3 + i, 0))
            normal, hidden, pre, cot = done
            sent, kept_products, bias_sum, cot_sum = run(
                "weights", weight_kernel, (tp, 3), (normal, pre, cot, hidden), [resident, hid_rows, resident, hid_rows],
                [shape((half, 2, feats, hidden_local), BF), shape((half, 2, feats, hidden_local), F32),
                 shape((hiddens, 128), F32), shape((feats, 128), F32)],
                [pl.BlockSpec((1, 2, feats, third), lambda k, i, o: (jnp.minimum(k, half - 1), 0, 0, jnp.where(k < half, i, 2))),
                 pl.BlockSpec((1, 2, feats, third), lambda k, i, o: (jnp.maximum(k - half, 0), 0, 0, jnp.where(k < half, 0, i))),
                 pl.BlockSpec((third, 128), lambda k, i, o: (o[k] * 3 + i, 0)), fixed((feats, 128))],
                [], 60, 0.01,
                (jnp.stack([t ^ k for k in (*range(1, tp, 2), *range(0, tp, 2))]).astype(jnp.int32),),
            )
            sgrad, sent, results, rows_out = lax.optimization_barrier((sgrad, sent, results, rows_out))
            came = lax.ppermute(sent, "t", [(a, a ^ 1) for a in range(tp)])
            send_results((2,))
        sgrads.append(sgrad)
        sums.append((s0, s1))
        received.append(section)
        start += n
    gain_sum, shift_sum = (a + b for a, b in zip(*sums))

    def trade(theirs, axes, bit, size):
        return lax.ppermute(theirs, axes, [(a, a ^ bit) for a in range(size)])

    def halves(array, bit):
        other = 1 - (me // bit) % 2
        return lax.dynamic_index_in_dim(array, 1 - other, 0, False), lax.dynamic_index_in_dim(array, other, 0, False)


    freq = run(
        "spectrum_back", functools.partial(spectrum_back_kernel, len(parts)), grid, (*sgrads, *weighted_t, lat_f),
        [*part_specs, *lon_f, *lat_specs], shape(mine_modes, BF), modes_spec, scratch, 48, 0.01,
    )
    freq, came = lax.optimization_barrier((freq, came))
    side = (me % 2).astype(jnp.int32).reshape(1)
    strip = feats // owners
    third = hidden_local // 3
    halves_shape = (2, 2, owners // 2, strip, hidden_local)
    halves_block = pl.BlockSpec((2, 1, owners // 2, strip, third), lambda kind, i, _: (0, kind, 0, 0, i))
    weights, theirs = run(
        "add", add_kernel, (2, 3), (kept_products, came),
        [pl.BlockSpec((half, 1, feats, third), lambda kind, i, _: (0, kind, 0, i))] * 2,
        (shape(halves_shape, F32), shape(halves_shape, BF)), (halves_block, halves_block), [], 48, 0.01, (side,),
    )
    freq, theirs, weights, results, rows_out = lax.optimization_barrier((freq, theirs, weights, results, rows_out))
    send_results((3,))
    came = trade(theirs, sp, 1, owners)
    freq, inner_grad, outer_grad, inner_bias_grad, outer_bias_grad = run(
        "filter_back", filter_back_kernel, (lats // step,), (to_blocks(freq), spec, mid, slope, bend, w1, w2),
        [*[block_spec] * 5, square_spec, square_spec],
        (shape(block_modes, BF), *[shape((2 * BLOCK, 2 * BLOCK), F32)] * 2, *[shape((2 * BLOCK, 128), F32)] * 2),
        (block_spec, *[fixed((2 * BLOCK, 2 * BLOCK))] * 2, *[fixed((2 * BLOCK, 128))] * 2), [], 48, 0.01,
    )
    freq, results = lax.optimization_barrier((freq, results))
    cuts = [grid[0] // 2, grid[0] - grid[0] // 2] if grid[0] > 1 else [1]
    grads, lines, first_sums, at = [], [], [], 0
    freq = to_features(freq)
    for i, n in enumerate(cuts):
        here = lambda g, at=at: g + at
        image_part = pl.BlockSpec((rows, some, width), lambda g: (0, g, 0))
        grad, line_sums, *sums_here = run(
            "last", functools.partial(last_kernel, order, len(parts)), (n,),
            (pieces, *sgrads, mean_one, rstd_one, scale1, freq, *plain_n, lat_b),
            [pl.BlockSpec((owners, per, some, width), lambda g, here=here: (0, 0, here(g), 0)),
             *[pl.BlockSpec((ranks, m, some, width), lambda g, here=here: (0, 0, here(g), 0)) for m in parts],
             stat_spec, stat_spec, pl.BlockSpec((some, width), lambda g, here=here: (here(g), 0)),
             pl.BlockSpec((2, rows, some, modes), lambda g, here=here: (0, 0, here(g), 0)), *lon_b, *lat_specs],
            (shape((rows, n * some, width), BF), shape((rows, 2, width), F32), *[shape((n * some, 128), F32)] * 2),
            (image_part, fixed((rows, 2, width)), *[pl.BlockSpec((some, 128), lambda g: (g, 0))] * 2),
            scratch, 56, 0.01,
        )
        grads.append(grad.reshape(owners, per, n * some, width))
        lines.append(line_sums)
        first_sums.append(sums_here)
        at += n
        if i < len(cuts) - 1:
            freq, came = lax.optimization_barrier((freq, came))
            grads[i] = lax.all_to_all(grads[i], sp, 0, 0, tiled=True)
    weights = weights + came.astype(F32)
    came = trade(weights[1].astype(BF), "t", 2, tp)
    first_gain_sum, first_shift_sum = (jnp.concatenate(sums_here, 0) for sums_here in zip(*first_sums))
    lines = sum(lines)
    def with_bias(full, bias):
        bias = jnp.sum(bias, 1).reshape(2, BLOCK)
        return jnp.concatenate([weight_pair(full), bias[:, :, None]], 2)

    filters = jnp.stack([with_bias(inner_grad, inner_bias_grad), with_bias(outer_grad, outer_bias_grad)])
    filters = jnp.moveaxis(filters, 2, 0).reshape(owners, -1)
    early = jnp.concatenate(
        [jnp.sum(gain_sum, 1), jnp.sum(shift_sum, 1), jnp.sum(cot_sum, 1), jnp.sum(bias_sum, 1), jnp.sum(share)[None]]
    )
    grads, lines, results, came = lax.optimization_barrier((grads, lines, results, came))
    weights = jnp.moveaxis(weights[0] + came.astype(F32), 1, 0)
    bit = 2
    while bit < inner:
        weights = weights.reshape(-1, 2, *weights.shape[1:])
        weights, theirs = halves(weights.swapaxes(0, 1), bit)
        weights = weights + trade(theirs.astype(BF), sp, bit, owners).astype(F32)
        bit *= 2
    line = per * width
    feature_sums = jnp.stack([jnp.sum(first_gain_sum, 1) * keep, jnp.sum(first_shift_sum, 1) * keep]).reshape(-1)
    tail = jnp.concatenate(
        [lines.reshape(owners, 2 * line), filters,
         jnp.broadcast_to(jnp.concatenate([feature_sums, early]), (owners, 2 * mine + early.shape[0]))], 1
    )
    tail = lax.all_to_all(tail, sp, 0, 0, tiled=True)
    tail, grads, weights = lax.optimization_barrier((tail, grads, weights))
    def along_z(weights, bit):
        weights = weights.reshape(-1, 2, *weights.shape[1:])
        side = (z // bit) % 2
        theirs = lax.dynamic_index_in_dim(weights, 1 - side, 1, False).astype(BF)
        return lax.dynamic_index_in_dim(weights, side, 1, False) + trade(theirs, "z", bit, planes).astype(F32)

    weights = along_z(weights, 1)
    grads[-1] = lax.all_to_all(grads[-1], sp, 0, 0, tiled=True)
    grads[-1], weights = lax.optimization_barrier((grads[-1], weights))
    cuts = [2 * line, 2 * line + filters.shape[1], 2 * line + filters.shape[1] + 2 * mine]
    lines, filters, feature_sums, early = jnp.split(tail, cuts, axis=1)
    lines = jnp.sum(lines.reshape(planes, inner, -1), 1).reshape(-1)
    filters = jnp.sum(filters.reshape(planes, blocks_local, cut, BLOCK // owners, 2, 2, BLOCK + 1), (0, 2))
    filters = jnp.transpose(filters, (2, 3, 0, 1, 4))
    feature_sums = jnp.sum(feature_sums.reshape(planes, inner, 2, mine), 0).swapaxes(0, 1)
    spread = lax.dynamic_update_slice(
        jnp.zeros((2, tp, quarter), F32), feature_sums.reshape(2, 1, quarter), (0, t, 0)
    ).reshape(-1)
    tail = jnp.concatenate([lines, spread, jnp.sum(early, 0)])
    bit = 1
    while bit < tp:
        tail = tail + trade(tail, "t", bit, tp)
        bit *= 2
    cuts = [planes * 2 * line, planes * 2 * line + 2 * feats]
    lines, last, early = jnp.split(tail, cuts)
    fixes = lines.reshape(planes, per, 2, 1, width)
    last = last.reshape(2, feats)

    starts = jnp.stack([jnp.asarray(held.start(z, part), jnp.int32) for part in range(2)])
    result = run(
        "widen", functools.partial(widen_kernel, parts), (tp,), results,
        [whole((quarter, n * width)) for _ in range(tp) for n in parts], shape((snaps, per, quarter, width), F32),
        pl.BlockSpec((1, per, quarter, width), lambda i, s, _: (s[i], 0, 0, 0)), [], 32, 8, (slot, starts),
    )
    one_spec = pl.BlockSpec((1, per, 1, width), lambda i: (i // inner, 0, 0, 0))
    patch_spec = pl.BlockSpec((1, per, mine, width), lambda i: (i // inner, 0, i % inner, 0))
    patches_grad = run(
        "finish", functools.partial(finish_kernel, feats), (owners,),
        (patches, stats[:, :, 0, None], stats[:, :, 1, None], fixes[:, :, 0], fixes[:, :, 1], *grads),
        [patch_spec, *[one_spec] * 4,
         *[pl.BlockSpec((1, per, grad.shape[2], width), lambda i: (i, 0, 0, 0)) for grad in grads]],
        shape((snaps, per, quarter, width), F32), patch_spec, [], 48, 100,
    )

    expand_sum, project_sum = along_z(weights, 2)[0]
    project_sum = project_sum.T
    return (
        result, patches_grad, last[0], last[1], filters[0, ..., :BLOCK], filters[0, ..., BLOCK],
        filters[1, ..., :BLOCK], filters[1, ..., BLOCK],
        early[:feats], early[feats : 2 * feats], expand_sum, early[3 * feats : 3 * feats + hiddens],
        project_sum, early[2 * feats : 3 * feats], early[-1] / (snaps * rows * modes * feats * 2),
    )


def solution(mesh):
    tp = mesh.shape["tp"]
    planes = tp
    inner = mesh.shape["sp"] // planes
    blocks_local = 2
    cut = inner // blocks_local
    mesh = Mesh(mesh.devices.reshape(planes, blocks_local, cut, tp), ("z", "y", "j", "t"))
    sp = ("z", "y", "j")
    image = P(None, sp, "t", None)
    return jax.shard_map(
        functools.partial(per_device, (planes, blocks_local, cut, tp)),
        mesh=mesh,
        in_specs=(
            image, P(None, "t"), P("t"), P("t"),
            P(None, "t", None, None), P(None, "t", None), P(None, "t", None, None), P(None, "t", None),
            P("t"), P("t"), P(None, "t"), P("t"), P("t", None), P("t"), image,
        ),
        out_specs=(
            image, image, P(), P(),
            P(None, "t", sp, None), P(None, "t", sp), P(None, "t", sp, None), P(None, "t", sp),
            P(), P(), P(sp, "t"), P(), P("t", sp), P(), P(),
        ),
        check_vma=False,
    )
```

```python
import functools
import math

import jax
import jax.numpy as jnp
import numpy as np
from jax import lax
from jax.experimental import pallas as pl
from jax.experimental.pallas import tpu as pltpu
from jax.sharding import Mesh, PartitionSpec as P

BLOCK = 96
SHRINK = 0.01
NORM_EPS = 1e-05
BF = jnp.bfloat16
F32 = jnp.float32
FLOPS, BYTES = 1_000_000_000, 3_400_000
NN = (((1,), (0,)), ((), ()))
NT = (((1,), (1,)), ((), ()))
TN = (((0,), (0,)), ((), ()))


def dot(left, right, dims=NN):
    return lax.dot_general(left, right, dims, preferred_element_type=F32)


def gelu_pair(value):
    phi = 0.5 * lax.erf(value * (1.0 / math.sqrt(2.0))) + 0.5
    bell = jnp.exp2(value * value * (-0.5 / math.log(2.0)))
    return value * phi, phi + value * bell * (1.0 / math.sqrt(2.0 * math.pi))


def split(value):
    high = value.astype(BF)
    return high, (value - high.astype(F32)).astype(BF)


def np_split(table):
    high = table.astype(np.float32).astype(jnp.bfloat16)
    low = (table - high.astype(np.float64)).astype(np.float32).astype(jnp.bfloat16)
    return jnp.asarray(high), jnp.asarray(low)


def lon_tables(width, modes):
    angle = 2.0 * np.pi * (np.outer(np.arange(modes), np.arange(width)) % width) / width
    scale = 1.0 / math.sqrt(width)
    cos, sin = np.cos(angle) * scale, np.sin(angle) * scale
    doubled = np.where(np.arange(modes) == 0, 1.0, 2.0)[:, None]
    plain = np.concatenate([cos, -sin], 0)
    weighted = np.concatenate([cos * doubled, -sin * doubled], 0)
    return plain, weighted


def swapped(index):
    return index % 2 * 2 + index // 2


class Rows:
    def __init__(self, per, inner, quarters):
        self.per, self.inner, self.quarters = per, inner, quarters
        self.even = per % 2 == 0
        self.sizes = [per // 2, per - per // 2]

    def block(self, t, part):
        return t % 2 * 2 + (t // 2 + part) % 2 if self.even else swapped(t)

    def quarter(self, block, part):
        return (block + part) % 2 * 2 + block // 2 if self.even else swapped(block)

    def start(self, block, part):
        return (block + part) % 2 * self.sizes[0] if self.even else part * self.sizes[0]

    def order(self):
        held = []
        for t in range(self.quarters):
            for r in range(self.inner):
                for part in range(2):
                    block = self.block(t, part)
                    held.append(((block * self.inner + r) * self.per + self.start(block, part), self.sizes[part]))
        return held


def in_order(array, order):
    return jnp.concatenate([array[at : at + n] for at, n in order], axis=0)


def out_of_order(array, order):
    at = 0
    for row, n in order:
        yield row, n, array[at : at + n]
        at += n


def lat_table(rows, order):
    angle = 2.0 * np.pi * (np.outer(np.arange(rows), np.arange(rows)) % rows) / rows
    scale = 1.0 / math.sqrt(rows)
    held = np.concatenate([np.arange(at, at + n) for at, n in order])
    cos, sin = np.cos(angle)[:, held] * scale, np.sin(angle)[:, held] * scale
    return np.block([[cos, sin], [-sin, cos]])


def fold_lanes(value):
    total = value[:, :128]
    for at in range(128, value.shape[1], 128):
        total = total + value[:, at : at + 128]
    return total


def collect(pieces, order):
    value = pieces[...].astype(F32)
    return in_order(value.reshape(value.shape[0] * value.shape[1], *value.shape[2:]), order)


def lat_product(lat, high, low=None):
    size = lat.shape[1]
    both = dot(lat, high)
    rest = both[size:] if low is None else both[size:] + dot(lat[:size], low)
    return both[:size] + rest


def plane_forward(parts, table, lat, lons, spectra):
    rows, modes = lat.shape[1] // 2, spectra.shape[1]
    feats = spectra.shape[0] // (2 * rows)
    table_hi, table_lo = table
    total = dot(parts[0], table_lo)
    if len(parts) > 1:
        total = total + dot(parts[1], table_hi)
    total = total + dot(parts[0], table_hi)
    for c in range(2):
        lons[c] = total[:, c * modes : (c + 1) * modes]
    for f in range(0, feats, 2):
        pair = []
        for g in (f, f + 1):
            pair.append(jnp.concatenate([lons[c, pl.ds(g, rows, stride=feats), :] for c in range(2)], axis=0))
        high, low = split(jnp.concatenate(pair, axis=1))
        out = lat_product(lat, high, low)
        for i, g in enumerate((f, f + 1)):
            spectra[pl.ds(g, 2 * rows, stride=feats), :] = out[:, i * modes : (i + 1) * modes]


def plane_inverse(table, lat, lons, spectra):
    rows, modes = lat.shape[1] // 2, spectra.shape[1]
    feats = spectra.shape[0] // (2 * rows)
    for f in range(0, feats, 2):
        pair = [spectra[pl.ds(g, 2 * rows, stride=feats), :] for g in (f, f + 1)]
        out = lat_product(lat, jnp.concatenate(pair, axis=1).astype(BF))
        for i, g in enumerate((f, f + 1)):
            for c in range(2):
                lons[c, pl.ds(g, rows, stride=feats), :] = out[c * rows : (c + 1) * rows, i * modes : (i + 1) * modes]
    table_hi, table_lo = table
    value = jnp.concatenate([lons[0], lons[1]], axis=1).astype(BF)
    return dot(value, table_hi) + dot(value, table_lo)


def spectrum_kernel(order, pieces, mean, rstd, scale, shift, hi, lo, lat, spec, lons, spectra):
    mixed = (collect(pieces, order) - mean[...]) * rstd[...] * scale[...] + shift[...]
    rows, feats, width = mixed.shape
    parts = split(mixed.reshape(rows * feats, width))
    plane_forward(parts, (hi[...], lo[...]), lat[...], lons, spectra)
    spec[...] = spectra[...].reshape(spec.shape).astype(BF)


def join_lines(parts):
    value = jnp.concatenate([part[...] for part in parts], axis=1)
    return value.reshape(value.shape[0] * value.shape[1], *value.shape[2:])


def spectrum_back_kernel(n, *refs):
    parts, (hi, lo, lat, freq, lons, spectra) = refs[:n], refs[n:]
    value = join_lines(parts)
    rows, feats, width = value.shape
    if feats % 16:
        value = value.astype(F32).reshape(rows * feats, width).astype(BF)
    else:
        value = value.reshape(rows * feats, width)
    plane_forward((value,), (hi[...], lo[...]), lat[...], lons, spectra)
    freq[...] = spectra[...].reshape(freq.shape).astype(BF)


def two_modes(ref, ky):
    return jnp.concatenate([jnp.concatenate([ref[0, k], ref[1, k]], axis=0) for k in (ky, ky + 1)], axis=1)


def put_modes(ref, ky, value):
    feats, modes = ref.shape[2], ref.shape[3]
    for i in range(2):
        for c in range(2):
            ref[c, ky + i] = value[c * feats : (c + 1) * feats, i * modes : (i + 1) * modes].astype(ref.dtype)


def filter_kernel(spec, w1, bias1, w2, bias2, kept, mid, slope, bend, share):
    @pl.when(pl.program_id(0) == 0)
    def _():
        share[...] = jnp.zeros_like(share)

    for ky in range(0, spec.shape[1], 2):
        act, deriv = gelu_pair(dot(w1[...], two_modes(spec, ky)) + bias1[...])
        act = act.astype(BF)
        put_modes(mid, ky, act)
        put_modes(slope, ky, deriv)
        second = dot(w2[...], act) + bias2[...]
        bent = jnp.tanh(second * (1.0 / SHRINK))
        square = bent * bent
        put_modes(bend, ky, square)
        put_modes(kept, ky, second - SHRINK * bent)
        share[...] += jnp.sum((1.0 - square).reshape(-1, 8, square.shape[1]), axis=0)


def filter_back_kernel(
    freq, spec, mid, slope, bend, w1, w2, sgrad, inner, outer, inner_bias, outer_bias
):
    @pl.when(pl.program_id(0) == 0)
    def _():
        for ref in (inner, outer, inner_bias, outer_bias):
            ref[...] = jnp.zeros_like(ref)

    for ky in range(0, spec.shape[1], 2):
        two = (two_modes(freq, ky).astype(F32) * two_modes(bend, ky).astype(F32)).astype(BF)
        outer[...] += dot(two_modes(mid, ky), two, NT)
        outer_bias[...] += fold_lanes(two.astype(F32))
        one = (dot(w2[...], two, TN) * two_modes(slope, ky).astype(F32)).astype(BF)
        inner[...] += dot(two_modes(spec, ky), one, NT)
        inner_bias[...] += fold_lanes(one.astype(F32))
        put_modes(sgrad, ky, dot(w1[...], one, TN))


def section_kernel(order, pieces, mean, rstd, scale, shift, kept, hi, lo, lat, *refs):
    outs, (lons, spectra) = refs[:-2], refs[-2:]
    spectra[...] = kept[...].astype(F32).reshape(spectra.shape)
    value = collect(pieces, order)
    mixed = (value - mean[...]) * rstd[...] * scale[...] + shift[...]
    spectral = plane_inverse((hi[...], lo[...]), lat[...], lons, spectra)
    section = (value + mixed + spectral.reshape(value.shape)).astype(BF)
    section = section.reshape(pieces.shape[0], pieces.shape[1], *value.shape[1:])
    at = 0
    for out in outs:
        out[...] = section[:, at : at + out.shape[1]]
        at += out.shape[1]


def last_kernel(order, n, pieces, *refs):
    sgrad, (mean, rstd, scale, freq, hi, lo, lat, out, sums, gain_sum, shift_sum, lons, spectra) = refs[:n], refs[n:]
    spectra[...] = freq[...].astype(F32).reshape(spectra.shape)
    normed = (collect(pieces, order) - mean[...]) * rstd[...]
    grad = join_lines(sgrad).astype(F32)
    mixed = grad + plane_inverse((hi[...], lo[...]), lat[...], lons, spectra).reshape(grad.shape)
    gain_sum[...] = fold_lanes(jnp.sum(mixed * normed, axis=0))
    shift_sum[...] = fold_lanes(jnp.sum(mixed, axis=0))
    scaled = mixed * scale[...]
    value = (grad + rstd[...] * scaled).astype(BF)
    for at, n, part in out_of_order(value, order):
        out[at : at + n] = part

    @pl.when(pl.program_id(0) == 0)
    def _():
        sums[...] = jnp.zeros_like(sums)

    for c, term in enumerate((scaled, scaled * normed)):
        term = jnp.sum(term, axis=1)
        for at, n, part in out_of_order(term, order):
            sums[at : at + n, c] += part


def column_norm(value):
    mean = jnp.mean(value, axis=0, keepdims=True)
    centered = value - mean
    var = jnp.mean(centered * centered, axis=0, keepdims=True)
    rstd = lax.rsqrt(var + NORM_EPS)
    return centered * rstd, rstd


def feed_kernel(
    n, quarter, chunk, place, *refs
):
    cots = refs[:n]
    section, we_t, wp, we, bias, gain, shift = refs[n : n + 7]
    normal, hidden, pre, cot, sgrad, gain_sum, shift_sum = refs[-7:]

    @pl.when(pl.program_id(0) == 0)
    def _():
        gain_sum[...] = jnp.zeros_like(gain_sum)
        shift_sum[...] = jnp.zeros_like(shift_sum)

    for k, piece in enumerate(cots):
        cot[pl.ds(place[k] * quarter, quarter), :] = piece[0]
    normed, rstd = column_norm(section[...].astype(F32).reshape(normal.shape))
    value = (normed * gain[...] + shift[...]).astype(BF)
    normal[...] = value
    wide = cot[...]

    def bend(start, before, grad):
        rows = slice(start, start + chunk)
        act, slope = gelu_pair(before + jnp.concatenate([bias[rows]] * (value.shape[1] // 128), axis=1))
        hidden[rows] = act.astype(BF)
        pre[rows] = (grad * slope).astype(BF)

    ready = None
    for start in range(0, hidden.shape[0], chunk):
        rows = slice(start, start + chunk)
        products = start, dot(we_t[rows], value), dot(wp[rows], wide)
        if ready:
            bend(*ready)
        ready = products
    bend(*ready)
    part = we.shape[2]
    total = sum(dot(we[t], pre[t * part : (t + 1) * part]) for t in range(we.shape[0]))
    gain_sum[...] += fold_lanes(total * normed)
    shift_sum[...] += fold_lanes(total)
    wide = wide.astype(F32)
    scaled = total * gain[...]
    one = jnp.mean(scaled, axis=0, keepdims=True)
    two = jnp.mean(scaled * normed, axis=0, keepdims=True)
    grad = wide + rstd * (scaled - one - normed * two)
    sgrad[...] = grad.reshape(sgrad.shape).astype(BF)


def result_kernel(quarter, parts, place, hidden, wp_t, bias, *refs):
    sections, outs, field = refs[: len(parts)], refs[len(parts) : -1], refs[-1]
    row = pl.program_id(0)
    value = dot(wp_t[...], hidden[...]) + jnp.concatenate([bias[...]] * (hidden.shape[1] // 128), axis=1)
    at = 0
    for i, (section, n) in enumerate(zip(sections, parts)):

        @pl.when((row >= at) & (row < at + n))
        def _(i=i, section=section):
            field[...] = value + section[...].astype(F32).reshape(value.shape)
            for k, out in enumerate(outs[i :: len(parts)]):
                out[...] = field[pl.ds(place[k] * quarter, quarter), :].astype(BF)

        at += n


def weight_kernel(order, normal, pre, cot, hidden, sent, kept, bias_sum, cot_sum):
    products = dot(normal[...], pre[...], NT), dot(cot[...], hidden[...], NT)
    bias_sum[...] = fold_lanes(pre[...].astype(F32))
    away = pl.program_id(0) < pl.num_programs(0) // 2

    @pl.when((pl.program_id(0) == 0) & (pl.program_id(1) == 0))
    def _():
        cot_sum[...] = fold_lanes(cot[...].astype(F32))

    @pl.when(away)
    def _():
        for kind in range(2):
            sent[0, kind] = products[kind].astype(BF)

    @pl.when(jnp.logical_not(away))
    def _():
        for kind in range(2):
            kept[0, kind] = products[kind]


def add_kernel(side, kept, came, mine, theirs):
    for i in range(2):
        value = (kept[i, 0] + came[i, 0].astype(F32)).reshape(mine.shape[2], 2, -1, mine.shape[4])
        odd = side[0] == 1
        mine[i, 0] = jnp.where(odd, value[:, 1], value[:, 0])
        theirs[i, 0] = jnp.where(odd, value[:, 0], value[:, 1]).astype(BF)


def widen_kernel(parts, slot, starts, *refs):
    pieces, out = refs[:-1], refs[-1]
    width = out.shape[3]
    for i, piece in enumerate(pieces):
        k, part = divmod(i, len(parts))

        @pl.when(pl.program_id(0) == k)
        def _(piece=piece, part=part):
            for row in range(parts[part]):
                out[0, starts[part] + row] = piece[:, row * width : (row + 1) * width].astype(F32)


def finish_kernel(feats, grad, patches, mean, rstd, one, two, *refs):
    out = refs[-1]
    normed = (patches[0].astype(F32) - mean[0]) * rstd[0]
    out[0] = grad[0].astype(F32) - rstd[0] * (one[0] + normed * two[0]) * (1.0 / feats)


def whole(shape):
    return pl.BlockSpec(shape, lambda *_: (0,) * len(shape), pipeline_mode=pl.Buffered(1))


def fixed(shape):
    return pl.BlockSpec(shape, lambda *_: (0,) * len(shape))


def run(name, kernel, grid, ins, specs, outs, out_specs, scratch, mib, micros, scalars=(), aliases=None):
    grid_spec = pltpu.PrefetchScalarGridSpec(
        num_scalar_prefetch=len(scalars), grid=grid, in_specs=specs, out_specs=out_specs, scratch_shapes=scratch
    )
    call = pl.pallas_call(
        kernel,
        grid_spec=grid_spec,
        out_shape=outs,
        compiler_params=pltpu.CompilerParams(vmem_limit_bytes=max(mib, 62) << 20),
        input_output_aliases=aliases or {},
        cost_estimate=pl.CostEstimate(flops=int(micros * FLOPS), bytes_accessed=int(micros * BYTES), transcendentals=0),
        name=name,
    )
    return call(*scalars, *ins)


def complex_weight(pair):
    real, imag = pair[0].T, pair[1].T
    return jnp.concatenate([jnp.concatenate([real, -imag], 1), jnp.concatenate([imag, real], 1)], 0)


def weight_pair(full):
    full = full.reshape(2, BLOCK, 2, BLOCK)
    return jnp.stack([full[0, :, 0] + full[1, :, 1], full[0, :, 1] - full[1, :, 0]])


def per_device(
    sizes, patches, present, first_gain, first_shift, filter_inner, inner_bias, filter_outer, outer_bias,
    second_gain, second_shift, expand_weight, expand_bias, project_weight, project_bias, cotangent,
):
    planes, blocks_local, cut, tp = sizes
    inner = blocks_local * cut
    ranks = inner * tp
    owners = planes * inner
    snaps, per, quarter, width = patches.shape
    feats = quarter * tp
    mine = quarter // inner
    modes = width // 2
    rows = per * ranks
    toks = per * width
    hidden_local = expand_bias.shape[0]
    hiddens = hidden_local * tp
    z, y, j, t = (lax.axis_index(name) for name in ("z", "y", "j", "t"))
    r = y * cut + j
    me = z * inner + r
    every, sp = ("z", "y", "j", "t"), ("z", "y", "j")
    shape = jax.ShapeDtypeStruct

    pieces = patches.reshape(snaps, per, inner, mine, width).swapaxes(1, 2).reshape(owners, per, mine, width)
    pieces, expand_weight, project_weight = lax.optimization_barrier((pieces, expand_weight, project_weight))
    pieces = lax.all_to_all(pieces, sp, 0, 0, tiled=True)

    held = Rows(per, inner, tp)
    order, parts = held.order(), held.sizes

    def route(k, part, back):
        pairs = [
            ((zz * inner + rr) * tp + tt, (((swapped(tt) + k) % tp) * inner + rr) * tp + held.quarter(zz, part))
            for zz in range(planes)
            for rr in range(inner)
            for tt in range(tp)
        ]
        return [(b, a) for a, b in pairs] if back else pairs

    place = jnp.stack([swapped((z - k) % tp) for k in range(tp)]).astype(jnp.int32)
    slot = jnp.stack([(swapped(t) + k) % tp for k in range(tp)]).astype(jnp.int32)
    field = patches.astype(F32)
    mean = jnp.mean(field, 2)
    square = jnp.sum(jnp.square(field - mean[:, :, None]), 2)
    gathered = lax.all_gather(jnp.stack([mean, square]), "t")
    packed = lax.all_gather(jnp.concatenate([second_gain, second_shift, project_bias, expand_bias]), "t")
    small = [packed[:, i * quarter : (i + 1) * quarter].reshape(-1) for i in range(3)]
    bias_all = packed[:, 3 * quarter :].reshape(-1)
    mean = jnp.mean(gathered[:, 0], 0)
    square = jnp.sum(gathered[:, 1] + quarter * jnp.square(gathered[:, 0] - mean), 0)
    stats = jnp.stack([mean, lax.rsqrt(square / feats + NORM_EPS)], 2)
    def lanes(vector, width=width):
        return jnp.broadcast_to(vector[:, None], (vector.shape[0], width))

    we = lax.all_gather(expand_weight, "t")
    wp = lax.all_gather(project_weight, "t", tiled=True)
    we_t, wp_t = jnp.swapaxes(we, 1, 2).reshape(hiddens, feats), wp.T
    gain2, shift2, bias_lanes = lanes(small[0]), lanes(small[1]), lanes(bias_all, 128)
    sent_stats, we, wp, we_t, wp_t, gain2, shift2, bias_lanes = lax.optimization_barrier(
        (stats, we, wp, we_t, wp_t, gain2, shift2, bias_lanes)
    )
    plane_stats = []
    for k in range(owners):
        piece = lax.dynamic_index_in_dim(sent_stats, (me ^ k) // inner, 0, False)
        plane_stats.append(lax.ppermute(piece, sp, [(a, a ^ k) for a in range(owners)]) if k else piece)
    bit = 1
    while bit < owners:
        turn = (me // bit) % 2 == 1
        plane_stats = [jnp.where(turn, plane_stats[k ^ bit], plane_stats[k]) for k in range(owners)]
        bit *= 2
    plane_stats = jnp.stack(plane_stats)
    plane_stats = in_order(plane_stats.reshape(rows, 2, 1, width), order)
    mean_one, rstd_one = plane_stats[:, 0], plane_stats[:, 1]

    def own_features(vector):
        return lax.dynamic_slice_in_dim(vector, r * mine, mine)

    keep = own_features(lax.dynamic_index_in_dim(present, z, 0, False).astype(F32))
    scale1, shift1 = lanes(own_features(first_gain) * keep), lanes(own_features(first_shift) * keep)

    def own_block(array):
        return lax.dynamic_index_in_dim(array, y, 1, False)

    w1, w2 = complex_weight(own_block(filter_inner)), complex_weight(own_block(filter_outer))
    bias1 = lanes(own_block(inner_bias).reshape(-1), 2 * modes)
    bias2 = lanes(own_block(outer_bias).reshape(-1), 2 * modes)
    plain, weighted = lon_tables(width, modes)
    lat = lat_table(rows, order)
    plain_t, weighted_t, plain_n, weighted_n = (np_split(a) for a in (plain.T, weighted.T, plain, weighted))
    lat_f, lat_b = (jnp.concatenate(np_split(a)) for a in (lat, lat.T))

    cotangents = [
        [lax.dynamic_slice(cotangent, (slot[k], held.start(z, part), 0, 0), (1, n, quarter, width))[0] for k in range(tp)]
        for part, n in enumerate(parts)
    ]
    late, pieces = lax.optimization_barrier((cotangents, pieces))
    cots = [[lax.ppermute(piece, every, route(k, 0, False)) for k, piece in enumerate(late[0])]]

    some = 16 if mine % 16 == 0 else mine
    grid = (mine // some,)
    piece_spec = pl.BlockSpec((owners, per, some, width), lambda g, *_: (0, 0, g, 0))
    stat_spec, feat_spec = whole((rows, 1, width)), pl.BlockSpec((some, width), lambda g, *_: (g, 0))
    lon_f, lon_b = [whole((width, 2 * modes))] * 2, [whole((2 * modes, width))] * 2
    lat_specs = [whole((4 * rows, 2 * rows))]
    image_spec = pl.BlockSpec((rows, some, width), lambda g, *_: (0, g, 0))
    modes_spec = pl.BlockSpec((2, rows, some, modes), lambda g, *_: (0, 0, g, 0))
    scratch = [
        pltpu.VMEM((2, rows * some, modes), F32),
        pltpu.VMEM((2 * rows * some, modes), F32),
    ]
    mine_modes = (2, rows, mine, modes)
    spec = run(
        "spectrum", functools.partial(spectrum_kernel, order), grid,
        (pieces, mean_one, rstd_one, scale1, shift1, *plain_t, lat_f),
        [piece_spec, stat_spec, stat_spec, feat_spec, feat_spec, *lon_f, *lat_specs],
        shape(mine_modes, BF), modes_spec, scratch, 48, 22,
    )

    def to_blocks(array):
        return lax.all_to_all(array, "j", 1, 2, tiled=True) if cut > 1 else array

    def to_features(array):
        return lax.all_to_all(array, "j", 2, 1, tiled=True) if cut > 1 else array

    spec = to_blocks(spec)
    lats = rows // cut
    step = 8
    block_modes = (2, lats, BLOCK, modes)
    block_spec = pl.BlockSpec((2, step, BLOCK, modes), lambda g: (0, g, 0, 0))
    square_spec, lane_spec = whole((2 * BLOCK, 2 * BLOCK)), whole((2 * BLOCK, 2 * modes))
    kept, mid, slope, bend, share = run(
        "filter", filter_kernel, (lats // step,), (spec, w1, bias1, w2, bias2),
        [block_spec, square_spec, lane_spec, square_spec, lane_spec],
        (*[shape(block_modes, BF)] * 4, shape((8, 2 * modes), F32)),
        (block_spec, block_spec, block_spec, block_spec, fixed((8, 2 * modes))), [], 48, 17,
    )
    part_specs = [pl.BlockSpec((ranks, n, some, width), lambda g, *_: (0, 0, g, 0)) for n in parts]
    sections = run(
        "section", functools.partial(section_kernel, order), grid,
        (pieces, mean_one, rstd_one, scale1, shift1, to_features(kept), *weighted_n, lat_b),
        [piece_spec, stat_spec, stat_spec, feat_spec, feat_spec, modes_spec, *lon_b, *lat_specs],
        [shape((ranks, n, mine, width), BF) for n in parts], part_specs, scratch, 56, 17,
    )

    sections, late, cots[0] = lax.optimization_barrier((sections, late, cots[0]))

    def exchange(array):
        return lax.all_to_all(array, ("t", "y", "j"), 0, 0, tiled=True)

    outs = (
        shape((feats, toks), BF), shape((hiddens, toks), BF), shape((hiddens, toks), BF), shape((feats, toks), BF),
    )
    sum_shapes = [shape((feats, 128), F32)] * 2
    sgrads, sums, done, start = [], [], (), 0
    received = []
    for n, section in zip(parts, sections):
        section = exchange(section)
        if not received:
            section, late = lax.optimization_barrier((section, late))
            cots.append([lax.ppermute(piece, every, route(k, 1, False)) for k, piece in enumerate(late[1])])
        tok_spec = pl.BlockSpec((feats, width), lambda h, *_, start=start: (0, h + start))
        hid_spec = pl.BlockSpec((hiddens, width), lambda h, *_, start=start: (0, h + start))
        cot_specs = [pl.BlockSpec((1, quarter, width), lambda h, *_: (h, 0, 0))] * tp
        line_spec = pl.BlockSpec((ranks, 1, mine, width), lambda h, *_: (0, h, 0, 0))
        any_spec = pl.BlockSpec(memory_space=pl.ANY)
        *done, sgrad, s0, s1 = run(
            "feed", functools.partial(feed_kernel, tp, quarter, min(256, hidden_local)), (n,),
            (*cots[len(received)], section, we_t, wp, we, bias_lanes, gain2, shift2, *done),
            [*cot_specs, line_spec, whole((hiddens, feats)), whole((hiddens, feats)),
             whole((tp, feats, hidden_local)), whole((hiddens, 128)), whole((feats, width)), whole((feats, width)),
             *[any_spec] * len(done)],
            (*outs, shape((ranks, n, mine, width), BF), *sum_shapes),
            (tok_spec, hid_spec, hid_spec, tok_spec, line_spec, *[fixed((feats, 128))] * 2),
            [], 60, 43, (place,), {8 + tp + i: i for i in range(len(done))},
        )
        if start:
            sgrad, done, sgrads = lax.optimization_barrier((sgrad, done, sgrads))
            rows_out = run(
                "result", functools.partial(result_kernel, quarter, parts), (per,),
                (done[1], wp_t, lanes(small[2], 128), *received, section),
                [pl.BlockSpec((hiddens, width), lambda h, *_: (0, h)), whole((feats, hiddens)), whole((feats, 128)),
                 *[pl.BlockSpec((ranks, 1, mine, width), lambda h, *_, at=at, m=m: (0, jnp.clip(h - at, 0, m - 1), 0, 0))
                   for at, m in zip((0, parts[0]), parts)]],
                [shape((quarter, m * width), BF) for _ in range(tp) for m in parts],
                [pl.BlockSpec((quarter, width), lambda h, *_, at=at, m=m: (0, jnp.clip(h - at, 0, m - 1)))
                 for _ in range(tp) for at, m in zip((0, parts[0]), parts)],
                [pltpu.VMEM((feats, width), F32)], 48, 0.01, (place,),
            )
            rows_out, done = lax.optimization_barrier((rows_out, done))
            results = [None] * (2 * tp)

            def send_results(rounds):
                for k in rounds:
                    for part in range(2):
                        results[2 * k + part] = lax.ppermute(rows_out[2 * k + part], every, route(k, part, True))

            send_results((0, 1))
        sgrad = exchange(sgrad)
        if start:
            third, half = hidden_local // 3, tp // 2
            resident = whole((feats, toks))
            hid_rows = pl.BlockSpec((third, toks), lambda k, i, o: (o[k] * 3 + i, 0))
            normal, hidden, pre, cot = done
            sent, kept_products, bias_sum, cot_sum = run(
                "weights", weight_kernel, (tp, 3), (normal, pre, cot, hidden), [resident, hid_rows, resident, hid_rows],
                [shape((half, 2, feats, hidden_local), BF), shape((half, 2, feats, hidden_local), F32),
                 shape((hiddens, 128), F32), shape((feats, 128), F32)],
                [pl.BlockSpec((1, 2, feats, third), lambda k, i, o: (jnp.minimum(k, half - 1), 0, 0, jnp.where(k < half, i, 2))),
                 pl.BlockSpec((1, 2, feats, third), lambda k, i, o: (jnp.maximum(k - half, 0), 0, 0, jnp.where(k < half, 0, i))),
                 pl.BlockSpec((third, 128), lambda k, i, o: (o[k] * 3 + i, 0)), fixed((feats, 128))],
                [], 60, 0.01,
                (jnp.stack([t ^ k for k in (*range(1, tp, 2), *range(0, tp, 2))]).astype(jnp.int32),),
            )
            sgrad, sent, results, rows_out = lax.optimization_barrier((sgrad, sent, results, rows_out))
            came = lax.ppermute(sent, "t", [(a, a ^ 1) for a in range(tp)])
            send_results((2,))
        sgrads.append(sgrad)
        sums.append((s0, s1))
        received.append(section)
        start += n
    gain_sum, shift_sum = (a + b for a, b in zip(*sums))

    def trade(theirs, axes, bit, size):
        return lax.ppermute(theirs, axes, [(a, a ^ bit) for a in range(size)])

    def halves(array, bit):
        other = 1 - (me // bit) % 2
        return lax.dynamic_index_in_dim(array, 1 - other, 0, False), lax.dynamic_index_in_dim(array, other, 0, False)


    freq = run(
        "spectrum_back", functools.partial(spectrum_back_kernel, len(parts)), grid, (*sgrads, *weighted_t, lat_f),
        [*part_specs, *lon_f, *lat_specs], shape(mine_modes, BF), modes_spec, scratch, 48, 0.01,
    )
    freq, came = lax.optimization_barrier((freq, came))
    side = (me % 2).astype(jnp.int32).reshape(1)
    strip = feats // owners
    third = hidden_local // 3
    halves_shape = (2, 2, owners // 2, strip, hidden_local)
    halves_block = pl.BlockSpec((2, 1, owners // 2, strip, third), lambda kind, i, _: (0, kind, 0, 0, i))
    weights, theirs = run(
        "add", add_kernel, (2, 3), (kept_products, came),
        [pl.BlockSpec((half, 1, feats, third), lambda kind, i, _: (0, kind, 0, i))] * 2,
        (shape(halves_shape, F32), shape(halves_shape, BF)), (halves_block, halves_block), [], 48, 0.01, (side,),
    )
    freq, theirs, weights, results, rows_out = lax.optimization_barrier((freq, theirs, weights, results, rows_out))
    send_results((3,))
    came = trade(theirs, sp, 1, owners)
    freq, inner_grad, outer_grad, inner_bias_grad, outer_bias_grad = run(
        "filter_back", filter_back_kernel, (lats // step,), (to_blocks(freq), spec, mid, slope, bend, w1, w2),
        [*[block_spec] * 5, square_spec, square_spec],
        (shape(block_modes, BF), *[shape((2 * BLOCK, 2 * BLOCK), F32)] * 2, *[shape((2 * BLOCK, 128), F32)] * 2),
        (block_spec, *[fixed((2 * BLOCK, 2 * BLOCK))] * 2, *[fixed((2 * BLOCK, 128))] * 2), [], 48, 0.01,
    )
    freq, results = lax.optimization_barrier((freq, results))
    cuts = [grid[0] // 2, grid[0] - grid[0] // 2] if grid[0] > 1 else [1]
    grads, lines, first_sums, at = [], [], [], 0
    freq = to_features(freq)
    for i, n in enumerate(cuts):
        here = lambda g, at=at: g + at
        image_part = pl.BlockSpec((rows, some, width), lambda g: (0, g, 0))
        grad, line_sums, *sums_here = run(
            "last", functools.partial(last_kernel, order, len(parts)), (n,),
            (pieces, *sgrads, mean_one, rstd_one, scale1, freq, *plain_n, lat_b),
            [pl.BlockSpec((owners, per, some, width), lambda g, here=here: (0, 0, here(g), 0)),
             *[pl.BlockSpec((ranks, m, some, width), lambda g, here=here: (0, 0, here(g), 0)) for m in parts],
             stat_spec, stat_spec, pl.BlockSpec((some, width), lambda g, here=here: (here(g), 0)),
             pl.BlockSpec((2, rows, some, modes), lambda g, here=here: (0, 0, here(g), 0)), *lon_b, *lat_specs],
            (shape((rows, n * some, width), BF), shape((rows, 2, width), F32), *[shape((n * some, 128), F32)] * 2),
            (image_part, fixed((rows, 2, width)), *[pl.BlockSpec((some, 128), lambda g: (g, 0))] * 2),
            scratch, 56, 0.01,
        )
        grads.append(grad.reshape(owners, per, n * some, width))
        lines.append(line_sums)
        first_sums.append(sums_here)
        at += n
        if i < len(cuts) - 1:
            freq, came = lax.optimization_barrier((freq, came))
            grads[i] = lax.all_to_all(grads[i], sp, 0, 0, tiled=True)
    weights = weights + came.astype(F32)
    came = trade(weights[1].astype(BF), "t", 2, tp)
    first_gain_sum, first_shift_sum = (jnp.concatenate(sums_here, 0) for sums_here in zip(*first_sums))
    lines = sum(lines)
    def with_bias(full, bias):
        bias = jnp.sum(bias, 1).reshape(2, BLOCK)
        return jnp.concatenate([weight_pair(full), bias[:, :, None]], 2)

    filters = jnp.stack([with_bias(inner_grad, inner_bias_grad), with_bias(outer_grad, outer_bias_grad)])
    filters = jnp.moveaxis(filters, 2, 0).reshape(owners, -1)
    early = jnp.concatenate(
        [jnp.sum(gain_sum, 1), jnp.sum(shift_sum, 1), jnp.sum(cot_sum, 1), jnp.sum(bias_sum, 1), jnp.sum(share)[None]]
    )
    grads, lines, results, came = lax.optimization_barrier((grads, lines, results, came))
    weights = jnp.moveaxis(weights[0] + came.astype(F32), 1, 0)
    bit = 2
    while bit < inner:
        weights = weights.reshape(-1, 2, *weights.shape[1:])
        weights, theirs = halves(weights.swapaxes(0, 1), bit)
        weights = weights + trade(theirs.astype(BF), sp, bit, owners).astype(F32)
        bit *= 2
    line = per * width
    feature_sums = jnp.stack([jnp.sum(first_gain_sum, 1) * keep, jnp.sum(first_shift_sum, 1) * keep]).reshape(-1)
    tail = jnp.concatenate(
        [lines.reshape(owners, 2 * line), filters,
         jnp.broadcast_to(jnp.concatenate([feature_sums, early]), (owners, 2 * mine + early.shape[0]))], 1
    )
    tail = lax.all_to_all(tail, sp, 0, 0, tiled=True)
    tail, grads, weights = lax.optimization_barrier((tail, grads, weights))
    def along_z(weights, bit):
        weights = weights.reshape(-1, 2, *weights.shape[1:])
        side = (z // bit) % 2
        theirs = lax.dynamic_index_in_dim(weights, 1 - side, 1, False).astype(BF)
        return lax.dynamic_index_in_dim(weights, side, 1, False) + trade(theirs, "z", bit, planes).astype(F32)

    weights = along_z(weights, 1)
    grads[-1] = lax.all_to_all(grads[-1], sp, 0, 0, tiled=True)
    grads[-1], weights = lax.optimization_barrier((grads[-1], weights))
    cuts = [2 * line, 2 * line + filters.shape[1], 2 * line + filters.shape[1] + 2 * mine]
    lines, filters, feature_sums, early = jnp.split(tail, cuts, axis=1)
    lines = jnp.sum(lines.reshape(planes, inner, -1), 1).reshape(-1)
    filters = jnp.sum(filters.reshape(planes, blocks_local, cut, BLOCK // owners, 2, 2, BLOCK + 1), (0, 2))
    filters = jnp.transpose(filters, (2, 3, 0, 1, 4))
    feature_sums = jnp.sum(feature_sums.reshape(planes, inner, 2, mine), 0).swapaxes(0, 1)
    spread = lax.dynamic_update_slice(
        jnp.zeros((2, tp, quarter), F32), feature_sums.reshape(2, 1, quarter), (0, t, 0)
    ).reshape(-1)
    tail = jnp.concatenate([lines, spread, jnp.sum(early, 0)])
    bit = 1
    while bit < tp:
        tail = tail + trade(tail, "t", bit, tp)
        bit *= 2
    cuts = [planes * 2 * line, planes * 2 * line + 2 * feats]
    lines, last, early = jnp.split(tail, cuts)
    fixes = lines.reshape(planes, per, 2, 1, width)
    last = last.reshape(2, feats)

    starts = jnp.stack([jnp.asarray(held.start(z, part), jnp.int32) for part in range(2)])
    result = run(
        "widen", functools.partial(widen_kernel, parts), (tp,), results,
        [whole((quarter, n * width)) for _ in range(tp) for n in parts], shape((snaps, per, quarter, width), F32),
        pl.BlockSpec((1, per, quarter, width), lambda i, s, _: (s[i], 0, 0, 0)), [], 32, 8, (slot, starts),
    )
    one_spec = pl.BlockSpec((1, per, 1, width), lambda i: (i // inner, 0, 0, 0))
    any_out = pl.BlockSpec(memory_space=pl.ANY)
    written = []
    for i, grad in enumerate(grads):
        n = grad.shape[2]
        part_spec = pl.BlockSpec(
            (1, per, n, width), lambda g, i=i, n=n: (g // inner, 0, g % inner * (mine // n) + i, 0)
        )
        written = [run(
            "finish", functools.partial(finish_kernel, feats), (owners,),
            (grad, patches, stats[:, :, 0, None], stats[:, :, 1, None], fixes[:, :, 0], fixes[:, :, 1], *written),
            [pl.BlockSpec((1, per, n, width), lambda g: (g, 0, 0, 0)), part_spec, *[one_spec] * 4,
             *[any_out] * len(written)],
            shape((snaps, per, quarter, width), F32), part_spec, [], 48, 100 if i == len(grads) - 1 else 5,
            aliases={6: 0} if written else None,
        )]
    patches_grad = written[0]
    expand_sum, project_sum = along_z(weights, 2)[0]
    project_sum = project_sum.T
    return (
        result, patches_grad, last[0], last[1], filters[0, ..., :BLOCK], filters[0, ..., BLOCK],
        filters[1, ..., :BLOCK], filters[1, ..., BLOCK],
        early[:feats], early[feats : 2 * feats], expand_sum, early[3 * feats : 3 * feats + hiddens],
        project_sum, early[2 * feats : 3 * feats], early[-1] / (snaps * rows * modes * feats * 2),
    )


def solution(mesh):
    tp = mesh.shape["tp"]
    planes = tp
    inner = mesh.shape["sp"] // planes
    blocks_local = 2
    cut = inner // blocks_local
    mesh = Mesh(mesh.devices.reshape(planes, blocks_local, cut, tp), ("z", "y", "j", "t"))
    sp = ("z", "y", "j")
    image = P(None, sp, "t", None)
    return jax.shard_map(
        functools.partial(per_device, (planes, blocks_local, cut, tp)),
        mesh=mesh,
        in_specs=(
            image, P(None, "t"), P("t"), P("t"),
            P(None, "t", None, None), P(None, "t", None), P(None, "t", None, None), P(None, "t", None),
            P("t"), P("t"), P(None, "t"), P("t"), P("t", None), P("t"), image,
        ),
        out_specs=(
            image, image, P(), P(),
            P(None, "t", sp, None), P(None, "t", sp), P(None, "t", sp, None), P(None, "t", sp),
            P(), P(), P(sp, "t"), P(), P("t", sp), P(), P(),
        ),
        check_vma=False,
    )
```

```python
import functools
import math

import jax
import jax.numpy as jnp
import numpy as np
from jax import lax
from jax.experimental import pallas as pl
from jax.experimental.pallas import tpu as pltpu
from jax.sharding import Mesh, PartitionSpec as P

BLOCK = 96
SHRINK = 0.01
NORM_EPS = 1e-05
BF = jnp.bfloat16
F32 = jnp.float32
FLOPS, BYTES = 1_000_000_000, 3_400_000
NN = (((1,), (0,)), ((), ()))
NT = (((1,), (1,)), ((), ()))
TN = (((0,), (0,)), ((), ()))


def dot(left, right, dims=NN):
    return lax.dot_general(left, right, dims, preferred_element_type=F32)


def gelu_pair(value):
    phi = 0.5 * lax.erf(value * (1.0 / math.sqrt(2.0))) + 0.5
    bell = jnp.exp2(value * value * (-0.5 / math.log(2.0)))
    return value * phi, phi + value * bell * (1.0 / math.sqrt(2.0 * math.pi))


def split(value):
    high = value.astype(BF)
    return high, (value - high.astype(F32)).astype(BF)


def np_split(table):
    high = table.astype(np.float32).astype(jnp.bfloat16)
    low = (table - high.astype(np.float64)).astype(np.float32).astype(jnp.bfloat16)
    return jnp.asarray(high), jnp.asarray(low)


def lon_tables(width, modes):
    angle = 2.0 * np.pi * (np.outer(np.arange(modes), np.arange(width)) % width) / width
    scale = 1.0 / math.sqrt(width)
    cos, sin = np.cos(angle) * scale, np.sin(angle) * scale
    doubled = np.where(np.arange(modes) == 0, 1.0, 2.0)[:, None]
    plain = np.concatenate([cos, -sin], 0)
    weighted = np.concatenate([cos * doubled, -sin * doubled], 0)
    return plain, weighted


def swapped(index):
    return index % 2 * 2 + index // 2


class Rows:
    def __init__(self, per, inner, quarters):
        self.per, self.inner, self.quarters = per, inner, quarters
        self.even = per % 2 == 0
        self.sizes = [per // 2, per - per // 2]

    def block(self, t, part):
        return t % 2 * 2 + (t // 2 + part) % 2 if self.even else swapped(t)

    def quarter(self, block, part):
        return (block + part) % 2 * 2 + block // 2 if self.even else swapped(block)

    def start(self, block, part):
        return (block + part) % 2 * self.sizes[0] if self.even else part * self.sizes[0]

    def order(self):
        held = []
        for t in range(self.quarters):
            for r in range(self.inner):
                for part in range(2):
                    block = self.block(t, part)
                    held.append(((block * self.inner + r) * self.per + self.start(block, part), self.sizes[part]))
        return held


def in_order(array, order):
    return jnp.concatenate([array[at : at + n] for at, n in order], axis=0)


def out_of_order(array, order):
    at = 0
    for row, n in order:
        yield row, n, array[at : at + n]
        at += n


def lat_table(rows, order):
    angle = 2.0 * np.pi * (np.outer(np.arange(rows), np.arange(rows)) % rows) / rows
    scale = 1.0 / math.sqrt(rows)
    held = np.concatenate([np.arange(at, at + n) for at, n in order])
    cos, sin = np.cos(angle)[:, held] * scale, np.sin(angle)[:, held] * scale
    return np.block([[cos, sin], [-sin, cos]])


def fold_lanes(value):
    total = value[:, :128]
    for at in range(128, value.shape[1], 128):
        total = total + value[:, at : at + 128]
    return total


def collect(pieces, order):
    value = pieces[...].astype(F32)
    return in_order(value.reshape(value.shape[0] * value.shape[1], *value.shape[2:]), order)


def lat_product(lat, high, low=None):
    size = lat.shape[1]
    both = dot(lat, high)
    rest = both[size:] if low is None else both[size:] + dot(lat[:size], low)
    return both[:size] + rest


def plane_forward(parts, table, lat, lons, spectra):
    rows, modes = lat.shape[1] // 2, spectra.shape[1]
    feats = spectra.shape[0] // (2 * rows)
    table_hi, table_lo = table
    total = dot(parts[0], table_lo)
    if len(parts) > 1:
        total = total + dot(parts[1], table_hi)
    total = total + dot(parts[0], table_hi)
    for c in range(2):
        lons[c, : rows * feats] = total[:, c * modes : (c + 1) * modes]
    for f in range(0, feats, 2):
        pair = []
        for g in (f, f + 1):
            pair.append(jnp.concatenate([lons[c, pl.ds(g, rows, stride=feats), :] for c in range(2)], axis=0))
        high, low = split(jnp.concatenate(pair, axis=1))
        out = lat_product(lat, high, low)
        for i, g in enumerate((f, f + 1)):
            spectra[pl.ds(g, 2 * rows, stride=feats), :] = out[:, i * modes : (i + 1) * modes]


def plane_inverse(table, lat, lons, spectra):
    rows, modes = lat.shape[1] // 2, spectra.shape[1]
    feats = spectra.shape[0] // (2 * rows)
    for f in range(0, feats, 2):
        pair = [spectra[pl.ds(g, 2 * rows, stride=feats), :] for g in (f, f + 1)]
        out = lat_product(lat, jnp.concatenate(pair, axis=1).astype(BF))
        for i, g in enumerate((f, f + 1)):
            for c in range(2):
                lons[c, pl.ds(g, rows, stride=feats), :] = out[c * rows : (c + 1) * rows, i * modes : (i + 1) * modes]
    table_hi, table_lo = table
    value = jnp.concatenate([lons[c, : rows * feats] for c in range(2)], axis=1).astype(BF)
    return dot(value, table_hi) + dot(value, table_lo)


def spectrum_kernel(order, pieces, mean, rstd, scale, shift, hi, lo, lat, spec, lons, spectra):
    mixed = (collect(pieces, order) - mean[...]) * rstd[...] * scale[...] + shift[...]
    rows, feats, width = mixed.shape
    parts = split(mixed.reshape(rows * feats, width))
    plane_forward(parts, (hi[...], lo[...]), lat[...], lons, spectra)
    spec[...] = spectra[: math.prod(spec.shape[:3])].reshape(spec.shape).astype(BF)


def join_lines(parts):
    value = jnp.concatenate([part[...] for part in parts], axis=1)
    return value.reshape(value.shape[0] * value.shape[1], *value.shape[2:])


def spectrum_back_kernel(n, *refs):
    parts, (hi, lo, lat, freq, lons, spectra) = refs[:n], refs[n:]
    value = join_lines(parts)
    rows, feats, width = value.shape
    if feats % 16:
        value = value.astype(F32).reshape(rows * feats, width).astype(BF)
    else:
        value = value.reshape(rows * feats, width)
    plane_forward((value,), (hi[...], lo[...]), lat[...], lons, spectra)
    freq[...] = spectra[: math.prod(freq.shape[:3])].reshape(freq.shape).astype(BF)


def two_modes(ref, ky):
    return jnp.concatenate([jnp.concatenate([ref[0, k], ref[1, k]], axis=0) for k in (ky, ky + 1)], axis=1)


def put_modes(ref, ky, value):
    feats, modes = ref.shape[2], ref.shape[3]
    for i in range(2):
        for c in range(2):
            ref[c, ky + i] = value[c * feats : (c + 1) * feats, i * modes : (i + 1) * modes].astype(ref.dtype)


def filter_kernel(spec, w1, bias1, w2, bias2, kept, mid, slope, bend, share):
    @pl.when(pl.program_id(0) == 0)
    def _():
        share[...] = jnp.zeros_like(share)

    for ky in range(0, spec.shape[1], 2):
        act, deriv = gelu_pair(dot(w1[...], two_modes(spec, ky)) + bias1[...])
        act = act.astype(BF)
        put_modes(mid, ky, act)
        put_modes(slope, ky, deriv)
        second = dot(w2[...], act) + bias2[...]
        bent = jnp.tanh(second * (1.0 / SHRINK))
        square = bent * bent
        put_modes(bend, ky, square)
        put_modes(kept, ky, second - SHRINK * bent)
        share[...] += jnp.sum((1.0 - square).reshape(-1, 8, square.shape[1]), axis=0)


def filter_back_kernel(
    freq, spec, mid, slope, bend, w1, w2, sgrad, inner, outer, inner_bias, outer_bias
):
    @pl.when(pl.program_id(0) == 0)
    def _():
        for ref in (inner, outer, inner_bias, outer_bias):
            ref[...] = jnp.zeros_like(ref)

    for ky in range(0, spec.shape[1], 2):
        two = (two_modes(freq, ky).astype(F32) * two_modes(bend, ky).astype(F32)).astype(BF)
        outer[...] += dot(two_modes(mid, ky), two, NT)
        outer_bias[...] += fold_lanes(two.astype(F32))
        one = (dot(w2[...], two, TN) * two_modes(slope, ky).astype(F32)).astype(BF)
        inner[...] += dot(two_modes(spec, ky), one, NT)
        inner_bias[...] += fold_lanes(one.astype(F32))
        put_modes(sgrad, ky, dot(w1[...], one, TN))


def section_kernel(order, pieces, mean, rstd, scale, shift, kept, hi, lo, lat, *refs):
    outs, (lons, spectra) = refs[:-2], refs[-2:]
    spectra[: math.prod(kept.shape[:3])] = kept[...].astype(F32).reshape(-1, kept.shape[3])
    value = collect(pieces, order)
    mixed = (value - mean[...]) * rstd[...] * scale[...] + shift[...]
    spectral = plane_inverse((hi[...], lo[...]), lat[...], lons, spectra)
    section = (value + mixed + spectral.reshape(value.shape)).astype(BF)
    section = section.reshape(pieces.shape[0], pieces.shape[1], *value.shape[1:])
    at = 0
    for out in outs:
        out[...] = section[:, at : at + out.shape[1]]
        at += out.shape[1]


def last_kernel(order, n, pieces, *refs):
    sgrad, (mean, rstd, scale, freq, hi, lo, lat, out, sums, gain_sum, shift_sum, lons, spectra) = refs[:n], refs[n:]
    spectra[: math.prod(freq.shape[:3])] = freq[...].astype(F32).reshape(-1, freq.shape[3])
    normed = (collect(pieces, order) - mean[...]) * rstd[...]
    grad = join_lines(sgrad).astype(F32)
    mixed = grad + plane_inverse((hi[...], lo[...]), lat[...], lons, spectra).reshape(grad.shape)
    gain_sum[...] = fold_lanes(jnp.sum(mixed * normed, axis=0))
    shift_sum[...] = fold_lanes(jnp.sum(mixed, axis=0))
    scaled = mixed * scale[...]
    value = (grad + rstd[...] * scaled).astype(BF)
    for at, n, part in out_of_order(value, order):
        out[at : at + n] = part

    @pl.when(pl.program_id(0) == 0)
    def _():
        sums[...] = jnp.zeros_like(sums)

    for c, term in enumerate((scaled, scaled * normed)):
        term = jnp.sum(term, axis=1)
        for at, n, part in out_of_order(term, order):
            sums[at : at + n, c] += part


def column_norm(value):
    mean = jnp.mean(value, axis=0, keepdims=True)
    centered = value - mean
    var = jnp.mean(centered * centered, axis=0, keepdims=True)
    rstd = lax.rsqrt(var + NORM_EPS)
    return centered * rstd, rstd


def feed_kernel(
    n, quarter, chunk, place, *refs
):
    cots = refs[:n]
    section, we_t, wp, we, bias, gain, shift = refs[n : n + 7]
    normal, hidden, pre, cot, sgrad, gain_sum, shift_sum = refs[-7:]

    @pl.when(pl.program_id(0) == 0)
    def _():
        gain_sum[...] = jnp.zeros_like(gain_sum)
        shift_sum[...] = jnp.zeros_like(shift_sum)

    for k, piece in enumerate(cots):
        cot[pl.ds(place[k] * quarter, quarter), :] = piece[0]
    normed, rstd = column_norm(section[...].astype(F32).reshape(normal.shape))
    value = (normed * gain[...] + shift[...]).astype(BF)
    normal[...] = value
    wide = cot[...]

    def bend(start, before, grad):
        rows = slice(start, start + chunk)
        act, slope = gelu_pair(before + jnp.concatenate([bias[rows]] * (value.shape[1] // 128), axis=1))
        hidden[rows] = act.astype(BF)
        pre[rows] = (grad * slope).astype(BF)

    ready = None
    for start in range(0, hidden.shape[0], chunk):
        rows = slice(start, start + chunk)
        products = start, dot(we_t[rows], value), dot(wp[rows], wide)
        if ready:
            bend(*ready)
        ready = products
    bend(*ready)
    part = we.shape[2]
    total = sum(dot(we[t], pre[t * part : (t + 1) * part]) for t in range(we.shape[0]))
    gain_sum[...] += fold_lanes(total * normed)
    shift_sum[...] += fold_lanes(total)
    wide = wide.astype(F32)
    scaled = total * gain[...]
    one = jnp.mean(scaled, axis=0, keepdims=True)
    two = jnp.mean(scaled * normed, axis=0, keepdims=True)
    grad = wide + rstd * (scaled - one - normed * two)
    sgrad[...] = grad.reshape(sgrad.shape).astype(BF)


def result_kernel(quarter, parts, place, hidden, wp_t, bias, *refs):
    sections, outs, field = refs[: len(parts)], refs[len(parts) : -1], refs[-1]
    row = pl.program_id(0)
    value = dot(wp_t[...], hidden[...]) + jnp.concatenate([bias[...]] * (hidden.shape[1] // 128), axis=1)
    at = 0
    for i, (section, n) in enumerate(zip(sections, parts)):

        @pl.when((row >= at) & (row < at + n))
        def _(i=i, section=section):
            field[...] = value + section[...].astype(F32).reshape(value.shape)
            for k, out in enumerate(outs[i :: len(parts)]):
                out[...] = field[pl.ds(place[k] * quarter, quarter), :].astype(BF)

        at += n


def weight_kernel(order, normal, pre, cot, hidden, sent, kept, bias_sum, cot_sum):
    products = dot(normal[...], pre[...], NT), dot(cot[...], hidden[...], NT)
    bias_sum[...] = fold_lanes(pre[...].astype(F32))
    away = pl.program_id(0) < pl.num_programs(0) // 2

    @pl.when((pl.program_id(0) == 0) & (pl.program_id(1) == 0))
    def _():
        cot_sum[...] = fold_lanes(cot[...].astype(F32))

    @pl.when(away)
    def _():
        for kind in range(2):
            sent[0, kind] = products[kind].astype(BF)

    @pl.when(jnp.logical_not(away))
    def _():
        for kind in range(2):
            kept[0, kind] = products[kind]


def add_kernel(side, kept, came, mine, theirs):
    for i in range(2):
        value = (kept[i, 0] + came[i, 0].astype(F32)).reshape(mine.shape[2], 2, -1, mine.shape[4])
        odd = side[0] == 1
        mine[i, 0] = jnp.where(odd, value[:, 1], value[:, 0])
        theirs[i, 0] = jnp.where(odd, value[:, 0], value[:, 1]).astype(BF)


def widen_kernel(parts, slot, starts, *refs):
    pieces, out = refs[:-1], refs[-1]
    width = out.shape[3]
    for i, piece in enumerate(pieces):
        k, part = divmod(i, len(parts))

        @pl.when(pl.program_id(0) == k)
        def _(piece=piece, part=part):
            for row in range(parts[part]):
                out[0, starts[part] + row] = piece[:, row * width : (row + 1) * width].astype(F32)


def finish_kernel(feats, grad, patches, mean, rstd, one, two, *refs):
    out = refs[-1]
    normed = (patches[0].astype(F32) - mean[0]) * rstd[0]
    out[0] = grad[0].astype(F32) - rstd[0] * (one[0] + normed * two[0]) * (1.0 / feats)


def whole(shape):
    return pl.BlockSpec(shape, lambda *_: (0,) * len(shape), pipeline_mode=pl.Buffered(1))


def fixed(shape):
    return pl.BlockSpec(shape, lambda *_: (0,) * len(shape))


def run(name, kernel, grid, ins, specs, outs, out_specs, scratch, mib, micros, scalars=(), aliases=None):
    grid_spec = pltpu.PrefetchScalarGridSpec(
        num_scalar_prefetch=len(scalars), grid=grid, in_specs=specs, out_specs=out_specs, scratch_shapes=scratch
    )
    call = pl.pallas_call(
        kernel,
        grid_spec=grid_spec,
        out_shape=outs,
        compiler_params=pltpu.CompilerParams(vmem_limit_bytes=max(mib, 62) << 20),
        input_output_aliases=aliases or {},
        cost_estimate=pl.CostEstimate(flops=int(micros * FLOPS), bytes_accessed=int(micros * BYTES), transcendentals=0),
        name=name,
    )
    return call(*scalars, *ins)


def complex_weight(pair):
    real, imag = pair[0].T, pair[1].T
    return jnp.concatenate([jnp.concatenate([real, -imag], 1), jnp.concatenate([imag, real], 1)], 0)


def weight_pair(full):
    full = full.reshape(2, BLOCK, 2, BLOCK)
    return jnp.stack([full[0, :, 0] + full[1, :, 1], full[0, :, 1] - full[1, :, 0]])


def per_device(
    sizes, patches, present, first_gain, first_shift, filter_inner, inner_bias, filter_outer, outer_bias,
    second_gain, second_shift, expand_weight, expand_bias, project_weight, project_bias, cotangent,
):
    planes, blocks_local, cut, tp = sizes
    inner = blocks_local * cut
    ranks = inner * tp
    owners = planes * inner
    snaps, per, quarter, width = patches.shape
    feats = quarter * tp
    mine = quarter // inner
    modes = width // 2
    rows = per * ranks
    toks = per * width
    hidden_local = expand_bias.shape[0]
    hiddens = hidden_local * tp
    z, y, j, t = (lax.axis_index(name) for name in ("z", "y", "j", "t"))
    r = y * cut + j
    me = z * inner + r
    every, sp = ("z", "y", "j", "t"), ("z", "y", "j")
    shape = jax.ShapeDtypeStruct

    pieces = patches.reshape(snaps, per, inner, mine, width).swapaxes(1, 2).reshape(owners, per, mine, width)
    pieces, expand_weight, project_weight = lax.optimization_barrier((pieces, expand_weight, project_weight))
    pieces = lax.all_to_all(pieces, sp, 0, 0, tiled=True)

    held = Rows(per, inner, tp)
    order, parts = held.order(), held.sizes

    def route(k, part, back):
        pairs = [
            ((zz * inner + rr) * tp + tt, (((swapped(tt) + k) % tp) * inner + rr) * tp + held.quarter(zz, part))
            for zz in range(planes)
            for rr in range(inner)
            for tt in range(tp)
        ]
        return [(b, a) for a, b in pairs] if back else pairs

    place = jnp.stack([swapped((z - k) % tp) for k in range(tp)]).astype(jnp.int32)
    slot = jnp.stack([(swapped(t) + k) % tp for k in range(tp)]).astype(jnp.int32)
    field = patches.astype(F32)
    mean = jnp.mean(field, 2)
    square = jnp.sum(jnp.square(field - mean[:, :, None]), 2)
    gathered = lax.all_gather(jnp.stack([mean, square]), "t")
    packed = lax.all_gather(jnp.concatenate([second_gain, second_shift, project_bias, expand_bias]), "t")
    small = [packed[:, i * quarter : (i + 1) * quarter].reshape(-1) for i in range(3)]
    bias_all = packed[:, 3 * quarter :].reshape(-1)
    mean = jnp.mean(gathered[:, 0], 0)
    square = jnp.sum(gathered[:, 1] + quarter * jnp.square(gathered[:, 0] - mean), 0)
    stats = jnp.stack([mean, lax.rsqrt(square / feats + NORM_EPS)], 2)
    def lanes(vector, width=width):
        return jnp.broadcast_to(vector[:, None], (vector.shape[0], width))

    we = lax.all_gather(expand_weight, "t")
    wp = lax.all_gather(project_weight, "t", tiled=True)
    we_t, wp_t = jnp.swapaxes(we, 1, 2).reshape(hiddens, feats), wp.T
    gain2, shift2, bias_lanes = lanes(small[0]), lanes(small[1]), lanes(bias_all, 128)
    sent_stats, we, wp, we_t, wp_t, gain2, shift2, bias_lanes = lax.optimization_barrier(
        (stats, we, wp, we_t, wp_t, gain2, shift2, bias_lanes)
    )
    plane_stats = []
    for k in range(owners):
        piece = lax.dynamic_index_in_dim(sent_stats, (me ^ k) // inner, 0, False)
        plane_stats.append(lax.ppermute(piece, sp, [(a, a ^ k) for a in range(owners)]) if k else piece)
    bit = 1
    while bit < owners:
        turn = (me // bit) % 2 == 1
        plane_stats = [jnp.where(turn, plane_stats[k ^ bit], plane_stats[k]) for k in range(owners)]
        bit *= 2
    plane_stats = jnp.stack(plane_stats)
    plane_stats = in_order(plane_stats.reshape(rows, 2, 1, width), order)
    mean_one, rstd_one = plane_stats[:, 0], plane_stats[:, 1]

    def own_features(vector):
        return lax.dynamic_slice_in_dim(vector, r * mine, mine)

    keep = own_features(lax.dynamic_index_in_dim(present, z, 0, False).astype(F32))
    scale1, shift1 = lanes(own_features(first_gain) * keep), lanes(own_features(first_shift) * keep)

    def own_block(array):
        return lax.dynamic_index_in_dim(array, y, 1, False)

    w1, w2 = complex_weight(own_block(filter_inner)), complex_weight(own_block(filter_outer))
    bias1 = lanes(own_block(inner_bias).reshape(-1), 2 * modes)
    bias2 = lanes(own_block(outer_bias).reshape(-1), 2 * modes)
    plain, weighted = lon_tables(width, modes)
    lat = lat_table(rows, order)
    plain_t, weighted_t, plain_n, weighted_n = (np_split(a) for a in (plain.T, weighted.T, plain, weighted))
    lat_f, lat_b = (jnp.concatenate(np_split(a)) for a in (lat, lat.T))

    cotangents = [
        [lax.dynamic_slice(cotangent, (slot[k], held.start(z, part), 0, 0), (1, n, quarter, width))[0] for k in range(tp)]
        for part, n in enumerate(parts)
    ]
    late, pieces = lax.optimization_barrier((cotangents, pieces))
    cots = [[lax.ppermute(piece, every, route(k, 0, False)) for k, piece in enumerate(late[0])]]

    some = 16 if mine % 16 == 0 else mine
    grid = (mine // some,)
    piece_spec = pl.BlockSpec((owners, per, some, width), lambda g, *_: (0, 0, g, 0))
    stat_spec, feat_spec = whole((rows, 1, width)), pl.BlockSpec((some, width), lambda g, *_: (g, 0))
    lon_f, lon_b = [whole((width, 2 * modes))] * 2, [whole((2 * modes, width))] * 2
    lat_specs = [whole((4 * rows, 2 * rows))]
    image_spec = pl.BlockSpec((rows, some, width), lambda g, *_: (0, g, 0))
    modes_spec = pl.BlockSpec((2, rows, some, modes), lambda g, *_: (0, 0, g, 0))
    scratch = [
        pltpu.VMEM((2, (rows + 1) * some, modes), F32),
        pltpu.VMEM(((2 * rows + 1) * some, modes), F32),
    ]
    mine_modes = (2, rows, mine, modes)
    spec = run(
        "spectrum", functools.partial(spectrum_kernel, order), grid,
        (pieces, mean_one, rstd_one, scale1, shift1, *plain_t, lat_f),
        [piece_spec, stat_spec, stat_spec, feat_spec, feat_spec, *lon_f, *lat_specs],
        shape(mine_modes, BF), modes_spec, scratch, 48, 22,
    )

    def to_blocks(array):
        return lax.all_to_all(array, "j", 1, 2, tiled=True) if cut > 1 else array

    def to_features(array):
        return lax.all_to_all(array, "j", 2, 1, tiled=True) if cut > 1 else array

    spec = to_blocks(spec)
    lats = rows // cut
    step = 16 if lats % 16 == 0 else 8
    block_modes = (2, lats, BLOCK, modes)
    block_spec = pl.BlockSpec((2, step, BLOCK, modes), lambda g: (0, g, 0, 0))
    square_spec, lane_spec = whole((2 * BLOCK, 2 * BLOCK)), whole((2 * BLOCK, 2 * modes))
    kept, mid, slope, bend, share = run(
        "filter", filter_kernel, (lats // step,), (spec, w1, bias1, w2, bias2),
        [block_spec, square_spec, lane_spec, square_spec, lane_spec],
        (*[shape(block_modes, BF)] * 4, shape((8, 2 * modes), F32)),
        (block_spec, block_spec, block_spec, block_spec, fixed((8, 2 * modes))), [], 48, 17,
    )
    part_specs = [pl.BlockSpec((ranks, n, some, width), lambda g, *_: (0, 0, g, 0)) for n in parts]
    sections = run(
        "section", functools.partial(section_kernel, order), grid,
        (pieces, mean_one, rstd_one, scale1, shift1, to_features(kept), *weighted_n, lat_b),
        [piece_spec, stat_spec, stat_spec, feat_spec, feat_spec, modes_spec, *lon_b, *lat_specs],
        [shape((ranks, n, mine, width), BF) for n in parts], part_specs, scratch, 56, 17,
    )

    sections, late, cots[0] = lax.optimization_barrier((sections, late, cots[0]))

    def exchange(array):
        return lax.all_to_all(array, ("t", "y", "j"), 0, 0, tiled=True)

    outs = (
        shape((feats, toks), BF), shape((hiddens, toks), BF), shape((hiddens, toks), BF), shape((feats, toks), BF),
    )
    sum_shapes = [shape((feats, 128), F32)] * 2
    sgrads, sums, done, start = [], [], (), 0
    received = []
    for n, section in zip(parts, sections):
        section = exchange(section)
        if not received:
            section, late = lax.optimization_barrier((section, late))
            cots.append([lax.ppermute(piece, every, route(k, 1, False)) for k, piece in enumerate(late[1])])
        tok_spec = pl.BlockSpec((feats, width), lambda h, *_, start=start: (0, h + start))
        hid_spec = pl.BlockSpec((hiddens, width), lambda h, *_, start=start: (0, h + start))
        cot_specs = [pl.BlockSpec((1, quarter, width), lambda h, *_: (h, 0, 0))] * tp
        line_spec = pl.BlockSpec((ranks, 1, mine, width), lambda h, *_: (0, h, 0, 0))
        any_spec = pl.BlockSpec(memory_space=pl.ANY)
        *done, sgrad, s0, s1 = run(
            "feed", functools.partial(feed_kernel, tp, quarter, min(256, hidden_local)), (n,),
            (*cots[len(received)], section, we_t, wp, we, bias_lanes, gain2, shift2, *done),
            [*cot_specs, line_spec, whole((hiddens, feats)), whole((hiddens, feats)),
             whole((tp, feats, hidden_local)), whole((hiddens, 128)), whole((feats, width)), whole((feats, width)),
             *[any_spec] * len(done)],
            (*outs, shape((ranks, n, mine, width), BF), *sum_shapes),
            (tok_spec, hid_spec, hid_spec, tok_spec, line_spec, *[fixed((feats, 128))] * 2),
            [], 60, 43, (place,), {8 + tp + i: i for i in range(len(done))},
        )
        if start:
            sgrad, done, sgrads = lax.optimization_barrier((sgrad, done, sgrads))
            rows_out = run(
                "result", functools.partial(result_kernel, quarter, parts), (per,),
                (done[1], wp_t, lanes(small[2], 128), *received, section),
                [pl.BlockSpec((hiddens, width), lambda h, *_: (0, h)), whole((feats, hiddens)), whole((feats, 128)),
                 *[pl.BlockSpec((ranks, 1, mine, width), lambda h, *_, at=at, m=m: (0, jnp.clip(h - at, 0, m - 1), 0, 0))
                   for at, m in zip((0, parts[0]), parts)]],
                [shape((quarter, m * width), BF) for _ in range(tp) for m in parts],
                [pl.BlockSpec((quarter, width), lambda h, *_, at=at, m=m: (0, jnp.clip(h - at, 0, m - 1)))
                 for _ in range(tp) for at, m in zip((0, parts[0]), parts)],
                [pltpu.VMEM((feats, width), F32)], 48, 0.01, (place,),
            )
            rows_out, done = lax.optimization_barrier((rows_out, done))
            results = [None] * (2 * tp)

            def send_results(rounds):
                for k in rounds:
                    for part in range(2):
                        results[2 * k + part] = lax.ppermute(rows_out[2 * k + part], every, route(k, part, True))

            send_results((0, 1))
        sgrad = exchange(sgrad)
        if start:
            third, half = hidden_local // 3, tp // 2
            resident = whole((feats, toks))
            hid_rows = pl.BlockSpec((third, toks), lambda k, i, o: (o[k] * 3 + i, 0))
            normal, hidden, pre, cot = done
            sent, kept_products, bias_sum, cot_sum = run(
                "weights", weight_kernel, (tp, 3), (normal, pre, cot, hidden), [resident, hid_rows, resident, hid_rows],
                [shape((half, 2, feats, hidden_local), BF), shape((half, 2, feats, hidden_local), F32),
                 shape((hiddens, 128), F32), shape((feats, 128), F32)],
                [pl.BlockSpec((1, 2, feats, third), lambda k, i, o: (jnp.minimum(k, half - 1), 0, 0, jnp.where(k < half, i, 2))),
                 pl.BlockSpec((1, 2, feats, third), lambda k, i, o: (jnp.maximum(k - half, 0), 0, 0, jnp.where(k < half, 0, i))),
                 pl.BlockSpec((third, 128), lambda k, i, o: (o[k] * 3 + i, 0)), fixed((feats, 128))],
                [], 60, 0.01,
                (jnp.stack([t ^ k for k in (*range(1, tp, 2), *range(0, tp, 2))]).astype(jnp.int32),),
            )
            sgrad, sent, results, rows_out = lax.optimization_barrier((sgrad, sent, results, rows_out))
            came = lax.ppermute(sent, "t", [(a, a ^ 1) for a in range(tp)])
            send_results((2,))
        sgrads.append(sgrad)
        sums.append((s0, s1))
        received.append(section)
        start += n
    gain_sum, shift_sum = (a + b for a, b in zip(*sums))

    def trade(theirs, axes, bit, size):
        return lax.ppermute(theirs, axes, [(a, a ^ bit) for a in range(size)])

    def halves(array, bit):
        other = 1 - (me // bit) % 2
        return lax.dynamic_index_in_dim(array, 1 - other, 0, False), lax.dynamic_index_in_dim(array, other, 0, False)


    freq = run(
        "spectrum_back", functools.partial(spectrum_back_kernel, len(parts)), grid, (*sgrads, *weighted_t, lat_f),
        [*part_specs, *lon_f, *lat_specs], shape(mine_modes, BF), modes_spec, scratch, 48, 0.01,
    )
    freq, came = lax.optimization_barrier((freq, came))
    side = (me % 2).astype(jnp.int32).reshape(1)
    strip = feats // owners
    third = hidden_local // 3
    halves_shape = (2, 2, owners // 2, strip, hidden_local)
    halves_block = pl.BlockSpec((2, 1, owners // 2, strip, third), lambda kind, i, _: (0, kind, 0, 0, i))
    weights, theirs = run(
        "add", add_kernel, (2, 3), (kept_products, came),
        [pl.BlockSpec((half, 1, feats, third), lambda kind, i, _: (0, kind, 0, i))] * 2,
        (shape(halves_shape, F32), shape(halves_shape, BF)), (halves_block, halves_block), [], 48, 0.01, (side,),
    )
    freq, theirs, weights, results, rows_out = lax.optimization_barrier((freq, theirs, weights, results, rows_out))
    send_results((3,))
    came = trade(theirs, sp, 1, owners)
    freq, inner_grad, outer_grad, inner_bias_grad, outer_bias_grad = run(
        "filter_back", filter_back_kernel, (lats // step,), (to_blocks(freq), spec, mid, slope, bend, w1, w2),
        [*[block_spec] * 5, square_spec, square_spec],
        (shape(block_modes, BF), *[shape((2 * BLOCK, 2 * BLOCK), F32)] * 2, *[shape((2 * BLOCK, 128), F32)] * 2),
        (block_spec, *[fixed((2 * BLOCK, 2 * BLOCK))] * 2, *[fixed((2 * BLOCK, 128))] * 2), [], 48, 0.01,
    )
    freq, results = lax.optimization_barrier((freq, results))
    cuts = [grid[0] // 2, grid[0] - grid[0] // 2] if grid[0] > 1 else [1]
    grads, lines, first_sums, at = [], [], [], 0
    freq = to_features(freq)
    for i, n in enumerate(cuts):
        here = lambda g, at=at: g + at
        image_part = pl.BlockSpec((rows, some, width), lambda g: (0, g, 0))
        grad, line_sums, *sums_here = run(
            "last", functools.partial(last_kernel, order, len(parts)), (n,),
            (pieces, *sgrads, mean_one, rstd_one, scale1, freq, *plain_n, lat_b),
            [pl.BlockSpec((owners, per, some, width), lambda g, here=here: (0, 0, here(g), 0)),
             *[pl.BlockSpec((ranks, m, some, width), lambda g, here=here: (0, 0, here(g), 0)) for m in parts],
             stat_spec, stat_spec, pl.BlockSpec((some, width), lambda g, here=here: (here(g), 0)),
             pl.BlockSpec((2, rows, some, modes), lambda g, here=here: (0, 0, here(g), 0)), *lon_b, *lat_specs],
            (shape((rows, n * some, width), BF), shape((rows, 2, width), F32), *[shape((n * some, 128), F32)] * 2),
            (image_part, fixed((rows, 2, width)), *[pl.BlockSpec((some, 128), lambda g: (g, 0))] * 2),
            scratch, 56, 0.01,
        )
        grads.append(grad.reshape(owners, per, n * some, width))
        lines.append(line_sums)
        first_sums.append(sums_here)
        at += n
        if i < len(cuts) - 1:
            freq, came = lax.optimization_barrier((freq, came))
            grads[i] = lax.all_to_all(grads[i], sp, 0, 0, tiled=True)
    weights = weights + came.astype(F32)
    came = trade(weights[1].astype(BF), "t", 2, tp)
    first_gain_sum, first_shift_sum = (jnp.concatenate(sums_here, 0) for sums_here in zip(*first_sums))
    lines = sum(lines)
    def with_bias(full, bias):
        bias = jnp.sum(bias, 1).reshape(2, BLOCK)
        return jnp.concatenate([weight_pair(full), bias[:, :, None]], 2)

    filters = jnp.stack([with_bias(inner_grad, inner_bias_grad), with_bias(outer_grad, outer_bias_grad)])
    filters = jnp.moveaxis(filters, 2, 0).reshape(owners, -1)
    early = jnp.concatenate(
        [jnp.sum(gain_sum, 1), jnp.sum(shift_sum, 1), jnp.sum(cot_sum, 1), jnp.sum(bias_sum, 1), jnp.sum(share)[None]]
    )
    grads, lines, results, came = lax.optimization_barrier((grads, lines, results, came))
    weights = jnp.moveaxis(weights[0] + came.astype(F32), 1, 0)
    bit = 2
    while bit < inner:
        weights = weights.reshape(-1, 2, *weights.shape[1:])
        weights, theirs = halves(weights.swapaxes(0, 1), bit)
        weights = weights + trade(theirs.astype(BF), sp, bit, owners).astype(F32)
        bit *= 2
    line = per * width
    feature_sums = jnp.stack([jnp.sum(first_gain_sum, 1) * keep, jnp.sum(first_shift_sum, 1) * keep]).reshape(-1)
    tail = jnp.concatenate(
        [lines.reshape(owners, 2 * line), filters,
         jnp.broadcast_to(jnp.concatenate([feature_sums, early]), (owners, 2 * mine + early.shape[0]))], 1
    )
    tail = lax.all_to_all(tail, sp, 0, 0, tiled=True)
    tail, grads, weights = lax.optimization_barrier((tail, grads, weights))
    def along_z(weights, bit):
        weights = weights.reshape(-1, 2, *weights.shape[1:])
        side = (z // bit) % 2
        theirs = lax.dynamic_index_in_dim(weights, 1 - side, 1, False).astype(BF)
        return lax.dynamic_index_in_dim(weights, side, 1, False) + trade(theirs, "z", bit, planes).astype(F32)

    weights = along_z(weights, 1)
    grads[-1] = lax.all_to_all(grads[-1], sp, 0, 0, tiled=True)
    grads[-1], weights = lax.optimization_barrier((grads[-1], weights))
    cuts = [2 * line, 2 * line + filters.shape[1], 2 * line + filters.shape[1] + 2 * mine]
    lines, filters, feature_sums, early = jnp.split(tail, cuts, axis=1)
    lines = jnp.sum(lines.reshape(planes, inner, -1), 1).reshape(-1)
    filters = jnp.sum(filters.reshape(planes, blocks_local, cut, BLOCK // owners, 2, 2, BLOCK + 1), (0, 2))
    filters = jnp.transpose(filters, (2, 3, 0, 1, 4))
    feature_sums = jnp.sum(feature_sums.reshape(planes, inner, 2, mine), 0).swapaxes(0, 1)
    spread = lax.dynamic_update_slice(
        jnp.zeros((2, tp, quarter), F32), feature_sums.reshape(2, 1, quarter), (0, t, 0)
    ).reshape(-1)
    tail = jnp.concatenate([lines, spread, jnp.sum(early, 0)])
    bit = 1
    while bit < tp:
        tail = tail + trade(tail, "t", bit, tp)
        bit *= 2
    cuts = [planes * 2 * line, planes * 2 * line + 2 * feats]
    lines, last, early = jnp.split(tail, cuts)
    fixes = lines.reshape(planes, per, 2, 1, width)
    last = last.reshape(2, feats)

    starts = jnp.stack([jnp.asarray(held.start(z, part), jnp.int32) for part in range(2)])
    result = run(
        "widen", functools.partial(widen_kernel, parts), (tp,), results,
        [whole((quarter, n * width)) for _ in range(tp) for n in parts], shape((snaps, per, quarter, width), F32),
        pl.BlockSpec((1, per, quarter, width), lambda i, s, _: (s[i], 0, 0, 0)), [], 32, 8, (slot, starts),
    )
    one_spec = pl.BlockSpec((1, per, 1, width), lambda i: (i // inner, 0, 0, 0))
    any_out = pl.BlockSpec(memory_space=pl.ANY)
    written = []
    for i, grad in enumerate(grads):
        n = grad.shape[2]
        part_spec = pl.BlockSpec(
            (1, per, n, width), lambda g, i=i, n=n: (g // inner, 0, g % inner * (mine // n) + i, 0)
        )
        written = [run(
            "finish", functools.partial(finish_kernel, feats), (owners,),
            (grad, patches, stats[:, :, 0, None], stats[:, :, 1, None], fixes[:, :, 0], fixes[:, :, 1], *written),
            [pl.BlockSpec((1, per, n, width), lambda g: (g, 0, 0, 0)), part_spec, *[one_spec] * 4,
             *[any_out] * len(written)],
            shape((snaps, per, quarter, width), F32), part_spec, [], 48, 100 if i == len(grads) - 1 else 5,
            aliases={6: 0} if written else None,
        )]
    patches_grad = written[0]
    expand_sum, project_sum = along_z(weights, 2)[0]
    project_sum = project_sum.T
    return (
        result, patches_grad, last[0], last[1], filters[0, ..., :BLOCK], filters[0, ..., BLOCK],
        filters[1, ..., :BLOCK], filters[1, ..., BLOCK],
        early[:feats], early[feats : 2 * feats], expand_sum, early[3 * feats : 3 * feats + hiddens],
        project_sum, early[2 * feats : 3 * feats], early[-1] / (snaps * rows * modes * feats * 2),
    )


def solution(mesh):
    tp = mesh.shape["tp"]
    planes = tp
    inner = mesh.shape["sp"] // planes
    blocks_local = 2
    cut = inner // blocks_local
    mesh = Mesh(mesh.devices.reshape(planes, blocks_local, cut, tp), ("z", "y", "j", "t"))
    sp = ("z", "y", "j")
    image = P(None, sp, "t", None)
    return jax.shard_map(
        functools.partial(per_device, (planes, blocks_local, cut, tp)),
        mesh=mesh,
        in_specs=(
            image, P(None, "t"), P("t"), P("t"),
            P(None, "t", None, None), P(None, "t", None), P(None, "t", None, None), P(None, "t", None),
            P("t"), P("t"), P(None, "t"), P("t"), P("t", None), P("t"), image,
        ),
        out_specs=(
            image, image, P(), P(),
            P(None, "t", sp, None), P(None, "t", sp), P(None, "t", sp, None), P(None, "t", sp),
            P(), P(), P(sp, "t"), P(), P("t", sp), P(), P(),
        ),
        check_vma=False,
    )
```
